32 devices in a mesh: ctx: 8 (over z, y), fsdp: 4 (over x, core).
Axes of the slice: x: 2, y: 2, z: 4, core: 2. Of those that a mesh axis runs over, the one named last changes fastest.
Arguments:
- inputs: bfloat16 [8, 1024, 1024], P('fsdp', 'ctx'), may hold values from -6 to 6
- lengths: int32 [8], P('fsdp'), may hold values from 256 to 1024, as said below
- positions: int32 [8, 1024], P('fsdp', 'ctx'), may hold values from 0 to 2046, as said below
- cotangent: bfloat16 [8, 1024, 1024], P('fsdp', 'ctx'), may hold values from -6 to 6
- w_query: float32 [1024, 1024], P('fsdp'), may hold values from -0.1875 to 0.1875
- w_key: float32 [1024, 512], P('fsdp'), may hold values from -0.1875 to 0.1875
- w_value: float32 [1024, 512], P('fsdp'), may hold values from -0.1875 to 0.1875
- w_output: float32 [1024, 1024], P('fsdp'), may hold values from -2 to 2
- w_gate: float32 [1024, 4608], P('fsdp'), may hold values from -0.1875 to 0.1875
- w_up: float32 [1024, 4608], P('fsdp'), may hold values from -0.1875 to 0.1875
- w_down: float32 [4608, 1024], P('fsdp'), may hold values from -0.09375 to 0.09375
- attn_gain: float32 [1024], P('fsdp'), may hold values from 0.5 to 1.5
- ffn_gain: float32 [1024], P('fsdp'), may hold values from 0.5 to 1.5
- query_gain: float32 [64], P('fsdp'), may hold values from 0.25 to 1.75
- key_gain: float32 [64], P('fsdp'), may hold values from 0.25 to 1.75
Outputs:
- block_output: bfloat16 [8, 1024, 1024], P('fsdp', 'ctx')
- input_grad: float32 [8, 1024, 1024], P('fsdp', 'ctx')
- query_grad: float32 [1024, 1024], P('fsdp')
- key_grad: float32 [1024, 512], P('fsdp')
- value_grad: float32 [1024, 512], P('fsdp')
- output_grad: float32 [1024, 1024], P('fsdp')
- gate_grad: float32 [1024, 4608], P('fsdp')
- up_grad: float32 [1024, 4608], P('fsdp')
- down_grad: float32 [4608, 1024], P('fsdp')
- attn_gain_grad: float32 [1024], P('fsdp')
- ffn_gain_grad: float32 [1024], P('fsdp')
- query_gain_grad: float32 [64], P('fsdp')
- key_gain_grad: float32 [64], P('fsdp')
The draws below stay inside these ranges and needn't reach their ends.
Inputs may be any that keep to these rules, and one draw needn't show every extreme that they name: `lengths`: of the 2 sequences of each index of fsdp, one (drawn from the seed) has length 1024; in the first index of fsdp another has length 256. Each sequence's positions start at 0 and rise by 1 or 2 from slot to slot; one sequence (drawn from the seed) rises by 2 at every slot.
All inputs are finite; a program needn't handle non-finite values.
Results may differ from the reference program's by a relative error of at most 0.017.
The reference program's roundings to bfloat16 on the way count: a program that leaves them out, or rounds other values in their place, can miss the bound.
Values may be sent and summed in bfloat16 or wider, within the bound.
No kernel may reach another device: no remote copies, remote signals or barrier semaphores. Data moves between devices by JAX's collectives and lax.ppermute only.
A program may use at most 320 MiB of HBM per device.

```python
import jax
import jax.numpy as jnp
from jax import lax

D = 1024
HEADS = 16
KV_HEADS = 8
HEAD = 64
FF = 4608
SEQ_GRP = 2
LEN = 1024
SEQS = 8
KBLOCK = 512


def draw_lengths(key, part):
    key = jax.random.fold_in(key, 11)
    first_key, second_key = jax.random.split(key)
    ragged = jax.random.randint(first_key, (SEQS,), LEN // 4, LEN + 1)
    chosen = jax.random.randint(second_key, (SEQS // SEQ_GRP,), 0, SEQ_GRP)
    full_one = jnp.arange(SEQS) % SEQ_GRP == jnp.repeat(chosen, SEQ_GRP)
    short_one = jnp.arange(SEQS) == (chosen[0] + 1) % SEQ_GRP
    picked = jnp.where(short_one, LEN // 4, ragged)
    return jnp.where(full_one, LEN, picked).astype(jnp.int32)


def draw_positions(key, part):
    key = jax.random.fold_in(key, 23)
    first_key, second_key = jax.random.split(key)
    strides = jax.random.randint(first_key, (SEQS, LEN), 1, 3)
    widest = jax.random.randint(second_key, (), 0, SEQS)
    strides = jnp.where(jnp.arange(SEQS)[:, None] == widest, 2, strides)
    return (jnp.cumsum(strides, axis=1) - strides[:, :1]).astype(jnp.int32)


def shard_levels(stream_key, extent, pieces, low, top_value):
    def one(axis_at, blocks):
        draws = jax.random.uniform(jax.random.fold_in(jax.random.fold_in(stream_key, 6), axis_at), (blocks,), jnp.float32, low / len(pieces), top_value / len(pieces))
        return jnp.repeat(jnp.exp(draws), extent[axis_at] // blocks).reshape((-1,) + (1,) * (len(extent) - axis_at - 1))

    loudness = one(*pieces[0])
    for cut in pieces[1:]:
        loudness = loudness * one(*cut)
    return loudness


def normal_values(own_key, shape, deviation, most, pieces=(), held_as=jnp.bfloat16):
    drawn = jax.random.normal(own_key, shape, jnp.float32) * deviation
    if len(pieces) > 0:
        drawn = shard_levels(own_key, shape, pieces, -0.22, 0.18) * drawn
    return jnp.clip(drawn, min=-most, max=most).astype(held_as)


def setup_inputs(seed: int = 0) -> dict:
    seeds = jax.random.split(jax.random.key(seed), 16)
    inputs = normal_values(seeds[0], (SEQS, LEN, D), 1.0, 6.0, ((0, 4), (1, 8)))
    lengths = draw_lengths(jax.random.fold_in(seeds[15], 71), 0)
    positions = draw_positions(jax.random.fold_in(seeds[15], 71), 0)
    cotangent = normal_values(seeds[3], (SEQS, LEN, D), 1.0, 6.0, ((0, 4), (1, 8)))
    w_query = normal_values(seeds[4], (D, HEADS * HEAD), D ** -0.5, 0.1875, ((0, 4),), jnp.float32)
    w_key = normal_values(seeds[5], (D, KV_HEADS * HEAD), D ** -0.5, 0.1875, ((0, 4),), jnp.float32)
    w_value = normal_values(seeds[6], (D, KV_HEADS * HEAD), D ** -0.5, 0.1875, ((0, 4),), jnp.float32)
    w_output = normal_values(seeds[7], (HEADS * HEAD, D), 8 ** -0.5, 2.0, ((0, 4),), jnp.float32)
    w_gate = normal_values(seeds[8], (D, FF), D ** -0.5, 0.1875, ((0, 4),), jnp.float32)
    w_up = normal_values(seeds[9], (D, FF), D ** -0.5, 0.1875, ((0, 4),), jnp.float32)
    w_down = normal_values(seeds[10], (FF, D), FF ** -0.5, 0.09375, ((0, 4),), jnp.float32)
    attn_gain = jnp.clip(1.0 + 0.1 * jax.random.normal(seeds[11], (D,), jnp.float32), 0.5, 1.5)
    ffn_gain = jnp.clip(1.0 + 0.1 * jax.random.normal(seeds[12], (D,), jnp.float32), 0.5, 1.5)
    query_gain = jnp.clip(1.0 + 0.15 * jax.random.normal(seeds[13], (HEAD,), jnp.float32), 0.25, 1.75)
    key_gain = jnp.clip(1.0 + 0.15 * jax.random.normal(seeds[14], (HEAD,), jnp.float32), 0.25, 1.75)
    return dict(inputs=inputs, lengths=lengths, positions=positions, cotangent=cotangent, w_query=w_query, w_key=w_key, w_value=w_value, w_output=w_output, w_gate=w_gate, w_up=w_up, w_down=w_down, attn_gain=attn_gain, ffn_gain=ffn_gain, query_gain=query_gain, key_gain=key_gain)


epsilon = 1e-05
rope_base = 1000000.0
masked = -1e+30

@jax.custom_vjp
def low(v):
    return lax.optimization_barrier(v.astype(jnp.bfloat16)).astype(jnp.float32)

@jax.custom_vjp
def low_back(v):
    return v

def low_keep(v):
    return (low(v), None)

def low_pass(kept, grad):
    return (grad,)

def back_keep(v):
    return (v, None)

def back_low(kept, grad):
    return (low(grad),)
low.defvjp(low_keep, low_pass)
low_back.defvjp(back_keep, back_low)

def matmul(left, right):
    return jnp.dot(left, right, precision=lax.Precision.HIGHEST, preferred_element_type=jnp.float32)

def rms_scale(values, scales):
    return values * lax.rsqrt(lax.optimization_barrier(jnp.mean(values * values, axis=-1, keepdims=True)) + epsilon) * scales

def rotate(values, cosine, sine_part):
    half_width = values.shape[-1] // 2
    first_half = values[..., :half_width]
    second_half = values[..., half_width:]
    return jnp.concatenate([first_half * cosine - second_half * sine_part, second_half * cosine + first_half * sine_part], axis=-1)

def angles(positions, head_width):
    frequency = rope_base ** (-jnp.arange(0, head_width, 2).astype(jnp.float32) / head_width)
    turned = positions.astype(jnp.float32)[..., None] * frequency
    return (jnp.cos(turned), jnp.sin(turned))

def prepare(projected, scales, cosine, sine_part):
    head_width = scales.shape[0]
    shaped = projected.reshape(projected.shape[0], projected.shape[1] // head_width, head_width)
    return rotate(rms_scale(shaped, scales), cosine[:, None], sine_part[:, None])

def swiglu(gate_proj, up_proj):
    return gate_proj * jax.nn.sigmoid(gate_proj) * up_proj

def attend(query_low, key_low, value_low, seq_len):
    row_count = query_low.shape[0]
    repeat = HEADS // KV_HEADS
    grouped = query_low.reshape(row_count // KBLOCK, KBLOCK, KV_HEADS, repeat, HEAD)
    key_slots = jnp.arange(row_count)
    starts = (jnp.arange(row_count // KBLOCK) * KBLOCK).astype(jnp.int32)

    def one_block(operands):
        query_block, block_start = operands
        query_slots = block_start + jnp.arange(KBLOCK)
        scores = jnp.einsum('ikrd,jkd->krij', query_block, key_low, precision=lax.Precision.HIGHEST) * HEAD ** (-0.5)
        allowed = (key_slots[None, :] <= query_slots[:, None]) & (key_slots[None, :] < seq_len)
        scores = low_back(jnp.where(allowed, scores, masked))
        top_row = lax.optimization_barrier(jnp.max(scores, axis=-1, keepdims=True))
        exponent = jnp.exp(scores - top_row)
        weights_low = low(exponent / lax.optimization_barrier(jnp.sum(exponent, axis=-1, keepdims=True)))
        attended = jnp.einsum('krij,jkd->ikrd', weights_low, value_low, precision=lax.Precision.HIGHEST)
        return attended.reshape(KBLOCK, HEADS * HEAD)
    return lax.map(jax.checkpoint(one_block), (grouped, starts)).reshape(row_count, HEADS * HEAD)

def layer(inputs, seq_len, positions, params):
    rounded = [low(member) for member in params]
    w_query, w_key, w_value, w_output, w_gate, w_up, w_down, attn_gain, ffn_gain, query_gain, key_gain = rounded
    row_count = inputs.shape[0]
    valid = (jnp.arange(row_count) < seq_len).astype(jnp.float32)[:, None]
    cosine, sine_part = angles(positions, HEAD)
    normed_low = low(rms_scale(inputs, attn_gain))
    query_proj = low_back(matmul(normed_low, w_query))
    key_proj = low_back(matmul(normed_low, w_key))
    value_proj = low_back(matmul(normed_low, w_value))
    query_low = low(prepare(query_proj, query_gain, cosine, sine_part))
    key_low = low(prepare(key_proj, key_gain, cosine, sine_part))
    value_low = low(value_proj).reshape(row_count, KV_HEADS, HEAD)
    attended = low_back(low(attend(query_low, key_low, value_low, seq_len)))
    hidden_res = inputs + low_back(matmul(attended, w_output))
    mid_low = low(rms_scale(hidden_res, ffn_gain))
    gate_proj = low_back(matmul(mid_low, w_gate))
    up_proj = low_back(matmul(mid_low, w_up))
    inner_low = low(swiglu(gate_proj, up_proj))
    return valid * (hidden_res + matmul(inner_low, w_down))

def reference(inputs, lengths, positions, cotangent, w_query, w_key, w_value, w_output, w_gate, w_up, w_down, attn_gain, ffn_gain, query_gain, key_gain):
    params = (w_query, w_key, w_value, w_output, w_gate, w_up, w_down, attn_gain, ffn_gain, query_gain, key_gain)

    def one_sequence(totals, operands):
        seq_inputs, seq_len, seq_positions, seq_cotangent = operands
        outputs, pull = jax.vjp(lambda values, weights: layer(values, seq_len, seq_positions, weights), seq_inputs.astype(jnp.float32), params)
        grad_inputs, grad_params = pull(seq_cotangent.astype(jnp.float32))
        totals = tuple((total_sum + grad_part for total_sum, grad_part in zip(totals, grad_params)))
        return (totals, (outputs.astype(jnp.bfloat16), grad_inputs))
    start_totals = tuple((jnp.zeros(member.shape, jnp.float32) for member in params))
    totals, outputs = lax.scan(one_sequence, start_totals, (inputs, lengths, positions, cotangent))
    return (outputs[0], outputs[1], totals[0], totals[1], totals[2], totals[3], totals[4], totals[5], totals[6], totals[7], totals[8], totals[9], totals[10])
```

```python
import functools

import jax
import jax.numpy as jnp
from jax import lax
from jax.experimental import pallas as pl
from jax.experimental.pallas import tpu as pltpu
from jax.sharding import PartitionSpec as P

HEADS = 16
KV_HEADS = 8
HEAD = 64
GROUP = HEADS // KV_HEADS


epsilon = 1e-05
rope_base = 1000000.0
masked = -1e30
F32 = jnp.float32
BF16 = jnp.bfloat16


def rms_scale(values, scales):
    return values * lax.rsqrt(jnp.mean(values * values, axis=-1, keepdims=True) + epsilon) * scales


def rotate(values, cosine, sine_part):
    half_width = values.shape[-1] // 2
    first_half = values[..., :half_width]
    second_half = values[..., half_width:]
    return jnp.concatenate(
        [
            first_half * cosine - second_half * sine_part,
            second_half * cosine + first_half * sine_part,
        ],
        axis=-1,
    )


def angles(positions, head_width):
    frequency = rope_base ** (-jnp.arange(0, head_width, 2).astype(F32) / head_width)
    turned = positions.astype(F32)[..., None] * frequency
    return (jnp.cos(turned), jnp.sin(turned))


def prepare(shaped, scales, cosine, sine_part):
    return rotate(rms_scale(shaped, scales), cosine[:, None], sine_part[:, None])


def swiglu(gate_proj, up_proj):
    return gate_proj * jax.nn.sigmoid(gate_proj) * up_proj


def dot_over(left, right, left_dim, right_dim):
    return lax.dot_general(
        left, right, (((left_dim,), (right_dim,)), ((), ())), preferred_element_type=F32
    )


def product(left, right):
    return dot_over(left, right, 1, 0)


def by_transpose(left, right):
    return dot_over(left, right, 1, 1)


def transpose_by(left, right):
    return dot_over(left, right, 0, 0)


def swap(values, axis, step):
    size = lax.axis_size(axis)
    return lax.ppermute(values, axis, [(i, i ^ step) for i in range(size)])


def pick(values, index, axis=0):
    return lax.dynamic_index_in_dim(values, index, axis, keepdims=False)


def gather_near(values):
    far = swap(values, "fsdp", 2)
    near = swap(values, "fsdp", 1)
    return [values, near, far, swap(far, "fsdp", 1)]


def scatter_near(blocks):
    got = swap(jnp.concatenate([blocks[1], blocks[3]], axis=0), "fsdp", 1)
    rows = blocks[0].shape[0]
    mine = blocks[0].astype(F32) + got[:rows].astype(F32)
    far = (blocks[2].astype(F32) + got[rows:].astype(F32)).astype(BF16)
    return mine, swap(far, "fsdp", 2)


def ctx_bits():
    size = lax.axis_size("ctx")
    bits = []
    step = 1
    while step < size:
        bits.append(step)
        step *= 2
    return bits


def ctx_scatter(values, axis):
    me = lax.axis_index("ctx")
    for step in ctx_bits():
        shape = values.shape
        halves = values.reshape(shape[:axis] + (2, shape[axis] // 2) + shape[axis + 1 :])
        mine = (me // step) % 2
        got = swap(pick(halves, 1 - mine, axis), "ctx", step)
        values = (pick(halves, mine, axis).astype(F32) + got.astype(F32)).astype(BF16)
    return values


def ctx_gather(values, axis):
    me = lax.axis_index("ctx")
    for step in reversed(ctx_bits()):
        mine = (me // step) % 2
        got = swap(values, "ctx", step)
        first = jnp.where(mine == 0, values, got)
        second = jnp.where(mine == 0, got, values)
        values = jnp.concatenate([first, second], axis=axis)
    return values


def two_heads(block):
    return jnp.concatenate([block[:, :HEAD], block[:, HEAD:]], axis=0)


def side_by_side(stacked):
    rows = stacked.shape[0] // 2
    return jnp.concatenate([stacked[:rows], stacked[rows:]], axis=1)


def allowed_mask(rows, count, first_query, first_key, seq_len):
    query_slot = first_query + lax.broadcasted_iota(jnp.int32, (rows, count), 0) % (rows // GROUP)
    key_slot = first_key + lax.broadcasted_iota(jnp.int32, (rows, count), 1)
    return (key_slot <= query_slot) & (key_slot < seq_len)


def whole_row(q_ref, kv_ref, index, seq_len):
    slots = q_ref.shape[2]
    count = (index + 1) * slots
    query = two_heads(q_ref[index, 0]) * (HEAD**-0.5)
    both = kv_ref[: index + 1, 0].reshape(count, 2 * HEAD)
    key, value = both[:, :HEAD], both[:, HEAD:]
    scores = by_transpose(query, key)
    scores = jnp.where(
        allowed_mask(GROUP * slots, count, index * slots, 0, seq_len), scores, masked
    )
    exponent = jnp.exp(scores - jnp.max(scores, axis=-1, keepdims=True))
    weights = exponent * (1.0 / jnp.sum(exponent, axis=-1, keepdims=True))
    return query, key, value, weights


def forward_small(info_ref, q_ref, kv_ref, out_ref):
    seq_len = info_ref[pl.program_id(0) + 1]
    slots = q_ref.shape[2]
    for index in range(q_ref.shape[0]):

        @pl.when(index * slots < seq_len)
        def _():
            _, _, value, weights = whole_row(q_ref, kv_ref, index, seq_len)
            out_ref[index, 0] = side_by_side(product(weights.astype(BF16), value)).astype(BF16)

        @pl.when(index * slots >= seq_len)
        def _():
            out_ref[index, 0] = jnp.zeros(out_ref.shape[2:], BF16)


def backward_small(info_ref, q_ref, kv_ref, grad_ref, out_ref, key_acc, value_acc):
    seq_len = info_ref[pl.program_id(0) + 1]
    blocks, _, slots, _ = q_ref.shape
    key_acc[...] = jnp.zeros_like(key_acc)
    value_acc[...] = jnp.zeros_like(value_acc)
    for index in range(blocks):

        @pl.when(index * slots < seq_len)
        def _():
            count = (index + 1) * slots
            query, key, value, weights = whole_row(q_ref, kv_ref, index, seq_len)
            grad = two_heads(grad_ref[index, 0])
            grad_weights = by_transpose(grad, value)
            delta = jnp.sum(weights * grad_weights, axis=-1, keepdims=True)
            grad_scores = (weights * (grad_weights - delta)).astype(BF16)
            out_ref[index, 0, :, : 2 * HEAD] = side_by_side(
                product(grad_scores, key) * (HEAD**-0.5)
            ).astype(BF16)
            key_acc[:count] += transpose_by(grad_scores, query)
            value_acc[:count] += transpose_by(weights.astype(BF16), grad)

        @pl.when(index * slots >= seq_len)
        def _():
            out_ref[index, 0, :, : 2 * HEAD] = jnp.zeros((slots, 2 * HEAD), BF16)

    for index in range(blocks):
        rows = slice(index * slots, (index + 1) * slots)
        out_ref[index, 0, :, 2 * HEAD :] = jnp.concatenate(
            [key_acc[rows], value_acc[rows]], axis=1
        ).astype(BF16)


def row_stats(query, kv_ref, index, first_query, seq_len):
    slots = kv_ref.shape[2]
    rows = query.shape[0]

    def scores_of(block):
        both = kv_ref[block, 0]
        scores = by_transpose(query, both[:, :HEAD])
        allowed = allowed_mask(rows, slots, first_query, block * slots, seq_len)
        return both, jnp.where(allowed, scores, masked)

    def step(block, state):
        top, total = state
        _, scores = scores_of(block)
        new_top = jnp.maximum(top, jnp.max(scores, axis=-1, keepdims=True))
        grown = jnp.sum(jnp.exp(scores - new_top), axis=-1, keepdims=True)
        return new_top, total * jnp.exp(top - new_top) + grown

    start = (jnp.full((rows, 1), masked, F32), jnp.zeros((rows, 1), F32))
    top, total = lax.fori_loop(0, index + 1, step, start)
    inverse = 1.0 / total

    def weights_of(block):
        both, scores = scores_of(block)
        return both, jnp.exp(scores - top) * inverse

    return weights_of


def forward_large(info_ref, q_ref, kv_ref, out_ref):
    seq_len = info_ref[pl.program_id(0) + 1]
    slots = q_ref.shape[2]
    index = info_ref[0] + pl.program_id(1)
    live = index * slots < seq_len

    @pl.when(live)
    def _():
        query = two_heads(q_ref[0, 0]) * (HEAD**-0.5)
        weights_of = row_stats(query, kv_ref, index, index * slots, seq_len)

        def step(block, total):
            both, weights = weights_of(block)
            return total + product(weights.astype(BF16), both[:, HEAD:])

        total = lax.fori_loop(0, index + 1, step, jnp.zeros((GROUP * slots, HEAD), F32))
        out_ref[0, 0] = side_by_side(total).astype(BF16)

    @pl.when(jnp.logical_not(live))
    def _():
        out_ref[0, 0] = jnp.zeros(out_ref.shape[2:], BF16)


def backward_large(info_ref, q_ref, kv_ref, grad_ref, out_ref, kv_out_ref):
    seq_len = info_ref[pl.program_id(0) + 1]
    slots = q_ref.shape[2]
    index = info_ref[0] + pl.program_id(1)
    live = index * slots < seq_len

    @pl.when(pl.program_id(1) == 0)
    def _():
        kv_out_ref[...] = jnp.zeros_like(kv_out_ref)

    @pl.when(live)
    def _():
        query = two_heads(q_ref[0, 0]) * (HEAD**-0.5)
        grad = two_heads(grad_ref[0, 0])
        weights_of = row_stats(query, kv_ref, index, index * slots, seq_len)

        def delta_step(block, total):
            both, weights = weights_of(block)
            grad_weights = by_transpose(grad, both[:, HEAD:])
            return total + jnp.sum(weights * grad_weights, axis=-1, keepdims=True)

        delta = lax.fori_loop(0, index + 1, delta_step, jnp.zeros((GROUP * slots, 1), F32))

        def step(block, total):
            both, weights = weights_of(block)
            grad_weights = by_transpose(grad, both[:, HEAD:])
            grad_scores = (weights * (grad_weights - delta)).astype(BF16)
            kv_out_ref[block, 0] += jnp.concatenate(
                [transpose_by(grad_scores, query), transpose_by(weights.astype(BF16), grad)], axis=1
            )
            return total + product(grad_scores, both[:, :HEAD])

        total = lax.fori_loop(0, index + 1, step, jnp.zeros((GROUP * slots, HEAD), F32))
        out_ref[0, 0] = side_by_side(total * (HEAD**-0.5)).astype(BF16)

    @pl.when(jnp.logical_not(live))
    def _():
        out_ref[0, 0] = jnp.zeros(out_ref.shape[2:], BF16)


def attention_cost(q_blocks, k_blocks, seqs, slots, products):
    pairs = seqs * GROUP * q_blocks * k_blocks * slots * slots // 2
    return pl.CostEstimate(
        flops=pairs * HEAD * 2 * products,
        transcendentals=pairs,
        bytes_accessed=4 * seqs * slots * 4 * HEAD * (q_blocks + k_blocks),
    )


def attention(info, mixed, shared, grad=None):
    blocks, seqs, slots, _ = mixed.shape
    wide = 2 * HEAD
    small = shared is mixed
    k_blocks = shared.shape[0]
    params = dict(vmem_limit_bytes=48 * 1024 * 1024)
    cost = attention_cost(blocks, k_blocks, seqs, slots, 2 if grad is None else 5)
    if small:
        whole = lambda part: pl.BlockSpec(
            (blocks, 1, slots, wide), lambda seq, info: (0, seq, 0, part)
        )
        if grad is None:
            return pl.pallas_call(
                forward_small,
                out_shape=jax.ShapeDtypeStruct((blocks, seqs, slots, wide), BF16),
                grid_spec=pltpu.PrefetchScalarGridSpec(
                    num_scalar_prefetch=1,
                    grid=(seqs,),
                    in_specs=[whole(0), whole(1)],
                    out_specs=whole(0),
                ),
                compiler_params=pltpu.CompilerParams(**params),
                cost_estimate=cost,
            )(info, mixed, mixed)
        return pl.pallas_call(
            backward_small,
            out_shape=jax.ShapeDtypeStruct((blocks, seqs, slots, 2 * wide), BF16),
            grid_spec=pltpu.PrefetchScalarGridSpec(
                num_scalar_prefetch=1,
                grid=(seqs,),
                in_specs=[whole(0), whole(1), whole(0)],
                out_specs=pl.BlockSpec(
                    (blocks, 1, slots, 2 * wide), lambda seq, info: (0, seq, 0, 0)
                ),
                scratch_shapes=[pltpu.VMEM((blocks * slots, HEAD), F32)] * 2,
            ),
            compiler_params=pltpu.CompilerParams(**params),
            cost_estimate=cost,
        )(info, mixed, mixed, grad)
    one = pl.BlockSpec((1, 1, slots, wide), lambda seq, block, info: (block, seq, 0, 0))
    every = pl.BlockSpec((k_blocks, 1, slots, wide), lambda seq, block, info: (0, seq, 0, 0))
    out = jax.ShapeDtypeStruct((blocks, seqs, slots, wide), BF16)
    if grad is None:
        return pl.pallas_call(
            forward_large,
            out_shape=out,
            grid_spec=pltpu.PrefetchScalarGridSpec(
                num_scalar_prefetch=1, grid=(seqs, blocks), in_specs=[one, every], out_specs=one
            ),
            compiler_params=pltpu.CompilerParams(**params),
            cost_estimate=cost,
        )(info, mixed, shared)
    return pl.pallas_call(
        backward_large,
        out_shape=(out, jax.ShapeDtypeStruct((k_blocks, seqs, slots, wide), F32)),
        grid_spec=pltpu.PrefetchScalarGridSpec(
            num_scalar_prefetch=1,
            grid=(seqs, blocks),
            in_specs=[one, every, one],
            out_specs=(one, every),
        ),
        compiler_params=pltpu.CompilerParams(**params),
        cost_estimate=cost,
    )(info, mixed, shared, grad)


def per_device(
    inputs,
    lengths,
    positions,
    cotangent,
    w_query,
    w_key,
    w_value,
    w_output,
    w_gate,
    w_up,
    w_down,
    attn_gain,
    ffn_gain,
    query_gain,
    key_gain,
):
    groups, slot_count, model_width = inputs.shape
    row_count = groups * slot_count
    own_rows = w_query.shape[0]
    ctx_size = lax.axis_size("ctx")
    fsdp_size = lax.axis_size("fsdp")
    me_f = lax.axis_index("fsdp")
    me_c = lax.axis_index("ctx")
    inner = min(ctx_size, KV_HEADS)
    outer = ctx_size // inner
    inner_groups = [[o * inner + i for i in range(inner)] for o in range(outer)]
    outer_groups = [[o * inner + i for o in range(outer)] for i in range(inner)]
    mix = 4 * HEAD
    ff_own = w_down.shape[0]

    slots = me_c * slot_count + jnp.arange(slot_count)
    valid = (slots[None, :] < lengths[:, None]).astype(F32).reshape(row_count, 1)
    info = jnp.concatenate([(me_c // inner * inner)[None].astype(jnp.int32), lengths])

    gains = jnp.concatenate([attn_gain, ffn_gain, query_gain, key_gain]).astype(BF16)
    gains = lax.all_gather(gains, "fsdp", axis=0, tiled=False).astype(F32)
    small = query_gain.shape[0]
    attn_scale = gains[:, :own_rows].reshape(-1)
    ffn_scale = gains[:, own_rows : 2 * own_rows].reshape(-1)
    qgain_scale = gains[:, 2 * own_rows : 2 * own_rows + small].reshape(-1)
    kgain_scale = gains[:, 2 * own_rows + small :].reshape(-1)

    qkv_own = jnp.concatenate(
        [
            w_query.reshape(own_rows, KV_HEADS, GROUP * HEAD),
            w_key.reshape(own_rows, KV_HEADS, HEAD),
            w_value.reshape(own_rows, KV_HEADS, HEAD),
        ],
        axis=-1,
    ).astype(BF16)
    qkv_weight = lax.all_gather(
        qkv_own.reshape(own_rows, KV_HEADS * mix), "fsdp", axis=0, tiled=True
    )
    output_weight = lax.all_gather(w_output.astype(BF16), "fsdp", axis=0, tiled=True)
    down_weight = w_down.astype(BF16)
    gu_own = jnp.concatenate(
        [
            w_gate.reshape(own_rows, fsdp_size, ff_own),
            w_up.reshape(own_rows, fsdp_size, ff_own),
        ],
        axis=-1,
    ).astype(BF16)
    gu_own = gu_own.transpose(1, 0, 2)
    gu_parts = [pick(gu_own, me_f)]
    for step in range(1, fsdp_size):
        gu_parts.append(swap(pick(gu_own, me_f ^ step), "fsdp", step))
    gu_weight = jnp.zeros_like(gu_own)
    for step in range(fsdp_size):
        gu_weight = lax.dynamic_update_index_in_dim(gu_weight, gu_parts[step], me_f ^ step, 0)
    gu_weight = gu_weight.reshape(fsdp_size * own_rows, 2 * ff_own)

    flat = inputs.reshape(row_count, model_width).astype(F32)
    cosine, sine_part = angles(positions.reshape(row_count), HEAD)
    normed_low = rms_scale(flat, attn_scale).astype(BF16)
    projected = product(normed_low, qkv_weight).reshape(row_count, KV_HEADS, mix)
    query_proj = projected[..., : GROUP * HEAD].reshape(row_count, HEADS, HEAD)
    key_proj = projected[..., GROUP * HEAD : GROUP * HEAD + HEAD]
    query_low = prepare(query_proj, qgain_scale, cosine, sine_part).astype(BF16)
    key_low = prepare(key_proj, kgain_scale, cosine, sine_part).astype(BF16)
    value_low = projected[..., GROUP * HEAD + HEAD :].astype(BF16)
    mixed = jnp.concatenate(
        [query_low.reshape(row_count, KV_HEADS, GROUP * HEAD), key_low, value_low], axis=-1
    ).transpose(1, 0, 2)

    def exchange(values):
        shape = values.shape
        return lax.all_to_all(values, "ctx", 0, 0, axis_index_groups=inner_groups, tiled=True)

    heads_each = KV_HEADS // inner
    mixed = exchange(mixed).reshape(inner, heads_each, groups, slot_count, mix)
    mixed = mixed.transpose(0, 1, 2, 3, 4).reshape(inner, heads_each * groups, slot_count, mix)
    if outer == 1:
        shared = mixed
    else:
        shared = lax.all_gather(
            mixed[..., 2 * HEAD :], "ctx", axis=0, axis_index_groups=outer_groups, tiled=True
        )
    attended = attention(info, mixed, shared)
    attended_low = (
        exchange(attended.reshape(KV_HEADS, row_count, 2 * HEAD))
        .transpose(1, 0, 2)
        .reshape(row_count, HEADS * HEAD)
    )
    hidden_res = flat + product(attended_low, output_weight)

    mid_low = rms_scale(hidden_res, ffn_scale).astype(BF16)
    mid_all = jnp.concatenate(gather_near(mid_low), axis=0)
    outer_grad = cotangent.reshape(row_count, model_width).astype(F32) * valid
    outer_low = outer_grad.astype(BF16)
    outer_all = jnp.concatenate(gather_near(outer_low), axis=0)
    gate_up = product(mid_all, gu_weight)
    gate_proj, up_proj = gate_up[:, :ff_own], gate_up[:, ff_own:]
    inner_low = swiglu(gate_proj, up_proj).astype(BF16)
    down_part = transpose_by(inner_low, outer_all).astype(BF16)
    down_sum = ctx_scatter(down_part.reshape(ctx_size, ff_own // ctx_size, model_width), 0)
    grad_inner = by_transpose(outer_all, down_weight)
    _, pull_swiglu = jax.vjp(swiglu, gate_proj, up_proj)
    grad_gate, grad_up = pull_swiglu(grad_inner)
    grad_gu = jnp.concatenate([grad_gate.astype(BF16), grad_up.astype(BF16)], axis=-1)
    grad_mid_part = by_transpose(grad_gu, gu_weight).astype(BF16)
    mine, far = scatter_near(jnp.split(grad_mid_part, fsdp_size, axis=0))
    grad_mid = mine + far.astype(F32)
    gu_part = transpose_by(mid_all, grad_gu).astype(BF16)
    gu_sum = ctx_scatter(
        gu_part.reshape(fsdp_size, ctx_size, own_rows // ctx_size, 2 * ff_own), 1
    )
    result_part = product(inner_low, down_weight).astype(BF16)
    mine, far = scatter_near(jnp.split(result_part, fsdp_size, axis=0))
    result = valid * (hidden_res + (mine + far.astype(F32)))
    block_output = result.astype(BF16).reshape(groups, slot_count, model_width)

    _, pull_mid = jax.vjp(rms_scale, hidden_res, ffn_scale)
    grad_hidden_norm, ffn_part = pull_mid(grad_mid)
    grad_hidden = outer_grad + grad_hidden_norm
    grad_attn_low = grad_hidden.astype(BF16)

    output_part = transpose_by(attended_low, grad_attn_low).astype(BF16)
    grad_heads_low = by_transpose(grad_attn_low, output_weight).astype(BF16)
    grad_heads = exchange(
        grad_heads_low.reshape(row_count, KV_HEADS, 2 * HEAD).transpose(1, 0, 2)
    ).reshape(inner, heads_each * groups, slot_count, 2 * HEAD)
    if outer == 1:
        grad_mixed = attention(info, mixed, shared, grad_heads)
    else:
        grad_q, grad_kv = attention(info, mixed, shared, grad_heads)
        grad_kv = lax.psum_scatter(
            grad_kv, "ctx", scatter_dimension=0, axis_index_groups=outer_groups, tiled=True
        )
        grad_mixed = jnp.concatenate([grad_q, grad_kv.astype(BF16)], axis=-1)
    grad_mixed = exchange(grad_mixed.reshape(KV_HEADS, row_count, mix)).transpose(1, 0, 2)
    grad_query_rot = grad_mixed[..., : GROUP * HEAD].astype(F32).reshape(row_count, HEADS, HEAD)
    grad_key_rot = grad_mixed[..., GROUP * HEAD : GROUP * HEAD + HEAD].astype(F32)
    grad_value_low = grad_mixed[..., GROUP * HEAD + HEAD :]
    _, pull_query = jax.vjp(
        lambda shaped, scales: prepare(shaped, scales, cosine, sine_part), query_proj, qgain_scale
    )
    grad_query_proj, qgain_part = pull_query(grad_query_rot)
    _, pull_key = jax.vjp(
        lambda shaped, scales: prepare(shaped, scales, cosine, sine_part), key_proj, kgain_scale
    )
    grad_key_proj, kgain_part = pull_key(grad_key_rot)
    grad_qkv = jnp.concatenate(
        [
            grad_query_proj.astype(BF16).reshape(row_count, KV_HEADS, GROUP * HEAD),
            grad_key_proj.astype(BF16),
            grad_value_low,
        ],
        axis=-1,
    ).reshape(row_count, KV_HEADS * mix)
    qkv_part = transpose_by(normed_low, grad_qkv).astype(BF16)
    grad_normed = by_transpose(grad_qkv, qkv_weight)
    _, pull_input = jax.vjp(rms_scale, flat, attn_scale)
    grad_flat_norm, attn_part = pull_input(grad_normed)
    input_grad = (grad_hidden + grad_flat_norm).reshape(groups, slot_count, model_width)

    gain_parts = jnp.concatenate(
        [
            attn_part.reshape(fsdp_size, own_rows),
            ffn_part.reshape(fsdp_size, own_rows),
            qgain_part.reshape(fsdp_size, small),
            kgain_part.reshape(fsdp_size, small),
        ],
        axis=-1,
    )
    gain_sum = pick(lax.psum(gain_parts, ("ctx", "fsdp")), me_f)

    def own_block(part):
        blocks = part.reshape(fsdp_size, own_rows, part.shape[1])
        mine, far = scatter_near([pick(blocks, me_f ^ k) for k in range(fsdp_size)])
        return (mine + far.astype(F32)).astype(BF16)

    def ctx_sum(own):
        blocks = own.reshape(ctx_size, own_rows // ctx_size, own.shape[1])
        return ctx_gather(ctx_scatter(blocks, 0), 0).reshape(own.shape)

    output_grad = ctx_sum(own_block(output_part)).astype(F32)
    qkv_grad = ctx_sum(own_block(qkv_part)).reshape(own_rows, KV_HEADS, mix)
    query_grad = qkv_grad[..., : GROUP * HEAD].reshape(own_rows, HEADS * HEAD).astype(F32)
    key_grad = (
        qkv_grad[..., GROUP * HEAD : GROUP * HEAD + HEAD]
        .reshape(own_rows, KV_HEADS * HEAD)
        .astype(F32)
    )
    value_grad = (
        qkv_grad[..., GROUP * HEAD + HEAD :].reshape(own_rows, KV_HEADS * HEAD).astype(F32)
    )
    down_grad = ctx_gather(down_sum, 0).reshape(ff_own, model_width).astype(F32)

    gu_sum = gu_sum.reshape(fsdp_size, own_rows // ctx_size, 2 * ff_own)
    gu_rows = jnp.zeros_like(gu_sum)
    for step in range(fsdp_size):
        block = pick(gu_sum, me_f ^ step)
        if step:
            block = swap(block, "fsdp", step)
        gu_rows = lax.dynamic_update_index_in_dim(gu_rows, block, me_f ^ step, 0)
    gu_all = ctx_gather(gu_rows[None], 0)
    gu_all = gu_all.transpose(0, 2, 1, 3).reshape(own_rows, fsdp_size, 2 * ff_own)
    gate_grad = gu_all[..., :ff_own].reshape(own_rows, fsdp_size * ff_own).astype(F32)
    up_grad = gu_all[..., ff_own:].reshape(own_rows, fsdp_size * ff_own).astype(F32)

    return (
        block_output,
        input_grad,
        query_grad,
        key_grad,
        value_grad,
        output_grad,
        gate_grad,
        up_grad,
        down_grad,
        gain_sum[:own_rows],
        gain_sum[own_rows : 2 * own_rows],
        gain_sum[2 * own_rows : 2 * own_rows + small],
        gain_sum[2 * own_rows + small :],
    )


def solution(mesh):
    return jax.shard_map(
        per_device,
        mesh=mesh,
        in_specs=(
            P("fsdp", "ctx", None),
            P("fsdp"),
            P("fsdp", "ctx"),
            P("fsdp", "ctx", None),
            P("fsdp", None),
            P("fsdp", None),
            P("fsdp", None),
            P("fsdp", None),
            P("fsdp", None),
            P("fsdp", None),
            P("fsdp", None),
            P("fsdp"),
            P("fsdp"),
            P("fsdp"),
            P("fsdp"),
        ),
        out_specs=(
            P("fsdp", "ctx", None),
            P("fsdp", "ctx", None),
            P("fsdp", None),
            P("fsdp", None),
            P("fsdp", None),
            P("fsdp", None),
            P("fsdp", None),
            P("fsdp", None),
            P("fsdp", None),
            P("fsdp"),
            P("fsdp"),
            P("fsdp"),
            P("fsdp"),
        ),
        check_vma=False,
    )
```

```python
import jax
import jax.numpy as jnp
from jax import lax
from jax.experimental import pallas as pl
from jax.experimental.pallas import tpu as pltpu
from jax.sharding import PartitionSpec as P

HEADS = 16
KV_HEADS = 8
HEAD = 64
GROUP = HEADS // KV_HEADS


epsilon = 1e-05
rope_base = 1000000.0
masked = -1e30
F32 = jnp.float32
BF16 = jnp.bfloat16


def dot_over(left, right, left_dim, right_dim):
    return lax.dot_general(
        left, right, (((left_dim,), (right_dim,)), ((), ())), preferred_element_type=F32
    )


def product(left, right):
    return dot_over(left, right, 1, 0)


def by_transpose(left, right):
    return dot_over(left, right, 1, 1)


def transpose_by(left, right):
    return dot_over(left, right, 0, 0)


PLANE = 8


def trade(values, step):
    size = lax.axis_size("ctx") * lax.axis_size("fsdp")
    return lax.ppermute(values, ("ctx", "fsdp"), [(i, i ^ step) for i in range(size)])


def pick(values, index, axis=0):
    return lax.dynamic_index_in_dim(values, index, axis, keepdims=False)


class Line:
    def __init__(self):
        self.last = None

    def __call__(self, step, *operands):
        if self.last is not None:
            operands = lax.optimization_barrier((*operands, self.last))[:-1]
        result = step(*operands)
        self.last = jax.tree.leaves(result)[0]
        return result

    def wait(self, *values):
        *values, self.last = lax.optimization_barrier((*values, self.last))
        return values


def add_low(first, second):
    return (first.astype(F32) + second.astype(F32)).astype(BF16)


def halves(values):
    half = values.shape[0] // 2
    return values[:half], values[half:]


def cut_far(over_x, over_y):
    return halves(over_x)[0], halves(over_y)[1]


def gather_plane(values, over_x, over_y, corner):
    far = [values, over_x, over_y, *corner]
    return [trade(block, 1) for block in far] + far


def plane_groups():
    size = lax.axis_size("ctx") * lax.axis_size("fsdp")
    return [list(range(start, start + PLANE)) for start in range(0, size, PLANE)]


def cut_plane(send_got, keep):
    pair = add_low(keep, send_got).reshape(4, -1, keep.shape[1])
    half = pair.shape[1] // 2
    low, high = pair[:, :half], pair[:, half:]
    return jnp.stack([low[1], low[3]]), jnp.stack([high[2], high[3]]), low[::2], high[:2]


def join_plane(low, high, low_got, high_got):
    low_own = low[0].astype(F32) + low_got[0].astype(F32)
    high_own = high[0].astype(F32) + high_got[0].astype(F32)
    return add_low(low[1], low_got[1]), add_low(high[1], high_got[1]), low_own, high_own


def cut_near(part, me_f):
    blocks = [pick(part, me_f ^ k) for k in range(4)]
    return jnp.stack([blocks[1], blocks[3]]), jnp.stack([blocks[0], blocks[2]])


def gather_near(values):
    far = trade(values, 2)
    near = trade(values, 1)
    return [values, near, far, trade(far, 1)]


def sum_everywhere(values):
    step = 1
    while step < lax.axis_size("ctx") * lax.axis_size("fsdp"):
        values = values + trade(values, step)
        step *= 2
    return values


RING = (0, 1, 3, 2)


def ring_step(values):
    following = {RING[i]: RING[(i + 1) % 4] for i in range(4)}
    pairs = []
    for c in range(lax.axis_size("ctx")):
        outer, place, low = c // 8, c // 2 % 4, c % 2
        pairs.append((c, outer * 8 + following[place] * 2 + low))
    return lax.ppermute(values, "ctx", pairs)


def ring_places(place):
    before = {RING[(i + 1) % 4]: RING[i] for i in range(4)}
    table = []
    for start in range(4):
        row = [start]
        for _ in range(3):
            row.append(before[row[-1]])
        table.append(row)
    return jnp.array(table, jnp.int32)[place]


def plane_step(values, moves):
    size = lax.axis_size("ctx") * lax.axis_size("fsdp")
    pairs = []
    for device in range(size):
        place, rest = device // PLANE, device % PLANE
        pairs += [(device, to * PLANE + rest) for start, to in moves if start == place]
    return lax.ppermute(values, ("ctx", "fsdp"), pairs)


def ctx_bits():
    size = lax.axis_size("ctx")
    bits = []
    step = 1
    while step < size:
        bits.append(step)
        step *= 2
    return bits


def ctx_sum(values):
    me = lax.axis_index("ctx")
    near = lax.axis_size("fsdp")
    for step in ctx_bits():
        shape = values.shape
        halves = values.reshape((2, shape[0] // 2) + shape[1:])
        mine = (me // step) % 2
        got = trade(pick(halves, 1 - mine), step * near)
        values = (pick(halves, mine).astype(F32) + got.astype(F32)).astype(BF16)
    for step in reversed(ctx_bits()):
        mine = (me // step) % 2
        got = trade(values, step * near)
        first = jnp.where(mine == 0, values, got)
        second = jnp.where(mine == 0, got, values)
        values = jnp.concatenate([first, second], axis=0)
    return values


def two_heads(block):
    return jnp.concatenate([block[:, :HEAD], block[:, HEAD:]], axis=0)


def side_by_side(stacked):
    rows = stacked.shape[0] // 2
    return jnp.concatenate([stacked[:rows], stacked[rows:]], axis=1)


def allowed_mask(rows, count, first_query, first_key, seq_len):
    query_slot = first_query + lax.broadcasted_iota(jnp.int32, (rows, count), 0) % (rows // GROUP)
    key_slot = first_key + lax.broadcasted_iota(jnp.int32, (rows, count), 1)
    return (key_slot <= query_slot) & (key_slot < seq_len)


def whole_row(q_ref, kv_ref, index, seq_len):
    slots = q_ref.shape[2]
    count = (index + 1) * slots
    query = two_heads(q_ref[index, 0]) * (HEAD**-0.5)
    both = kv_ref[: index + 1, 0].reshape(count, 2 * HEAD)
    key, value = both[:, :HEAD], both[:, HEAD:]
    scores = by_transpose(query, key)
    scores = jnp.where(
        allowed_mask(GROUP * slots, count, index * slots, 0, seq_len), scores, masked
    )
    exponent = jnp.exp(scores - jnp.max(scores, axis=-1, keepdims=True))
    weights = exponent * (1.0 / jnp.sum(exponent, axis=-1, keepdims=True))
    return query, key, value, weights


def forward_small(info_ref, q_ref, kv_ref, *refs):
    out_ref = refs[-1]
    seq_len = info_ref[pl.program_id(0) + 1]
    slots = q_ref.shape[2]
    for index in range(q_ref.shape[0]):

        @pl.when(index * slots < seq_len)
        def _():
            _, _, value, weights = whole_row(q_ref, kv_ref, index, seq_len)
            out_ref[index, 0] = side_by_side(product(weights.astype(BF16), value)).astype(BF16)

        @pl.when(index * slots >= seq_len)
        def _():
            out_ref[index, 0] = jnp.zeros(out_ref.shape[2:], BF16)


def backward_small(info_ref, q_ref, kv_ref, grad_ref, *refs):
    out_ref, key_acc, value_acc = refs[-3:]
    seq_len = info_ref[pl.program_id(0) + 1]
    blocks, _, slots, _ = q_ref.shape
    key_acc[...] = jnp.zeros_like(key_acc)
    value_acc[...] = jnp.zeros_like(value_acc)
    for index in range(blocks):

        @pl.when(index * slots < seq_len)
        def _():
            count = (index + 1) * slots
            query, key, value, weights = whole_row(q_ref, kv_ref, index, seq_len)
            grad = two_heads(grad_ref[index, 0])
            grad_weights = by_transpose(grad, value)
            delta = jnp.sum(weights * grad_weights, axis=-1, keepdims=True)
            grad_scores = (weights * (grad_weights - delta)).astype(BF16)
            out_ref[index, 0, :, : 2 * HEAD] = side_by_side(
                product(grad_scores, key) * (HEAD**-0.5)
            )
            key_acc[:count] += transpose_by(grad_scores, query)
            value_acc[:count] += transpose_by(weights.astype(BF16), grad)

        @pl.when(index * slots >= seq_len)
        def _():
            out_ref[index, 0, :, : 2 * HEAD] = jnp.zeros((slots, 2 * HEAD), F32)

    for index in range(blocks):
        rows = slice(index * slots, (index + 1) * slots)
        out_ref[index, 0, :, 2 * HEAD :] = jnp.concatenate(
            [key_acc[rows], value_acc[rows]], axis=1
        )


def row_stats(query, kv_ref, index, first_query, seq_len):
    slots = kv_ref.shape[2]
    rows = query.shape[0]

    def scores_of(block):
        both = kv_ref[block, 0]
        scores = by_transpose(query, both[:, :HEAD])
        allowed = allowed_mask(rows, slots, first_query, block * slots, seq_len)
        return both, jnp.where(allowed, scores, masked)

    def step(block, state):
        top, total = state
        _, scores = scores_of(block)
        new_top = jnp.maximum(top, jnp.max(scores, axis=-1, keepdims=True))
        grown = jnp.sum(jnp.exp(scores - new_top), axis=-1, keepdims=True)
        return new_top, total * jnp.exp(top - new_top) + grown

    start = (jnp.full((rows, 1), masked, F32), jnp.zeros((rows, 1), F32))
    top, total = lax.fori_loop(0, index + 1, step, start)
    inverse = 1.0 / total

    def weights_of(block):
        both, scores = scores_of(block)
        return both, jnp.exp(scores - top) * inverse

    return weights_of


def forward_large(info_ref, q_ref, kv_ref, out_ref):
    seq_len = info_ref[pl.program_id(0) + 1]
    slots = q_ref.shape[2]
    index = info_ref[0] + pl.program_id(1)
    live = index * slots < seq_len

    @pl.when(live)
    def _():
        query = two_heads(q_ref[0, 0]) * (HEAD**-0.5)
        weights_of = row_stats(query, kv_ref, index, index * slots, seq_len)

        def step(block, total):
            both, weights = weights_of(block)
            return total + product(weights.astype(BF16), both[:, HEAD:])

        total = lax.fori_loop(0, index + 1, step, jnp.zeros((GROUP * slots, HEAD), F32))
        out_ref[0, 0] = side_by_side(total).astype(BF16)

    @pl.when(jnp.logical_not(live))
    def _():
        out_ref[0, 0] = jnp.zeros(out_ref.shape[2:], BF16)


def backward_large(info_ref, q_ref, kv_ref, grad_ref, out_ref, kv_out_ref):
    seq_len = info_ref[pl.program_id(0) + 1]
    slots = q_ref.shape[2]
    index = info_ref[0] + pl.program_id(1)
    live = index * slots < seq_len

    @pl.when(pl.program_id(1) == 0)
    def _():
        kv_out_ref[...] = jnp.zeros_like(kv_out_ref)

    @pl.when(live)
    def _():
        query = two_heads(q_ref[0, 0]) * (HEAD**-0.5)
        grad = two_heads(grad_ref[0, 0])
        weights_of = row_stats(query, kv_ref, index, index * slots, seq_len)

        def delta_step(block, total):
            both, weights = weights_of(block)
            grad_weights = by_transpose(grad, both[:, HEAD:])
            return total + jnp.sum(weights * grad_weights, axis=-1, keepdims=True)

        delta = lax.fori_loop(0, index + 1, delta_step, jnp.zeros((GROUP * slots, 1), F32))

        def step(block, total):
            both, weights = weights_of(block)
            grad_weights = by_transpose(grad, both[:, HEAD:])
            grad_scores = (weights * (grad_weights - delta)).astype(BF16)
            kv_out_ref[block, 0] += jnp.concatenate(
                [transpose_by(grad_scores, query), transpose_by(weights.astype(BF16), grad)], axis=1
            )
            return total + product(grad_scores, both[:, :HEAD])

        total = lax.fori_loop(0, index + 1, step, jnp.zeros((GROUP * slots, HEAD), F32))
        out_ref[0, 0] = side_by_side(total * (HEAD**-0.5))

    @pl.when(jnp.logical_not(live))
    def _():
        out_ref[0, 0] = jnp.zeros(out_ref.shape[2:], F32)


def attention_cost(q_blocks, k_blocks, seqs, slots, products):
    pairs = seqs * GROUP * q_blocks * k_blocks * slots * slots // 2
    return pl.CostEstimate(
        flops=pairs * HEAD * 2 * products,
        transcendentals=pairs,
        bytes_accessed=4 * seqs * slots * 4 * HEAD * (q_blocks + k_blocks),
    )


def attention(info, mixed, shared, grad=None, awaited=()):
    blocks, seqs, slots, _ = mixed.shape
    wide = 2 * HEAD
    small = shared is mixed
    k_blocks = shared.shape[0]
    params = dict(vmem_limit_bytes=48 * 1024 * 1024)
    cost = attention_cost(blocks, k_blocks, seqs, slots, 2 if grad is None else 5)
    if small:
        whole = lambda part: pl.BlockSpec(
            (blocks, 1, slots, wide), lambda seq, info: (0, seq, 0, part)
        )
        if grad is None:
            return pl.pallas_call(
                forward_small,
                out_shape=jax.ShapeDtypeStruct((blocks, seqs, slots, wide), BF16),
                grid_spec=pltpu.PrefetchScalarGridSpec(
                    num_scalar_prefetch=1,
                    grid=(seqs,),
                    in_specs=[whole(0), whole(1)]
                    + [pl.BlockSpec(memory_space=pl.ANY)] * len(awaited),
                    out_specs=whole(0),
                ),
                compiler_params=pltpu.CompilerParams(**params),
                cost_estimate=cost,
            )(info, mixed, mixed, *awaited)
        return pl.pallas_call(
            backward_small,
            out_shape=jax.ShapeDtypeStruct((blocks, seqs, slots, 2 * wide), F32),
            grid_spec=pltpu.PrefetchScalarGridSpec(
                num_scalar_prefetch=1,
                grid=(seqs,),
                in_specs=[whole(0), whole(1), whole(0)]
                + [pl.BlockSpec(memory_space=pl.ANY)] * len(awaited),
                out_specs=pl.BlockSpec(
                    (blocks, 1, slots, 2 * wide), lambda seq, info: (0, seq, 0, 0)
                ),
                scratch_shapes=[pltpu.VMEM((blocks * slots, HEAD), F32)] * 2,
            ),
            compiler_params=pltpu.CompilerParams(**params),
            cost_estimate=cost,
        )(info, mixed, mixed, grad, *awaited)
    one = pl.BlockSpec((1, 1, slots, wide), lambda seq, block, info: (block, seq, 0, 0))
    every = pl.BlockSpec((k_blocks, 1, slots, wide), lambda seq, block, info: (0, seq, 0, 0))
    out = jax.ShapeDtypeStruct((blocks, seqs, slots, wide), BF16)
    if grad is None:
        return pl.pallas_call(
            forward_large,
            out_shape=out,
            grid_spec=pltpu.PrefetchScalarGridSpec(
                num_scalar_prefetch=1, grid=(seqs, blocks), in_specs=[one, every], out_specs=one
            ),
            compiler_params=pltpu.CompilerParams(**params),
            cost_estimate=cost,
        )(info, mixed, shared)
    return pl.pallas_call(
        backward_large,
        out_shape=(
            jax.ShapeDtypeStruct((blocks, seqs, slots, wide), F32),
            jax.ShapeDtypeStruct((k_blocks, seqs, slots, wide), F32),
        ),
        grid_spec=pltpu.PrefetchScalarGridSpec(
            num_scalar_prefetch=1,
            grid=(seqs, blocks),
            in_specs=[one, every, one],
            out_specs=(one, every),
        ),
        compiler_params=pltpu.CompilerParams(**params),
        cost_estimate=cost,
    )(info, mixed, shared, grad)


POSITION_ROWS = 16
POSITION_BASE = 256


def lane_of(shape):
    return lax.broadcasted_iota(jnp.int32, shape, 1)


def head_mean(values):
    lanes = values.shape[1]
    same = (
        lax.broadcasted_iota(jnp.int32, (lanes, lanes), 0) // HEAD
        == lax.broadcasted_iota(jnp.int32, (lanes, lanes), 1) // HEAD
    )
    ones = jnp.where(same, 1.0, 0.0).astype(BF16)
    high = values.astype(BF16)
    rest = values - high.astype(F32)
    middle = rest.astype(BF16)
    low = (rest - middle.astype(F32)).astype(BF16)
    return (product(high, ones) + product(middle, ones) + product(low, ones)) * (1.0 / HEAD)


def turn(values):
    lanes = values.shape[1]
    first = lane_of(values.shape) % HEAD < HEAD // 2
    return jnp.where(
        first,
        -pltpu.roll(values, lanes - HEAD // 2, 1),
        pltpu.roll(values, HEAD // 2, 1),
    )


def project_kernel(info_ref, near_ref, far_ref, weight_ref, gain_ref, head_gain_ref, freq_ref, *rest):
    normed_ref, projected_ref, mixed_ref, cosine_ref, sine_ref = rest[-5:]
    my_row, my_place = info_ref[0], info_ref[1]
    depth = weight_ref.shape[1]
    rows = normed_ref.shape[1]
    wide = 2 * HEAD
    for which, ref in enumerate((near_ref, far_ref)):
        place = my_place if which == 0 else 1 - my_place
        values = ref[:rows].astype(F32)
        scale = lax.rsqrt(jnp.mean(values * values, axis=-1, keepdims=True) + epsilon)
        normed = (values * scale * gain_ref[...]).astype(BF16)
        normed_ref[place] = normed
        total = jnp.zeros((rows, weight_ref.shape[2]), F32)
        for block in range(weight_ref.shape[0]):
            weight = weight_ref[block ^ my_row]
            total = total + product(normed[:, block * depth : (block + 1) * depth], weight)
        projected_ref[place] = total
        digits = ref[rows : rows + POSITION_ROWS, :rows].astype(F32)
        position = digits[0:1] * POSITION_BASE + digits[1:2]
        angle = jnp.broadcast_to(position, (wide, rows)).T * freq_ref[...]
        cosine, sine = jnp.cos(angle), jnp.sin(angle)
        cosine_ref[place] = cosine
        sine_ref[place] = sine
        for part in range(2):
            lanes = slice(part * wide, (part + 1) * wide)
            piece = total[:, lanes]
            scaled = piece * lax.rsqrt(head_mean(piece * piece) + epsilon) * head_gain_ref[:, lanes]
            turned = scaled * cosine + turn(scaled) * sine
            if part == 1:
                turned = jnp.where(lane_of(turned.shape) < HEAD, turned, piece)
            mixed_ref[place, :, lanes] = turned.astype(BF16)


def project(info, near, far, weight, gain, head_gain, frequency, blocks, earlier):
    rows, width = near.shape
    rows -= POSITION_ROWS
    mix = weight.shape[2]
    wide = 2 * HEAD
    whole = lambda *shape: pl.BlockSpec(shape, lambda step, info: (0,) * len(shape))
    pair = lambda last: pl.BlockSpec((2, rows, last), lambda step, info: (info[2], 0, 0))
    outs = ((width, BF16), (mix, F32), (mix, BF16), (wide, F32), (wide, F32))
    in_specs = [
        whole(*near.shape),
        whole(*near.shape),
        whole(*weight.shape),
        whole(1, width),
        whole(1, mix),
        whole(1, wide),
    ]
    aliases = {}
    operands = [near, far, weight, gain, head_gain, frequency]
    if earlier is not None:
        aliases = {1 + len(operands) + i: i for i in range(len(outs))}
        in_specs += [pl.BlockSpec(memory_space=pl.ANY)] * len(outs)
        operands += list(earlier)
    return pl.pallas_call(
        project_kernel,
        out_shape=tuple(jax.ShapeDtypeStruct((blocks, rows, last), kind) for last, kind in outs),
        grid_spec=pltpu.PrefetchScalarGridSpec(
            num_scalar_prefetch=1,
            grid=(1,),
            in_specs=in_specs,
            out_specs=tuple(pair(last) for last, _ in outs),
        ),
        input_output_aliases=aliases,
        compiler_params=pltpu.CompilerParams(vmem_limit_bytes=32 * 1024 * 1024),
        cost_estimate=pl.CostEstimate(
            flops=4 * rows * width * mix, transcendentals=0, bytes_accessed=8 * rows * width
        ),
    )(info, *operands)


def unproject_kernel(
    grad_ref, projected_ref, head_gain_ref, cosine_ref, sine_ref, *refs
):
    out_ref, gain_ref = refs[-2:]
    wide = 2 * HEAD

    @pl.when(pl.program_id(0) == 0)
    def _():
        gain_ref[...] = jnp.zeros_like(gain_ref)

    cosine, sine = cosine_ref[0], sine_ref[0]
    for part in range(2):
        lanes = slice(part * wide, (part + 1) * wide)
        grad = grad_ref[0, :, lanes]
        piece = projected_ref[0, :, lanes]
        back = grad * cosine - turn(grad) * sine
        scale = lax.rsqrt(head_mean(piece * piece) + epsilon)
        hat = piece * scale
        gain_ref[:, lanes] += jnp.sum(back * hat, axis=0, keepdims=True)
        back = back * head_gain_ref[:, lanes]
        back = scale * (back - hat * head_mean(back * hat))
        if part == 1:
            back = jnp.where(lane_of(back.shape) < HEAD, back, grad)
        out_ref[0, :, lanes] = back.astype(BF16)


def unproject(grad, projected, head_gain, cosine, sine, awaited=()):
    blocks, rows, mix = grad.shape
    one = lambda last: pl.BlockSpec((1, rows, last), lambda step: (step, 0, 0))
    flat = pl.BlockSpec((1, mix), lambda step: (0, 0))
    return pl.pallas_call(
        unproject_kernel,
        out_shape=(
            jax.ShapeDtypeStruct((blocks, rows, mix), BF16),
            jax.ShapeDtypeStruct((1, mix), F32),
        ),
        grid=(blocks,),
        in_specs=[one(mix), one(mix), flat, one(cosine.shape[2]), one(cosine.shape[2])]
        + [pl.BlockSpec(memory_space=pl.ANY)] * len(awaited),
        out_specs=(one(mix), flat),
        compiler_params=pltpu.CompilerParams(vmem_limit_bytes=32 * 1024 * 1024),
        cost_estimate=pl.CostEstimate(
            flops=100 * blocks * rows * mix, transcendentals=0, bytes_accessed=12 * blocks * rows * mix
        ),
    )(grad, projected, head_gain, cosine, sine, *awaited)


TAIL = 64


def half_tile(low, tile, keep_low):
    rolled = pltpu.roll(tile, TAIL, 1)
    return jnp.where(low, tile, rolled) if keep_low else jnp.where(low, rolled, tile)


def pack_kernel(info_ref, gate_ref, up_ref, *out_refs):
    low = info_ref[1] == 0
    main = (gate_ref.shape[1] - 2 * TAIL) // 2
    for index, out_ref in enumerate(out_refs):

        @pl.when(pl.program_id(0) == index)
        def _():
            for place in range(2):

                @pl.when(info_ref[1] == place)
                def _():
                    lanes = slice(place * main, (place + 1) * main)
                    out_ref[:, :main] = gate_ref[:, lanes].astype(BF16)
                    out_ref[:, main : 2 * main] = up_ref[:, lanes].astype(BF16)

            gate = half_tile(low, gate_ref[:, 2 * main :], True)
            up = half_tile(low, up_ref[:, 2 * main :], False)
            both = jnp.where(lane_of(gate.shape) < TAIL, gate, up)
            out_ref[:, 2 * main :] = both.astype(BF16)


def pack(info, gate, up, near):
    rows, width = gate.shape
    shard = width // near
    block = pl.BlockSpec((rows, shard), lambda step, info: (0, info[0] ^ step))
    out = pl.BlockSpec((rows, shard), lambda step, info: (0, 0))
    return pl.pallas_call(
        pack_kernel,
        out_shape=(jax.ShapeDtypeStruct((rows, shard), BF16),) * near,
        grid_spec=pltpu.PrefetchScalarGridSpec(
            num_scalar_prefetch=1, grid=(near,), in_specs=[block, block], out_specs=(out,) * near
        ),
        compiler_params=pltpu.CompilerParams(vmem_limit_bytes=32 * 1024 * 1024),
        cost_estimate=pl.CostEstimate(
            flops=0, transcendentals=0, bytes_accessed=10 * rows * width
        ),
    )(info, gate, up)


def spread_kernel(info_ref, *refs):
    pieces = (len(refs) - 2) // 2
    gate_ref, up_ref = refs[2 * pieces :]
    rows, shard = gate_ref.shape
    main = (shard - 2 * TAIL) // 2
    low = info_ref[1] == 0

    def whole(parts):
        parts = [ref[:, 0] for ref in parts]
        return jnp.concatenate(parts, axis=1).reshape(rows, shard).astype(F32)

    mine, other = whole(refs[:pieces]), whole(refs[pieces : 2 * pieces])
    first = jnp.where(low, mine, other)
    second = jnp.where(low, other, mine)
    gate_ref[:, :main] = first[:, :main]
    gate_ref[:, main : 2 * main] = second[:, :main]
    up_ref[:, :main] = first[:, main : 2 * main]
    up_ref[:, main : 2 * main] = second[:, main : 2 * main]
    first, second = first[:, 2 * main :], second[:, 2 * main :]
    lower = lane_of(first.shape) < TAIL
    gate_ref[:, 2 * main :] = jnp.where(lower, first, pltpu.roll(second, TAIL, 1))
    up_ref[:, 2 * main :] = jnp.where(lower, pltpu.roll(first, TAIL, 1), second)


def spread(info, mine, other):
    planes, near, _, width = mine[0].shape
    rows = planes * sum(piece.shape[2] for piece in mine)
    block = lambda piece: pl.BlockSpec(
        (planes, 1, piece.shape[2], width), lambda step, info: (0, step, 0, 0)
    )
    out = pl.BlockSpec((rows, width), lambda step, info: (0, info[0] ^ step))
    shape = jax.ShapeDtypeStruct((rows, near * width), F32)
    return pl.pallas_call(
        spread_kernel,
        out_shape=(shape, shape),
        grid_spec=pltpu.PrefetchScalarGridSpec(
            num_scalar_prefetch=1,
            grid=(near,),
            in_specs=[block(piece) for piece in (*mine, *other)],
            out_specs=(out, out),
        ),
        compiler_params=pltpu.CompilerParams(vmem_limit_bytes=40 * 1024 * 1024),
        cost_estimate=pl.CostEstimate(
            flops=0, transcendentals=0, bytes_accessed=12 * near * rows * width
        ),
    )(info, *mine, *other)


def mix_heads_kernel(query_ref, key_ref, value_ref, out_ref):
    wide = 2 * HEAD
    for head in range(KV_HEADS):
        out_ref[:, 2 * head * wide : (2 * head + 1) * wide] = query_ref[
            :, head * wide : (head + 1) * wide
        ].astype(BF16)
        tile = slice(head // 2 * wide, (head // 2 + 1) * wide)
        key, value = key_ref[:, tile], value_ref[:, tile]
        if head % 2 == 0:
            value = pltpu.roll(value, HEAD, 1)
        else:
            key = pltpu.roll(key, HEAD, 1)
        both = jnp.where(lane_of(key.shape) < HEAD, key, value)
        out_ref[:, (2 * head + 1) * wide : (2 * head + 2) * wide] = both.astype(BF16)


def mix_heads(query, key, value):
    rows = query.shape[0]
    width = query.shape[1] + key.shape[1] + value.shape[1]
    return pl.pallas_call(
        mix_heads_kernel,
        out_shape=jax.ShapeDtypeStruct((rows, width), BF16),
        compiler_params=pltpu.CompilerParams(vmem_limit_bytes=32 * 1024 * 1024),
        cost_estimate=pl.CostEstimate(flops=0, transcendentals=0, bytes_accessed=6 * rows * width),
    )(query, key, value)


def part_heads_kernel(mixed_ref, query_ref, key_ref, value_ref):
    wide = 2 * HEAD
    for pair in range(KV_HEADS // 2):
        tile = slice(pair * wide, (pair + 1) * wide)
        for head in (2 * pair, 2 * pair + 1):
            query_ref[:, head * wide : (head + 1) * wide] = mixed_ref[head, :, :wide].astype(F32)
        first = mixed_ref[2 * pair, :, wide:].astype(F32)
        second = mixed_ref[2 * pair + 1, :, wide:].astype(F32)
        lower = lane_of(first.shape) < HEAD
        key_ref[:, tile] = jnp.where(lower, first, pltpu.roll(second, HEAD, 1))
        value_ref[:, tile] = jnp.where(lower, pltpu.roll(first, HEAD, 1), second)


def part_heads(mixed, rows):
    heads, _, mix = mixed.shape
    block = pl.BlockSpec((heads, rows, mix), lambda step: (0, 0, 0))
    out = lambda count: pl.BlockSpec((rows, count * HEAD), lambda step: (0, 0))
    shape = lambda count: jax.ShapeDtypeStruct((rows, count * HEAD), F32)
    return pl.pallas_call(
        part_heads_kernel,
        out_shape=(shape(GROUP * heads), shape(heads), shape(heads)),
        grid=(1,),
        in_specs=[block],
        out_specs=(out(GROUP * heads), out(heads), out(heads)),
        compiler_params=pltpu.CompilerParams(vmem_limit_bytes=32 * 1024 * 1024),
        cost_estimate=pl.CostEstimate(
            flops=0, transcendentals=0, bytes_accessed=6 * rows * heads * 4 * HEAD
        ),
    )(mixed)


def row_scale(values):
    return lax.rsqrt(jnp.mean(values * values, axis=-1, keepdims=True) + epsilon)


def norm_back(grad, values, gain):
    scale = row_scale(values)
    gain_grad = jnp.sum(grad * values * scale, axis=0, keepdims=True)
    grad = grad * gain
    mean = jnp.mean(grad * values, axis=-1, keepdims=True)
    return scale * grad - values * (scale * scale * scale) * mean, gain_grad


def row_call(kernel, outs, flops, *operands, awaited=()):
    moved = sum(a.size * a.dtype.itemsize for a in operands)
    count = len(operands)

    def body(*refs):
        kernel(*refs[:count], *refs[count + len(awaited) :])

    return pl.pallas_call(
        body,
        grid=(1,),
        in_specs=[whole_spec(a.shape) for a in operands] + awaiting(len(awaited)),
        out_specs=tuple(whole_spec(shape) for shape, _ in outs),
        out_shape=tuple(jax.ShapeDtypeStruct(shape, kind) for shape, kind in outs),
        compiler_params=pltpu.CompilerParams(vmem_limit_bytes=40 * 1024 * 1024),
        cost_estimate=pl.CostEstimate(flops=flops, transcendentals=0, bytes_accessed=moved),
    )(*operands, *awaited)


def join_kernel(heads_ref, weight_ref, input_ref, gain_ref, hidden_ref, mid_ref):
    wide = heads_ref.shape[2]
    total = input_ref[...].astype(F32)
    for head in range(0, heads_ref.shape[0], 2):
        both = jnp.concatenate([heads_ref[head], heads_ref[head + 1]], axis=1)
        total = total + product(both, weight_ref[head * wide : (head + 2) * wide])
    hidden_ref[...] = total
    mid_ref[...] = (total * row_scale(total) * gain_ref[...]).astype(BF16)


def middle_kernel(
    low_own, low_got, high_own, high_got, hidden_ref, outer_ref, gain_ref, weight_ref,
    grad_ref, low_ref, heads_ref, part_ref,
):
    grad_mid = jnp.concatenate(
        [
            low_own[...] + low_got[...].astype(F32),
            high_own[...] + high_got[...].astype(F32),
        ],
        axis=0,
    )
    through, gain_grad = norm_back(grad_mid, hidden_ref[...], gain_ref[...])
    part_ref[...] = gain_grad
    grad = outer_ref[...].astype(F32) + through
    grad_ref[...] = grad
    low = grad.astype(BF16)
    low_ref[...] = low
    wide = heads_ref.shape[2]
    for head in range(0, heads_ref.shape[0], 2):
        both = by_transpose(low, weight_ref[head * wide : (head + 2) * wide]).astype(BF16)
        heads_ref[head] = both[:, :wide]
        heads_ref[head + 1] = both[:, wide:]


def output_weight_kernel(heads_ref, grad_ref, out_ref):
    wide = heads_ref.shape[2]
    for head in range(heads_ref.shape[0]):
        out_ref[head * wide : (head + 1) * wide] = transpose_by(
            heads_ref[head], grad_ref[...]
        ).astype(BF16)


def input_kernel(heads_ref, weight_ref, input_ref, hidden_ref, gain_ref, grad_ref, part_ref):
    mix = heads_ref.shape[2]
    total = jnp.zeros(grad_ref.shape, F32)
    for head in range(heads_ref.shape[0]):
        total = total + by_transpose(
            heads_ref[head], weight_ref[:, head * mix : (head + 1) * mix]
        )
    through, gain_grad = norm_back(total, input_ref[...].astype(F32), gain_ref[...])
    part_ref[...] = gain_grad
    grad_ref[...] = hidden_ref[...] + through


def feed_kernel(info_ref, *refs):
    mids, outers, weights = refs[:10], refs[10], refs[11:15]
    down_ref = refs[15]
    mid_ref, outer_ref, inner_ref, grads_ref, send_ref, keep_ref = refs[-12:-6]
    mid_all, outer_all, weight_all, mid_sem, outer_sem, weight_sem = refs[-6:]
    step = pl.program_id(0)
    main = inner_ref.shape[1] - TAIL

    def weight_copy(block):
        return pltpu.make_async_copy(
            weights[block], weight_all.at[info_ref[0] ^ block], weight_sem.at[block]
        )

    @pl.when(step == 0)
    def _():
        for block in range(len(weights)):
            weight_copy(block).start()
        for block in range(PLANE):
            change = 2 * block + 1 if block < 4 else 2 * block - 8
            pltpu.make_async_copy(
                outers.at[change ^ info_ref[2]], outer_all.at[block], outer_sem.at[block]
            ).start()
            first = 5 * (block // 4) + block % 4
            if block % 4 < 3:
                pltpu.make_async_copy(mids[first], mid_all.at[block], mid_sem.at[block]).start()
            else:
                half = mids[first].shape[0]
                for part in range(2):
                    target = mid_all.at[block].at[pl.ds(part * half, half)]
                    pltpu.make_async_copy(mids[first + part], target, mid_sem.at[block]).start()
        for block in range(len(weights)):
            weight_copy(block).wait()

    for which in range(2):
        block = 2 * step + which
        pltpu.make_async_copy(mids[0], mid_all.at[block], mid_sem.at[block]).wait()
        pltpu.make_async_copy(outers.at[0], outer_all.at[block], outer_sem.at[block]).wait()
    fsdp, depth, width = weight_all.shape
    weight = weight_all[...].reshape(fsdp * depth, width)
    rows = mid_all.shape[1]

    def unit(gate, up, back):
        share = jax.nn.sigmoid(gate)
        silu = gate * share
        inner = (silu * up).astype(BF16)
        grad_gate = (back * up * (share + silu * (1.0 - share))).astype(BF16)
        return inner, grad_gate, (back * silu).astype(BF16)

    tail = slice(2 * main, 2 * main + TAIL)
    last = slice(2 * main + TAIL, 2 * main + 2 * TAIL)
    parts = []
    for which in range(2):
        mine = slice(which * rows, (which + 1) * rows)
        mid, outer = mid_all[2 * step + which], outer_all[2 * step + which]
        mid_ref[mine] = mid
        outer_ref[mine] = outer
        both = product(mid, weight)
        back = by_transpose(outer, down_ref[...])
        inner, gate, up = unit(both[:, :main], both[:, main : 2 * main], back[:, :main])
        inner_ref[mine, :main] = inner
        inner, gate_tail, up_tail = unit(both[:, tail], both[:, last], back[:, main:])
        inner_ref[mine, main:] = inner
        grads = jnp.concatenate([gate, up, gate_tail, up_tail], axis=1)
        grads_ref[mine] = grads
        parts.append(by_transpose(grads, weight).astype(BF16))

    @pl.when(step < 2)
    def _():
        send_ref[:rows] = parts[0]
        send_ref[rows:] = parts[1]

    @pl.when(step >= 2)
    def _():
        keep_ref[:rows] = parts[0]
        keep_ref[rows:] = parts[1]


def feed(info, mids, outers, weights, down, awaited=()):
    rows, width = mids[0].shape
    depth, units2 = weights[0].shape
    units = units2 // 2
    count = PLANE
    anywhere = pl.BlockSpec(memory_space=pl.ANY)
    flat = lambda last: pl.BlockSpec((2 * rows, last), lambda step, info: (step, 0))
    send = pl.BlockSpec((2 * rows, width), lambda step, info: (jnp.minimum(step, 1), 0))
    keep = pl.BlockSpec((2 * rows, width), lambda step, info: (jnp.maximum(step - 2, 0), 0))
    shape = lambda tall, last: jax.ShapeDtypeStruct((tall * rows, last), BF16)
    return pl.pallas_call(
        feed_kernel,
        out_shape=(
            shape(count, width),
            shape(count, width),
            shape(count, units),
            shape(count, units2),
            shape(count // 2, width),
            shape(count // 2, width),
        ),
        grid_spec=pltpu.PrefetchScalarGridSpec(
            num_scalar_prefetch=1,
            grid=(count // 2,),
            in_specs=[anywhere] * (len(mids) + 1 + len(weights))
            + [pl.BlockSpec(down.shape, lambda step, info: (0, 0))]
            + [anywhere] * len(awaited),
            out_specs=(flat(width), flat(width), flat(units), flat(units2), send, keep),
            scratch_shapes=[
                pltpu.VMEM((count, rows, width), BF16),
                pltpu.VMEM((count, rows, width), BF16),
                pltpu.VMEM((len(weights), depth, units2), BF16),
                pltpu.SemaphoreType.DMA((count,)),
                pltpu.SemaphoreType.DMA((count,)),
                pltpu.SemaphoreType.DMA((len(weights),)),
            ],
        ),
        compiler_params=pltpu.CompilerParams(vmem_limit_bytes=56 * 1024 * 1024),
        cost_estimate=pl.CostEstimate(
            flops=10 * count * rows * width * units,
            transcendentals=count * rows * units,
            bytes_accessed=12 * count * rows * width,
        ),
    )(info, *mids, outers, *weights, down, *awaited)


def hidden_weight_kernel(mid_ref, grads_ref, out_ref):
    planes, _, rows, width = out_ref.shape
    total = transpose_by(mid_ref[...], grads_ref[...])
    out_ref[:, 0] = total.reshape(planes, rows, width).astype(BF16)


def hidden_weight(mid, grads, near, planes):
    count, width = mid.shape
    units2 = grads.shape[1]
    rows = width // near // planes
    return pl.pallas_call(
        hidden_weight_kernel,
        out_shape=jax.ShapeDtypeStruct((planes, near, rows, units2), BF16),
        grid=(near,),
        in_specs=[
            pl.BlockSpec((count, width // near), lambda step: (0, step)),
            pl.BlockSpec((count, units2), lambda step: (0, 0)),
        ],
        out_specs=pl.BlockSpec((planes, 1, rows, units2), lambda step: (0, step, 0, 0)),
        compiler_params=pltpu.CompilerParams(vmem_limit_bytes=48 * 1024 * 1024),
        cost_estimate=pl.CostEstimate(
            flops=2 * count * width * units2,
            transcendentals=0,
            bytes_accessed=2 * count * (width + units2) + 2 * width * units2,
        ),
    )(mid, grads)


def awaiting(count):
    return [pl.BlockSpec(memory_space=pl.ANY)] * count


def whole_spec(shape):
    return pl.BlockSpec(shape, lambda *_: (0,) * len(shape))


def split_rows(blocks, cut, awaited):
    rows, width = blocks[0].shape
    count = len(blocks)

    def kernel(*refs):
        for index in range(count):
            refs[-2][index] = refs[index][:cut]
            refs[-1][index] = refs[index][cut:]

    return pl.pallas_call(
        kernel,
        out_shape=(
            jax.ShapeDtypeStruct((count, cut, width), BF16),
            jax.ShapeDtypeStruct((count, rows - cut, width), BF16),
        ),
        grid=(1,),
        in_specs=[whole_spec((rows, width))] * count + awaiting(len(awaited)),
        out_specs=(whole_spec((count, cut, width)), whole_spec((count, rows - cut, width))),
        cost_estimate=pl.CostEstimate(
            flops=0, transcendentals=0, bytes_accessed=4 * count * rows * width
        ),
    )(*blocks, *awaited)


def head_message(first, second, rest, awaited):
    def kernel(first_ref, second_ref, rest_ref, *refs):
        rows = first_ref.shape[0]
        refs[-1][:rows] = (first_ref[...].astype(F32) + second_ref[...].astype(F32)).astype(BF16)
        refs[-1][rows:] = rest_ref[...].astype(BF16)

    rows, width = first.shape
    shape = (rows + rest.shape[0], width)
    return pl.pallas_call(
        kernel,
        out_shape=jax.ShapeDtypeStruct(shape, BF16),
        grid=(1,),
        in_specs=[whole_spec(a.shape) for a in (first, second, rest)] + awaiting(len(awaited)),
        out_specs=whole_spec(shape),
        cost_estimate=pl.CostEstimate(
            flops=0, transcendentals=0, bytes_accessed=6 * rows * width
        ),
    )(first, second, rest, *awaited)


def per_device(
    inputs,
    lengths,
    positions,
    cotangent,
    w_query,
    w_key,
    w_value,
    w_output,
    w_gate,
    w_up,
    w_down,
    attn_gain,
    ffn_gain,
    query_gain,
    key_gain,
):
    groups, slot_count, model_width = inputs.shape
    row_count = groups * slot_count
    own_rows = w_query.shape[0]
    ctx_size = lax.axis_size("ctx")
    fsdp_size = lax.axis_size("fsdp")
    me_f = lax.axis_index("fsdp")
    me_c = lax.axis_index("ctx")
    inner = KV_HEADS
    outer = ctx_size // inner
    inner_groups = [[o * inner + i for i in range(inner)] for o in range(outer)]
    outer_groups = [[o * inner + i for o in range(outer)] for i in range(inner)]
    planes = ctx_size // 2
    plane_groups_z = [[2 * i + low for i in range(planes)] for low in range(2)]
    low_bit = me_c % 2
    my_head = me_c % inner
    mix = 4 * HEAD
    wide = GROUP * HEAD
    ff_shard = w_down.shape[0]
    ff_own = ff_shard // 2
    ff_main = ff_own - TAIL

    slots = me_c * slot_count + jnp.arange(slot_count)
    valid = (slots[None, :] < lengths[:, None]).astype(F32).reshape(row_count, 1)
    info = jnp.concatenate([(me_c // inner * inner)[None].astype(jnp.int32), lengths])
    device_info = jnp.stack([me_f, low_bit]).astype(jnp.int32)
    plane_info = jnp.stack([me_f, low_bit, low_bit * fsdp_size + me_f]).astype(jnp.int32)

    small = query_gain.shape[0]
    gains = jnp.concatenate([attn_gain, ffn_gain, query_gain, key_gain]).astype(BF16)[None]
    gains = jnp.concatenate(gather_near(gains), axis=0).astype(F32)
    gains = jnp.stack([pick(gains, me_f ^ k) for k in range(fsdp_size)])
    attn_scale = gains[:, :own_rows].reshape(1, model_width)
    ffn_scale = gains[:, own_rows : 2 * own_rows].reshape(1, model_width)
    qgain_scale = gains[:, 2 * own_rows : 2 * own_rows + small].reshape(-1)
    kgain_scale = gains[:, 2 * own_rows + small :].reshape(-1)
    head_gain = jnp.concatenate(
        [qgain_scale] * GROUP + [kgain_scale, jnp.ones((HEAD,), F32)]
    ).reshape(1, mix)

    line = Line()
    rows_shape = (row_count, model_width)

    line = Line()
    rows_shape = (row_count, model_width)
    rows_flops = 2 * row_count * model_width * model_width

    flat_low = inputs.reshape(row_count, model_width)
    place_row = positions.reshape(1, row_count)
    digits = jnp.concatenate([place_row // POSITION_BASE, place_row % POSITION_BASE], axis=0)
    digits = jnp.pad(
        digits.astype(BF16), ((0, POSITION_ROWS - 2), (0, model_width - row_count))
    )
    near = line(lambda a, b: jnp.concatenate([a, b], axis=0), flat_low, digits)
    far, following = trade(near, 4), ring_step(near)
    places = ring_places(my_head // 2)
    frequency = rope_base ** (-jnp.arange(0, HEAD, 2).astype(F32) / HEAD)
    frequency = jnp.concatenate([frequency] * (2 * GROUP)).reshape(1, wide)

    qkv_own = line(mix_heads, w_query, w_key, w_value)
    head_weight = lax.dynamic_slice_in_dim(qkv_own, my_head * mix, mix, 1)
    head_weight = jnp.stack(gather_near(head_weight))
    output_own = line(lambda a: a.astype(BF16), w_output)
    output_weight = lax.all_gather(output_own, "fsdp", axis=0, tiled=True)
    gu_own = line(lambda a, b: pack(device_info, a, b, fsdp_size), w_gate, w_up)
    gu_parts = [gu_own[0]] + [trade(gu_own[k], k) for k in range(1, fsdp_size)]

    earlier = ()
    for step in range(4):
        if step < 3:
            far, following = line.wait(far, following)
            next_far = trade(following, 4)
            after_next = ring_step(following) if step < 2 else None
        else:
            gu_parts = line.wait(*gu_parts)
        project_info = jnp.stack([me_f, low_bit, places[step]]).astype(jnp.int32)
        earlier = line(
            lambda a, b, c, *rest: project(
                project_info, a, b, c, attn_scale, head_gain, frequency, inner, rest or None
            ),
            near,
            far,
            head_weight,
            *earlier,
        )
        near, far, following = following, next_far, after_next
    normed_all, projected, mixed, cosine, sine = earlier
    mixed = mixed.reshape(inner, groups, slot_count, mix)

    qkv_weight = lax.all_gather(qkv_own, "fsdp", axis=0, tiled=True)
    if outer == 1:
        attended = line(lambda a: attention(info, a, a, None, (qkv_weight,)), mixed)
    else:
        shared = lax.all_gather(
            mixed[..., 2 * HEAD :], "ctx", axis=0, axis_index_groups=outer_groups, tiled=True
        )
        attended = line(lambda a, b: attention(info, a, b), mixed, shared)

    def exchange(values):
        return lax.all_to_all(values, "ctx", 0, 0, axis_index_groups=inner_groups, tiled=True)

    attended = exchange(attended.reshape(inner, row_count, wide))
    outer_low = line(
        lambda a: (a.reshape(rows_shape).astype(F32) * valid).astype(BF16), cotangent
    )
    outer_all = lax.all_gather(
        outer_low, ("ctx", "fsdp"), axis=0, axis_index_groups=plane_groups(), tiled=False
    )
    down_weight = line(
        lambda a: jnp.concatenate(
            [
                lax.dynamic_slice_in_dim(a, low_bit * ff_main, ff_main, 0),
                lax.dynamic_slice_in_dim(a, 2 * ff_main + low_bit * TAIL, TAIL, 0),
            ],
            axis=0,
        ).astype(BF16),
        w_down,
    )
    hidden_res, mid_low = line(
        lambda *a: row_call(
            join_kernel, ((rows_shape, F32), (rows_shape, BF16)), rows_flops, *a
        ),
        attended,
        output_weight,
        flat_low,
        ffn_scale,
    )
    mid_x, mid_y = trade(mid_low, 2), trade(mid_low, 4)
    mid_cut = line(cut_far, mid_x, mid_y)
    mid_corner = trade(mid_cut[0], 4), trade(mid_cut[1], 2)
    mid_all = gather_plane(mid_low, mid_x, mid_y, mid_corner)

    mid_all, outer_all, inner_low, grad_gu, send, keep = line(
        lambda *a: feed(plane_info, a[:10], a[10], a[11:15], a[15]),
        *mid_all,
        outer_all,
        *gu_parts,
        down_weight,
    )
    got = trade(send, 1)
    gu_part = line(lambda a, b: hidden_weight(a, b, fsdp_size, planes), mid_all, grad_gu)
    gu_sum = lax.psum_scatter(
        gu_part.reshape(-1, 2 * ff_own),
        "ctx",
        scatter_dimension=0,
        axis_index_groups=plane_groups_z,
        tiled=True,
    )
    low_send, high_send, low, high = line(cut_plane, got, keep)
    low_got, high_got = trade(low_send, 2), trade(high_send, 4)
    down_part = line(lambda a, b: transpose_by(a, b).astype(BF16), inner_low, outer_all)
    down_sum = lax.psum(down_part, "ctx", axis_index_groups=plane_groups_z)
    result_part = line(lambda a, b: product(a, b).astype(BF16), inner_low, down_weight)
    low_far, high_far, low_own, high_own = line(join_plane, low, high, low_got, high_got)
    low_got, high_got = trade(low_far, 4), trade(high_far, 2)
    (qkv_weight,) = line.wait(qkv_weight)
    grad_hidden, grad_attn_low, grad_heads, ffn_part = line(
        lambda *a: row_call(
            middle_kernel,
            (
                (rows_shape, F32),
                (rows_shape, BF16),
                ((inner, row_count, wide), BF16),
                ((1, model_width), F32),
            ),
            rows_flops,
            *a,
        ),
        low_own,
        low_got,
        high_own,
        high_got,
        hidden_res,
        outer_low,
        ffn_scale,
        output_weight,
    )

    grad_heads = exchange(grad_heads).reshape(inner, groups, slot_count, wide)
    (output_part,) = line(
        lambda *a: row_call(
            output_weight_kernel, (((model_width, model_width), BF16),), rows_flops, *a
        ),
        attended,
        grad_attn_low,
    )
    gu_own = line(
        lambda a: tuple(
            pick(a.reshape(fsdp_size, own_rows // planes, 2 * ff_own), me_f ^ k)
            for k in range(fsdp_size)
        ),
        gu_sum,
    )
    gu_blocks = [gu_own[0]] + [trade(gu_own[k], k) for k in range(1, fsdp_size)]
    if outer == 1:
        grad_mixed = line(
            lambda a, b: attention(info, a, a, b, gu_own[1:]), mixed, grad_heads
        )
    else:
        grad_q, grad_kv = line(
            lambda a, b, c: attention(info, a, b, c), mixed, shared, grad_heads
        )
        grad_kv = lax.psum_scatter(
            grad_kv, "ctx", scatter_dimension=0, axis_index_groups=outer_groups, tiled=True
        )
        grad_mixed = jnp.concatenate([grad_q, grad_kv], axis=-1)
    grad_head, head_part = line(
        lambda *a: unproject(*a, gu_blocks[1:]),
        grad_mixed.reshape(inner, row_count, mix),
        projected,
        head_gain,
        cosine,
        sine,
    )
    grad_qkv = exchange(grad_head)
    head_rows = line(
        lambda a, b: transpose_by(
            a.reshape(inner * row_count, model_width), b.reshape(-1, mix)
        ).astype(BF16),
        normed_all,
        grad_head,
    )
    head_send, head_keep = line(
        lambda a: cut_near(a.reshape(fsdp_size, own_rows, mix), me_f), head_rows
    )
    head_got = trade(head_send, 1)
    cut = own_rows // planes // 2
    first_half, second_half = split_rows(gu_blocks, cut, (down_sum,))
    gu_mine = [
        lax.all_gather(piece, "ctx", axis=0, axis_index_groups=plane_groups_z, tiled=False)
        for piece in (first_half, second_half)
    ]
    gu_other = [trade(piece, fsdp_size) for piece in gu_mine]

    head_pair = line(add_low, head_keep, head_got)
    head_far = trade(head_pair[1], 2)
    output_send, output_keep = line(
        lambda a: cut_near(a.reshape(fsdp_size, own_rows, model_width), me_f), output_part
    )
    output_got = trade(output_send, 1)
    output_pair = line(add_low, output_keep, output_got)
    output_far = trade(output_pair[1], 2)
    down_other = trade(down_sum, fsdp_size)
    input_grad, attn_part = line(
        lambda *a: row_call(
            input_kernel,
            ((rows_shape, F32), ((1, model_width), F32)),
            rows_flops * KV_HEADS * mix // model_width,
            *a,
            awaited=(gu_mine[0],),
        ),
        grad_qkv,
        qkv_weight,
        flat_low,
        grad_hidden,
        attn_scale,
    )
    input_grad = input_grad.reshape(groups, slot_count, model_width)
    qgain_part = sum(head_part[0, i * HEAD : (i + 1) * HEAD] for i in range(GROUP))
    kgain_part = head_part[0, GROUP * HEAD : (GROUP + 1) * HEAD]
    gain_parts = jnp.concatenate(
        [
            attn_part.reshape(fsdp_size, own_rows),
            ffn_part.reshape(fsdp_size, own_rows),
            qgain_part.reshape(fsdp_size, small),
            kgain_part.reshape(fsdp_size, small),
        ],
        axis=-1,
    )
    output_own = line(add_low, output_pair[0], output_far)
    output_grad = (
        ctx_sum(output_own.reshape(ctx_size, own_rows // ctx_size, model_width))
        .reshape(own_rows, model_width)
        .astype(F32)
    )
    result_send, result_keep = halves(result_part)
    got = trade(result_send, 1)
    gain_count = gain_parts.size
    gain_near = gain_parts + trade(gain_parts, 1)
    gain_near = gain_near + trade(gain_near, 2)
    gain_rows = -(-gain_count // (16 * mix)) * 16
    gain_near = jnp.pad(gain_near.reshape(-1), (0, gain_rows * mix - gain_count))
    gain_near = gain_near.reshape(gain_rows, mix)
    head_first, head_second = head_pair[0], head_far
    if outer > 1:
        gain_near = lax.psum(gain_near, "ctx", axis_index_groups=outer_groups)
        head_first = lax.psum(
            add_low(head_first, head_second).astype(F32), "ctx", axis_index_groups=outer_groups
        ).astype(BF16)
        head_second = jnp.zeros_like(head_first)
    head_own = head_message(head_first, head_second, gain_near, (gu_other[0],))
    head_blocks = lax.all_gather(
        head_own, "ctx", axis=0, axis_index_groups=inner_groups, tiled=False
    )
    gain_sum = jnp.sum(head_blocks[:, own_rows:].astype(F32), axis=0)
    gain_sum = pick(gain_sum.reshape(-1)[:gain_count].reshape(gain_parts.shape), me_f)
    low_send, high_send, result_low, result_high = line(cut_plane, got, result_keep)
    result_low_got, result_high_got = trade(low_send, 2), trade(high_send, 4)
    low_far, high_far, low_own, high_own = line(
        join_plane, result_low, result_high, result_low_got, result_high_got
    )
    low_got, high_got = trade(low_far, 4), trade(high_far, 2)
    result = line(
        lambda a, b, c, d, e: (
            valid * (e + jnp.concatenate([a + b.astype(F32), c + d.astype(F32)], axis=0))
        ).astype(BF16),
        low_own,
        low_got,
        high_own,
        high_got,
        hidden_res,
    )
    block_output = result.reshape(groups, slot_count, model_width)

    query_grad, key_grad, value_grad = part_heads(head_blocks, own_rows)
    first = jnp.where(low_bit == 0, down_sum, down_other)
    second = jnp.where(low_bit == 0, down_other, down_sum)
    down_grad = jnp.concatenate(
        [first[:ff_main], second[:ff_main], first[ff_main:], second[ff_main:]], axis=0
    ).astype(F32)
    gate_grad, up_grad = spread(device_info, gu_mine, gu_other)

    return (
        block_output,
        input_grad,
        query_grad,
        key_grad,
        value_grad,
        output_grad,
        gate_grad,
        up_grad,
        down_grad,
        gain_sum[:own_rows],
        gain_sum[own_rows : 2 * own_rows],
        gain_sum[2 * own_rows : 2 * own_rows + small],
        gain_sum[2 * own_rows + small :],
    )


def solution(mesh):
    return jax.shard_map(
        per_device,
        mesh=mesh,
        in_specs=(
            P("fsdp", "ctx", None),
            P("fsdp"),
            P("fsdp", "ctx"),
            P("fsdp", "ctx", None),
            P("fsdp", None),
            P("fsdp", None),
            P("fsdp", None),
            P("fsdp", None),
            P("fsdp", None),
            P("fsdp", None),
            P("fsdp", None),
            P("fsdp"),
            P("fsdp"),
            P("fsdp"),
            P("fsdp"),
        ),
        out_specs=(
            P("fsdp", "ctx", None),
            P("fsdp", "ctx", None),
            P("fsdp", None),
            P("fsdp", None),
            P("fsdp", None),
            P("fsdp", None),
            P("fsdp", None),
            P("fsdp", None),
            P("fsdp", None),
            P("fsdp"),
            P("fsdp"),
            P("fsdp"),
            P("fsdp"),
        ),
        check_vma=False,
    )
```

```python
import jax
import jax.numpy as jnp
from jax import lax
from jax.experimental import pallas as pl
from jax.experimental.pallas import tpu as pltpu
from jax.sharding import PartitionSpec as P

HEADS = 16
KV_HEADS = 8
HEAD = 64
GROUP = HEADS // KV_HEADS


epsilon = 1e-05
rope_base = 1000000.0
masked = -1e30
F32 = jnp.float32
BF16 = jnp.bfloat16


def dot_over(left, right, left_dim, right_dim):
    return lax.dot_general(
        left, right, (((left_dim,), (right_dim,)), ((), ())), preferred_element_type=F32
    )


def product(left, right):
    return dot_over(left, right, 1, 0)


def by_transpose(left, right):
    return dot_over(left, right, 1, 1)


def transpose_by(left, right):
    return dot_over(left, right, 0, 0)


PLANE = 8


def trade(values, step):
    size = lax.axis_size("ctx") * lax.axis_size("fsdp")
    return lax.ppermute(values, ("ctx", "fsdp"), [(i, i ^ step) for i in range(size)])


def pick(values, index, axis=0):
    return lax.dynamic_index_in_dim(values, index, axis, keepdims=False)


class Line:
    def __init__(self):
        self.last = None

    def __call__(self, step, *operands):
        if self.last is not None:
            operands = lax.optimization_barrier((*operands, self.last))[:-1]
        result = step(*operands)
        self.last = jax.tree.leaves(result)[0]
        return result

    def wait(self, *values):
        *values, self.last = lax.optimization_barrier((*values, self.last))
        return values


def add_low(first, second):
    return (first.astype(F32) + second.astype(F32)).astype(BF16)


def halves(values):
    half = values.shape[0] // 2
    return values[:half], values[half:]


def cut_far(over_x, over_y):
    return halves(over_x)[0], halves(over_y)[1]


def gather_plane(values, over_x, over_y, corner):
    far = [values, over_x, over_y, *corner]
    return [trade(block, 1) for block in far] + far


def plane_groups():
    size = lax.axis_size("ctx") * lax.axis_size("fsdp")
    return [list(range(start, start + PLANE)) for start in range(0, size, PLANE)]


def cut_plane(send_got, keep):
    pair = add_low(keep, send_got).reshape(4, -1, keep.shape[1])
    half = pair.shape[1] // 2
    low, high = pair[:, :half], pair[:, half:]
    return jnp.stack([low[1], low[3]]), jnp.stack([high[2], high[3]]), low[::2], high[:2]


def join_plane(low, high, low_got, high_got):
    low_own = low[0].astype(F32) + low_got[0].astype(F32)
    high_own = high[0].astype(F32) + high_got[0].astype(F32)
    return add_low(low[1], low_got[1]), add_low(high[1], high_got[1]), low_own, high_own


def cut_near(part, me_f):
    blocks = [pick(part, me_f ^ k) for k in range(4)]
    return jnp.stack([blocks[1], blocks[3]]), jnp.stack([blocks[0], blocks[2]])


def gather_near(values):
    far = trade(values, 2)
    near = trade(values, 1)
    return [values, near, far, trade(far, 1)]


def sum_everywhere(values):
    step = 1
    while step < lax.axis_size("ctx") * lax.axis_size("fsdp"):
        values = values + trade(values, step)
        step *= 2
    return values


RING = (0, 1, 3, 2)


def ring_step(values):
    following = {RING[i]: RING[(i + 1) % 4] for i in range(4)}
    pairs = []
    for c in range(lax.axis_size("ctx")):
        outer, place, low = c // 8, c // 2 % 4, c % 2
        pairs.append((c, outer * 8 + following[place] * 2 + low))
    return lax.ppermute(values, "ctx", pairs)


def ring_places(place):
    before = {RING[(i + 1) % 4]: RING[i] for i in range(4)}
    table = []
    for start in range(4):
        row = [start]
        for _ in range(3):
            row.append(before[row[-1]])
        table.append(row)
    return jnp.array(table, jnp.int32)[place]


def plane_step(values, moves):
    size = lax.axis_size("ctx") * lax.axis_size("fsdp")
    pairs = []
    for device in range(size):
        place, rest = device // PLANE, device % PLANE
        pairs += [(device, to * PLANE + rest) for start, to in moves if start == place]
    return lax.ppermute(values, ("ctx", "fsdp"), pairs)


def ctx_bits():
    size = lax.axis_size("ctx")
    bits = []
    step = 1
    while step < size:
        bits.append(step)
        step *= 2
    return bits


def ctx_sum(values):
    me = lax.axis_index("ctx")
    near = lax.axis_size("fsdp")
    for step in ctx_bits():
        shape = values.shape
        halves = values.reshape((2, shape[0] // 2) + shape[1:])
        mine = (me // step) % 2
        got = trade(pick(halves, 1 - mine), step * near)
        values = (pick(halves, mine).astype(F32) + got.astype(F32)).astype(BF16)
    for step in reversed(ctx_bits()):
        mine = (me // step) % 2
        got = trade(values, step * near)
        first = jnp.where(mine == 0, values, got)
        second = jnp.where(mine == 0, got, values)
        values = jnp.concatenate([first, second], axis=0)
    return values


def two_heads(block):
    return jnp.concatenate([block[:, :HEAD], block[:, HEAD:]], axis=0)


def side_by_side(stacked):
    rows = stacked.shape[0] // 2
    return jnp.concatenate([stacked[:rows], stacked[rows:]], axis=1)


def allowed_mask(rows, count, first_query, first_key, seq_len):
    query_slot = first_query + lax.broadcasted_iota(jnp.int32, (rows, count), 0) % (rows // GROUP)
    key_slot = first_key + lax.broadcasted_iota(jnp.int32, (rows, count), 1)
    return (key_slot <= query_slot) & (key_slot < seq_len)


def whole_row(q_ref, kv_ref, index, seq_len):
    slots = q_ref.shape[2]
    count = (index + 1) * slots
    query = two_heads(q_ref[index, 0]) * (HEAD**-0.5)
    both = kv_ref[: index + 1, 0].reshape(count, 2 * HEAD)
    key, value = both[:, :HEAD], both[:, HEAD:]
    scores = by_transpose(query, key)
    scores = jnp.where(
        allowed_mask(GROUP * slots, count, index * slots, 0, seq_len), scores, masked
    )
    exponent = jnp.exp(scores - jnp.max(scores, axis=-1, keepdims=True))
    weights = exponent * (1.0 / jnp.sum(exponent, axis=-1, keepdims=True))
    return query, key, value, weights


def forward_small(info_ref, q_ref, kv_ref, *refs):
    out_ref = refs[-1]
    seq_len = info_ref[pl.program_id(0) + 1]
    slots = q_ref.shape[2]
    for index in range(q_ref.shape[0]):

        @pl.when(index * slots < seq_len)
        def _():
            _, _, value, weights = whole_row(q_ref, kv_ref, index, seq_len)
            out_ref[index, 0] = side_by_side(product(weights.astype(BF16), value)).astype(BF16)

        @pl.when(index * slots >= seq_len)
        def _():
            out_ref[index, 0] = jnp.zeros(out_ref.shape[2:], BF16)


def backward_small(info_ref, q_ref, kv_ref, grad_ref, *refs):
    out_ref, key_acc, value_acc = refs[-3:]
    seq_len = info_ref[pl.program_id(0) + 1]
    blocks, _, slots, _ = q_ref.shape
    key_acc[...] = jnp.zeros_like(key_acc)
    value_acc[...] = jnp.zeros_like(value_acc)
    for index in range(blocks):

        @pl.when(index * slots < seq_len)
        def _():
            count = (index + 1) * slots
            query, key, value, weights = whole_row(q_ref, kv_ref, index, seq_len)
            grad = two_heads(grad_ref[index, 0])
            grad_weights = by_transpose(grad, value)
            delta = jnp.sum(weights * grad_weights, axis=-1, keepdims=True)
            grad_scores = (weights * (grad_weights - delta)).astype(BF16)
            out_ref[index, 0, :, : 2 * HEAD] = side_by_side(
                product(grad_scores, key) * (HEAD**-0.5)
            )
            key_acc[:count] += transpose_by(grad_scores, query)
            value_acc[:count] += transpose_by(weights.astype(BF16), grad)

        @pl.when(index * slots >= seq_len)
        def _():
            out_ref[index, 0, :, : 2 * HEAD] = jnp.zeros((slots, 2 * HEAD), F32)

    for index in range(blocks):
        rows = slice(index * slots, (index + 1) * slots)
        out_ref[index, 0, :, 2 * HEAD :] = jnp.concatenate(
            [key_acc[rows], value_acc[rows]], axis=1
        )


def row_stats(query, kv_ref, index, first_query, seq_len):
    slots = kv_ref.shape[2]
    rows = query.shape[0]

    def scores_of(block):
        both = kv_ref[block, 0]
        scores = by_transpose(query, both[:, :HEAD])
        allowed = allowed_mask(rows, slots, first_query, block * slots, seq_len)
        return both, jnp.where(allowed, scores, masked)

    def step(block, state):
        top, total = state
        _, scores = scores_of(block)
        new_top = jnp.maximum(top, jnp.max(scores, axis=-1, keepdims=True))
        grown = jnp.sum(jnp.exp(scores - new_top), axis=-1, keepdims=True)
        return new_top, total * jnp.exp(top - new_top) + grown

    start = (jnp.full((rows, 1), masked, F32), jnp.zeros((rows, 1), F32))
    top, total = lax.fori_loop(0, index + 1, step, start)
    inverse = 1.0 / total

    def weights_of(block):
        both, scores = scores_of(block)
        return both, jnp.exp(scores - top) * inverse

    return weights_of


def forward_large(info_ref, q_ref, kv_ref, out_ref):
    seq_len = info_ref[pl.program_id(0) + 1]
    slots = q_ref.shape[2]
    index = info_ref[0] + pl.program_id(1)
    live = index * slots < seq_len

    @pl.when(live)
    def _():
        query = two_heads(q_ref[0, 0]) * (HEAD**-0.5)
        weights_of = row_stats(query, kv_ref, index, index * slots, seq_len)

        def step(block, total):
            both, weights = weights_of(block)
            return total + product(weights.astype(BF16), both[:, HEAD:])

        total = lax.fori_loop(0, index + 1, step, jnp.zeros((GROUP * slots, HEAD), F32))
        out_ref[0, 0] = side_by_side(total).astype(BF16)

    @pl.when(jnp.logical_not(live))
    def _():
        out_ref[0, 0] = jnp.zeros(out_ref.shape[2:], BF16)


def backward_large(info_ref, q_ref, kv_ref, grad_ref, out_ref, kv_out_ref):
    seq_len = info_ref[pl.program_id(0) + 1]
    slots = q_ref.shape[2]
    index = info_ref[0] + pl.program_id(1)
    live = index * slots < seq_len

    @pl.when(pl.program_id(1) == 0)
    def _():
        kv_out_ref[...] = jnp.zeros_like(kv_out_ref)

    @pl.when(live)
    def _():
        query = two_heads(q_ref[0, 0]) * (HEAD**-0.5)
        grad = two_heads(grad_ref[0, 0])
        weights_of = row_stats(query, kv_ref, index, index * slots, seq_len)

        def delta_step(block, total):
            both, weights = weights_of(block)
            grad_weights = by_transpose(grad, both[:, HEAD:])
            return total + jnp.sum(weights * grad_weights, axis=-1, keepdims=True)

        delta = lax.fori_loop(0, index + 1, delta_step, jnp.zeros((GROUP * slots, 1), F32))

        def step(block, total):
            both, weights = weights_of(block)
            grad_weights = by_transpose(grad, both[:, HEAD:])
            grad_scores = (weights * (grad_weights - delta)).astype(BF16)
            kv_out_ref[block, 0] += jnp.concatenate(
                [transpose_by(grad_scores, query), transpose_by(weights.astype(BF16), grad)], axis=1
            )
            return total + product(grad_scores, both[:, :HEAD])

        total = lax.fori_loop(0, index + 1, step, jnp.zeros((GROUP * slots, HEAD), F32))
        out_ref[0, 0] = side_by_side(total * (HEAD**-0.5))

    @pl.when(jnp.logical_not(live))
    def _():
        out_ref[0, 0] = jnp.zeros(out_ref.shape[2:], F32)


def attention_cost(q_blocks, k_blocks, seqs, slots, products):
    pairs = seqs * GROUP * q_blocks * k_blocks * slots * slots // 2
    return pl.CostEstimate(
        flops=pairs * HEAD * 2 * products,
        transcendentals=pairs,
        bytes_accessed=4 * seqs * slots * 4 * HEAD * (q_blocks + k_blocks),
    )


def attention(info, mixed, shared, grad=None, awaited=()):
    blocks, seqs, slots, _ = mixed.shape
    wide = 2 * HEAD
    small = shared is mixed
    k_blocks = shared.shape[0]
    params = dict(vmem_limit_bytes=48 * 1024 * 1024)
    cost = attention_cost(blocks, k_blocks, seqs, slots, 2 if grad is None else 5)
    if small:
        whole = lambda part: pl.BlockSpec(
            (blocks, 1, slots, wide), lambda seq, info: (0, seq, 0, part)
        )
        if grad is None:
            return pl.pallas_call(
                forward_small,
                out_shape=jax.ShapeDtypeStruct((blocks, seqs, slots, wide), BF16),
                grid_spec=pltpu.PrefetchScalarGridSpec(
                    num_scalar_prefetch=1,
                    grid=(seqs,),
                    in_specs=[whole(0), whole(1)]
                    + [pl.BlockSpec(memory_space=pl.ANY)] * len(awaited),
                    out_specs=whole(0),
                ),
                compiler_params=pltpu.CompilerParams(**params),
                cost_estimate=cost,
            )(info, mixed, mixed, *awaited)
        return pl.pallas_call(
            backward_small,
            out_shape=jax.ShapeDtypeStruct((blocks, seqs, slots, 2 * wide), F32),
            grid_spec=pltpu.PrefetchScalarGridSpec(
                num_scalar_prefetch=1,
                grid=(seqs,),
                in_specs=[whole(0), whole(1), whole(0)]
                + [pl.BlockSpec(memory_space=pl.ANY)] * len(awaited),
                out_specs=pl.BlockSpec(
                    (blocks, 1, slots, 2 * wide), lambda seq, info: (0, seq, 0, 0)
                ),
                scratch_shapes=[pltpu.VMEM((blocks * slots, HEAD), F32)] * 2,
            ),
            compiler_params=pltpu.CompilerParams(**params),
            cost_estimate=cost,
        )(info, mixed, mixed, grad, *awaited)
    one = pl.BlockSpec((1, 1, slots, wide), lambda seq, block, info: (block, seq, 0, 0))
    every = pl.BlockSpec((k_blocks, 1, slots, wide), lambda seq, block, info: (0, seq, 0, 0))
    out = jax.ShapeDtypeStruct((blocks, seqs, slots, wide), BF16)
    if grad is None:
        return pl.pallas_call(
            forward_large,
            out_shape=out,
            grid_spec=pltpu.PrefetchScalarGridSpec(
                num_scalar_prefetch=1, grid=(seqs, blocks), in_specs=[one, every], out_specs=one
            ),
            compiler_params=pltpu.CompilerParams(**params),
            cost_estimate=cost,
        )(info, mixed, shared)
    return pl.pallas_call(
        backward_large,
        out_shape=(
            jax.ShapeDtypeStruct((blocks, seqs, slots, wide), F32),
            jax.ShapeDtypeStruct((k_blocks, seqs, slots, wide), F32),
        ),
        grid_spec=pltpu.PrefetchScalarGridSpec(
            num_scalar_prefetch=1,
            grid=(seqs, blocks),
            in_specs=[one, every, one],
            out_specs=(one, every),
        ),
        compiler_params=pltpu.CompilerParams(**params),
        cost_estimate=cost,
    )(info, mixed, shared, grad)


POSITION_ROWS = 16
POSITION_BASE = 256


def lane_of(shape):
    return lax.broadcasted_iota(jnp.int32, shape, 1)


def head_mean(values):
    lanes = values.shape[1]
    same = (
        lax.broadcasted_iota(jnp.int32, (lanes, lanes), 0) // HEAD
        == lax.broadcasted_iota(jnp.int32, (lanes, lanes), 1) // HEAD
    )
    ones = jnp.where(same, 1.0, 0.0).astype(BF16)
    high = values.astype(BF16)
    rest = values - high.astype(F32)
    middle = rest.astype(BF16)
    low = (rest - middle.astype(F32)).astype(BF16)
    return (product(high, ones) + product(middle, ones) + product(low, ones)) * (1.0 / HEAD)


def turn(values):
    lanes = values.shape[1]
    first = lane_of(values.shape) % HEAD < HEAD // 2
    return jnp.where(
        first,
        -pltpu.roll(values, lanes - HEAD // 2, 1),
        pltpu.roll(values, HEAD // 2, 1),
    )


def project_kernel(info_ref, near_ref, far_ref, weight_ref, gain_ref, head_gain_ref, freq_ref, *rest):
    normed_ref, projected_ref, mixed_ref, cosine_ref, sine_ref = rest[-5:]
    my_row, my_place = info_ref[0], info_ref[1]
    depth = weight_ref.shape[1]
    rows = normed_ref.shape[1]
    wide = 2 * HEAD
    for which, ref in enumerate((near_ref, far_ref)):
        place = my_place if which == 0 else 1 - my_place
        values = ref[:rows].astype(F32)
        scale = lax.rsqrt(jnp.mean(values * values, axis=-1, keepdims=True) + epsilon)
        normed = (values * scale * gain_ref[...]).astype(BF16)
        normed_ref[place] = normed
        total = jnp.zeros((rows, weight_ref.shape[2]), F32)
        for block in range(weight_ref.shape[0]):
            weight = weight_ref[block ^ my_row]
            total = total + product(normed[:, block * depth : (block + 1) * depth], weight)
        projected_ref[place] = total
        digits = ref[rows : rows + POSITION_ROWS, :rows].astype(F32)
        position = digits[0:1] * POSITION_BASE + digits[1:2]
        angle = jnp.broadcast_to(position, (wide, rows)).T * freq_ref[...]
        cosine, sine = jnp.cos(angle), jnp.sin(angle)
        cosine_ref[place] = cosine
        sine_ref[place] = sine
        for part in range(2):
            lanes = slice(part * wide, (part + 1) * wide)
            piece = total[:, lanes]
            scaled = piece * lax.rsqrt(head_mean(piece * piece) + epsilon) * head_gain_ref[:, lanes]
            turned = scaled * cosine + turn(scaled) * sine
            if part == 1:
                turned = jnp.where(lane_of(turned.shape) < HEAD, turned, piece)
            mixed_ref[place, :, lanes] = turned.astype(BF16)


def project(info, near, far, weight, gain, head_gain, frequency, blocks, earlier):
    rows, width = near.shape
    rows -= POSITION_ROWS
    mix = weight.shape[2]
    wide = 2 * HEAD
    whole = lambda *shape: pl.BlockSpec(shape, lambda step, info: (0,) * len(shape))
    pair = lambda last: pl.BlockSpec((2, rows, last), lambda step, info: (info[2], 0, 0))
    outs = ((width, BF16), (mix, F32), (mix, BF16), (wide, F32), (wide, F32))
    in_specs = [
        whole(*near.shape),
        whole(*near.shape),
        whole(*weight.shape),
        whole(1, width),
        whole(1, mix),
        whole(1, wide),
    ]
    aliases = {}
    operands = [near, far, weight, gain, head_gain, frequency]
    if earlier is not None:
        aliases = {1 + len(operands) + i: i for i in range(len(outs))}
        in_specs += [pl.BlockSpec(memory_space=pl.ANY)] * len(outs)
        operands += list(earlier)
    return pl.pallas_call(
        project_kernel,
        out_shape=tuple(jax.ShapeDtypeStruct((blocks, rows, last), kind) for last, kind in outs),
        grid_spec=pltpu.PrefetchScalarGridSpec(
            num_scalar_prefetch=1,
            grid=(1,),
            in_specs=in_specs,
            out_specs=tuple(pair(last) for last, _ in outs),
        ),
        input_output_aliases=aliases,
        compiler_params=pltpu.CompilerParams(vmem_limit_bytes=32 * 1024 * 1024),
        cost_estimate=pl.CostEstimate(
            flops=4 * rows * width * mix, transcendentals=0, bytes_accessed=8 * rows * width
        ),
    )(info, *operands)


def unproject_kernel(
    grad_ref, projected_ref, head_gain_ref, cosine_ref, sine_ref, *refs
):
    out_ref, gain_ref = refs[-2:]
    wide = 2 * HEAD

    @pl.when(pl.program_id(0) == 0)
    def _():
        gain_ref[...] = jnp.zeros_like(gain_ref)

    cosine, sine = cosine_ref[0], sine_ref[0]
    for part in range(2):
        lanes = slice(part * wide, (part + 1) * wide)
        grad = grad_ref[0, :, lanes]
        piece = projected_ref[0, :, lanes]
        back = grad * cosine - turn(grad) * sine
        scale = lax.rsqrt(head_mean(piece * piece) + epsilon)
        hat = piece * scale
        gain_ref[:, lanes] += jnp.sum(back * hat, axis=0, keepdims=True)
        back = back * head_gain_ref[:, lanes]
        back = scale * (back - hat * head_mean(back * hat))
        if part == 1:
            back = jnp.where(lane_of(back.shape) < HEAD, back, grad)
        out_ref[0, :, lanes] = back.astype(BF16)


def unproject(grad, projected, head_gain, cosine, sine, awaited=()):
    blocks, rows, mix = grad.shape
    one = lambda last: pl.BlockSpec((1, rows, last), lambda step: (step, 0, 0))
    flat = pl.BlockSpec((1, mix), lambda step: (0, 0))
    return pl.pallas_call(
        unproject_kernel,
        out_shape=(
            jax.ShapeDtypeStruct((blocks, rows, mix), BF16),
            jax.ShapeDtypeStruct((1, mix), F32),
        ),
        grid=(blocks,),
        in_specs=[one(mix), one(mix), flat, one(cosine.shape[2]), one(cosine.shape[2])]
        + [pl.BlockSpec(memory_space=pl.ANY)] * len(awaited),
        out_specs=(one(mix), flat),
        compiler_params=pltpu.CompilerParams(vmem_limit_bytes=32 * 1024 * 1024),
        cost_estimate=pl.CostEstimate(
            flops=100 * blocks * rows * mix, transcendentals=0, bytes_accessed=12 * blocks * rows * mix
        ),
    )(grad, projected, head_gain, cosine, sine, *awaited)


TAIL = 64


def half_tile(low, tile, keep_low):
    rolled = pltpu.roll(tile, TAIL, 1)
    return jnp.where(low, tile, rolled) if keep_low else jnp.where(low, rolled, tile)


def pack_kernel(info_ref, gate_ref, up_ref, *out_refs):
    low = info_ref[1] == 0
    main = (gate_ref.shape[1] - 2 * TAIL) // 2
    for index, out_ref in enumerate(out_refs):

        @pl.when(pl.program_id(0) == index)
        def _():
            for place in range(2):

                @pl.when(info_ref[1] == place)
                def _():
                    lanes = slice(place * main, (place + 1) * main)
                    out_ref[:, :main] = gate_ref[:, lanes].astype(BF16)
                    out_ref[:, main : 2 * main] = up_ref[:, lanes].astype(BF16)

            gate = half_tile(low, gate_ref[:, 2 * main :], True)
            up = half_tile(low, up_ref[:, 2 * main :], False)
            both = jnp.where(lane_of(gate.shape) < TAIL, gate, up)
            out_ref[:, 2 * main :] = both.astype(BF16)


def pack(info, gate, up, near):
    rows, width = gate.shape
    shard = width // near
    block = pl.BlockSpec((rows, shard), lambda step, info: (0, info[0] ^ step))
    out = pl.BlockSpec((rows, shard), lambda step, info: (0, 0))
    return pl.pallas_call(
        pack_kernel,
        out_shape=(jax.ShapeDtypeStruct((rows, shard), BF16),) * near,
        grid_spec=pltpu.PrefetchScalarGridSpec(
            num_scalar_prefetch=1, grid=(near,), in_specs=[block, block], out_specs=(out,) * near
        ),
        compiler_params=pltpu.CompilerParams(vmem_limit_bytes=32 * 1024 * 1024),
        cost_estimate=pl.CostEstimate(
            flops=0, transcendentals=0, bytes_accessed=10 * rows * width
        ),
    )(info, gate, up)


def spread_kernel(info_ref, *refs):
    pieces = (len(refs) - 2) // 2
    gate_ref, up_ref = refs[2 * pieces :]
    rows, shard = gate_ref.shape
    main = (shard - 2 * TAIL) // 2
    low = info_ref[1] == 0

    def whole(parts):
        parts = [ref[:, 0] for ref in parts]
        return jnp.concatenate(parts, axis=1).reshape(rows, shard).astype(F32)

    mine, other = whole(refs[:pieces]), whole(refs[pieces : 2 * pieces])
    first = jnp.where(low, mine, other)
    second = jnp.where(low, other, mine)
    gate_ref[:, :main] = first[:, :main]
    gate_ref[:, main : 2 * main] = second[:, :main]
    up_ref[:, :main] = first[:, main : 2 * main]
    up_ref[:, main : 2 * main] = second[:, main : 2 * main]
    first, second = first[:, 2 * main :], second[:, 2 * main :]
    lower = lane_of(first.shape) < TAIL
    gate_ref[:, 2 * main :] = jnp.where(lower, first, pltpu.roll(second, TAIL, 1))
    up_ref[:, 2 * main :] = jnp.where(lower, pltpu.roll(first, TAIL, 1), second)


def spread(info, mine, other):
    planes, near, _, width = mine[0].shape
    rows = planes * sum(piece.shape[2] for piece in mine)
    block = lambda piece: pl.BlockSpec(
        (planes, 1, piece.shape[2], width), lambda step, info: (0, step, 0, 0)
    )
    out = pl.BlockSpec((rows, width), lambda step, info: (0, info[0] ^ step))
    shape = jax.ShapeDtypeStruct((rows, near * width), F32)
    return pl.pallas_call(
        spread_kernel,
        out_shape=(shape, shape),
        grid_spec=pltpu.PrefetchScalarGridSpec(
            num_scalar_prefetch=1,
            grid=(near,),
            in_specs=[block(piece) for piece in (*mine, *other)],
            out_specs=(out, out),
        ),
        compiler_params=pltpu.CompilerParams(vmem_limit_bytes=40 * 1024 * 1024),
        cost_estimate=pl.CostEstimate(
            flops=0, transcendentals=0, bytes_accessed=12 * near * rows * width
        ),
    )(info, *mine, *other)


def mix_heads_kernel(query_ref, key_ref, value_ref, out_ref):
    wide = 2 * HEAD
    for head in range(KV_HEADS):
        out_ref[:, 2 * head * wide : (2 * head + 1) * wide] = query_ref[
            :, head * wide : (head + 1) * wide
        ].astype(BF16)
        tile = slice(head // 2 * wide, (head // 2 + 1) * wide)
        key, value = key_ref[:, tile], value_ref[:, tile]
        if head % 2 == 0:
            value = pltpu.roll(value, HEAD, 1)
        else:
            key = pltpu.roll(key, HEAD, 1)
        both = jnp.where(lane_of(key.shape) < HEAD, key, value)
        out_ref[:, (2 * head + 1) * wide : (2 * head + 2) * wide] = both.astype(BF16)


def mix_heads(query, key, value):
    rows = query.shape[0]
    width = query.shape[1] + key.shape[1] + value.shape[1]
    return pl.pallas_call(
        mix_heads_kernel,
        out_shape=jax.ShapeDtypeStruct((rows, width), BF16),
        compiler_params=pltpu.CompilerParams(vmem_limit_bytes=32 * 1024 * 1024),
        cost_estimate=pl.CostEstimate(flops=0, transcendentals=0, bytes_accessed=6 * rows * width),
    )(query, key, value)


def part_heads_kernel(mixed_ref, query_ref, key_ref, value_ref):
    wide = 2 * HEAD
    for pair in range(KV_HEADS // 2):
        tile = slice(pair * wide, (pair + 1) * wide)
        for head in (2 * pair, 2 * pair + 1):
            query_ref[:, head * wide : (head + 1) * wide] = mixed_ref[head, :, :wide].astype(F32)
        first = mixed_ref[2 * pair, :, wide:].astype(F32)
        second = mixed_ref[2 * pair + 1, :, wide:].astype(F32)
        lower = lane_of(first.shape) < HEAD
        key_ref[:, tile] = jnp.where(lower, first, pltpu.roll(second, HEAD, 1))
        value_ref[:, tile] = jnp.where(lower, pltpu.roll(first, HEAD, 1), second)


def part_heads(mixed, rows):
    heads, _, mix = mixed.shape
    block = pl.BlockSpec((heads, rows, mix), lambda step: (0, 0, 0))
    out = lambda count: pl.BlockSpec((rows, count * HEAD), lambda step: (0, 0))
    shape = lambda count: jax.ShapeDtypeStruct((rows, count * HEAD), F32)
    return pl.pallas_call(
        part_heads_kernel,
        out_shape=(shape(GROUP * heads), shape(heads), shape(heads)),
        grid=(1,),
        in_specs=[block],
        out_specs=(out(GROUP * heads), out(heads), out(heads)),
        compiler_params=pltpu.CompilerParams(vmem_limit_bytes=32 * 1024 * 1024),
        cost_estimate=pl.CostEstimate(
            flops=0, transcendentals=0, bytes_accessed=6 * rows * heads * 4 * HEAD
        ),
    )(mixed)


def row_scale(values):
    return lax.rsqrt(jnp.mean(values * values, axis=-1, keepdims=True) + epsilon)


def norm_back(grad, values, gain):
    scale = row_scale(values)
    gain_grad = jnp.sum(grad * values * scale, axis=0, keepdims=True)
    grad = grad * gain
    mean = jnp.mean(grad * values, axis=-1, keepdims=True)
    return scale * grad - values * (scale * scale * scale) * mean, gain_grad


def row_call(kernel, outs, flops, *operands, awaited=()):
    moved = sum(a.size * a.dtype.itemsize for a in operands)
    count = len(operands)

    def body(*refs):
        kernel(*refs[:count], *refs[count + len(awaited) :])

    return pl.pallas_call(
        body,
        grid=(1,),
        in_specs=[whole_spec(a.shape) for a in operands] + awaiting(len(awaited)),
        out_specs=tuple(whole_spec(shape) for shape, _ in outs),
        out_shape=tuple(jax.ShapeDtypeStruct(shape, kind) for shape, kind in outs),
        compiler_params=pltpu.CompilerParams(vmem_limit_bytes=40 * 1024 * 1024),
        cost_estimate=pl.CostEstimate(flops=flops, transcendentals=0, bytes_accessed=moved),
    )(*operands, *awaited)


def join_kernel(heads_ref, weight_ref, input_ref, gain_ref, hidden_ref, mid_ref):
    wide = heads_ref.shape[2]
    total = input_ref[...].astype(F32)
    for head in range(0, heads_ref.shape[0], 2):
        both = jnp.concatenate([heads_ref[head], heads_ref[head + 1]], axis=1)
        total = total + product(both, weight_ref[head * wide : (head + 2) * wide])
    hidden_ref[...] = total
    mid_ref[...] = (total * row_scale(total) * gain_ref[...]).astype(BF16)


def middle_kernel(
    low_own, low_got, high_own, high_got, hidden_ref, outer_ref, gain_ref, weight_ref,
    grad_ref, low_ref, heads_ref, part_ref,
):
    grad_mid = jnp.concatenate(
        [
            low_own[...] + low_got[...].astype(F32),
            high_own[...] + high_got[...].astype(F32),
        ],
        axis=0,
    )
    through, gain_grad = norm_back(grad_mid, hidden_ref[...], gain_ref[...])
    part_ref[...] = gain_grad
    grad = outer_ref[...].astype(F32) + through
    grad_ref[...] = grad
    low = grad.astype(BF16)
    low_ref[...] = low
    wide = heads_ref.shape[2]
    for head in range(0, heads_ref.shape[0], 2):
        both = by_transpose(low, weight_ref[head * wide : (head + 2) * wide]).astype(BF16)
        heads_ref[head] = both[:, :wide]
        heads_ref[head + 1] = both[:, wide:]


def output_weight_kernel(heads_ref, grad_ref, out_ref):
    wide = heads_ref.shape[2]
    for head in range(heads_ref.shape[0]):
        out_ref[head * wide : (head + 1) * wide] = transpose_by(
            heads_ref[head], grad_ref[...]
        ).astype(BF16)


def input_kernel(heads_ref, weight_ref, input_ref, hidden_ref, gain_ref, grad_ref, part_ref):
    mix = heads_ref.shape[2]
    total = jnp.zeros(grad_ref.shape, F32)
    for head in range(heads_ref.shape[0]):
        total = total + by_transpose(
            heads_ref[head], weight_ref[:, head * mix : (head + 1) * mix]
        )
    through, gain_grad = norm_back(total, input_ref[...].astype(F32), gain_ref[...])
    part_ref[...] = gain_grad
    grad_ref[...] = hidden_ref[...] + through


def feed_kernel(info_ref, *refs):
    mids, outers, weights = refs[:10], refs[10], refs[11:15]
    down_ref = refs[15]
    mid_ref, outer_ref, inner_ref, grads_ref, send_ref, keep_ref = refs[-12:-6]
    mid_all, outer_all, weight_all, mid_sem, outer_sem, weight_sem = refs[-6:]
    step = pl.program_id(0)
    main = inner_ref.shape[1] - TAIL

    def weight_copy(block):
        return pltpu.make_async_copy(
            weights[block], weight_all.at[info_ref[0] ^ block], weight_sem.at[block]
        )

    @pl.when(step == 0)
    def _():
        for block in range(len(weights)):
            weight_copy(block).start()
        for block in range(PLANE):
            change = 2 * block + 1 if block < 4 else 2 * block - 8
            pltpu.make_async_copy(
                outers.at[change ^ info_ref[2]], outer_all.at[block], outer_sem.at[block]
            ).start()
            first = 5 * (block // 4) + block % 4
            if block % 4 < 3:
                pltpu.make_async_copy(mids[first], mid_all.at[block], mid_sem.at[block]).start()
            else:
                half = mids[first].shape[0]
                for part in range(2):
                    target = mid_all.at[block].at[pl.ds(part * half, half)]
                    pltpu.make_async_copy(mids[first + part], target, mid_sem.at[block]).start()
        for block in range(len(weights)):
            weight_copy(block).wait()

    for which in range(2):
        block = 2 * step + which
        pltpu.make_async_copy(mids[0], mid_all.at[block], mid_sem.at[block]).wait()
        pltpu.make_async_copy(outers.at[0], outer_all.at[block], outer_sem.at[block]).wait()
    fsdp, depth, width = weight_all.shape
    weight = weight_all[...].reshape(fsdp * depth, width)
    rows = mid_all.shape[1]

    def unit(gate, up, back):
        share = jax.nn.sigmoid(gate)
        silu = gate * share
        inner = (silu * up).astype(BF16)
        grad_gate = (back * up * (share + silu * (1.0 - share))).astype(BF16)
        return inner, grad_gate, (back * silu).astype(BF16)

    tail = slice(2 * main, 2 * main + TAIL)
    last = slice(2 * main + TAIL, 2 * main + 2 * TAIL)
    parts = []
    for which in range(2):
        mine = slice(which * rows, (which + 1) * rows)
        mid, outer = mid_all[2 * step + which], outer_all[2 * step + which]
        mid_ref[mine] = mid
        outer_ref[mine] = outer
        both = product(mid, weight)
        back = by_transpose(outer, down_ref[...])
        inner, gate, up = unit(both[:, :main], both[:, main : 2 * main], back[:, :main])
        inner_ref[mine, :main] = inner
        inner, gate_tail, up_tail = unit(both[:, tail], both[:, last], back[:, main:])
        inner_ref[mine, main:] = inner
        grads = jnp.concatenate([gate, up, gate_tail, up_tail], axis=1)
        grads_ref[mine] = grads
        parts.append(by_transpose(grads, weight).astype(BF16))

    @pl.when(step < 2)
    def _():
        send_ref[:rows] = parts[0]
        send_ref[rows:] = parts[1]

    @pl.when(step >= 2)
    def _():
        keep_ref[:rows] = parts[0]
        keep_ref[rows:] = parts[1]


def feed(info, mids, outers, weights, down, awaited=()):
    rows, width = mids[0].shape
    depth, units2 = weights[0].shape
    units = units2 // 2
    count = PLANE
    anywhere = pl.BlockSpec(memory_space=pl.ANY)
    flat = lambda last: pl.BlockSpec((2 * rows, last), lambda step, info: (step, 0))
    send = pl.BlockSpec((2 * rows, width), lambda step, info: (jnp.minimum(step, 1), 0))
    keep = pl.BlockSpec((2 * rows, width), lambda step, info: (jnp.maximum(step - 2, 0), 0))
    shape = lambda tall, last: jax.ShapeDtypeStruct((tall * rows, last), BF16)
    return pl.pallas_call(
        feed_kernel,
        out_shape=(
            shape(count, width),
            shape(count, width),
            shape(count, units),
            shape(count, units2),
            shape(count // 2, width),
            shape(count // 2, width),
        ),
        grid_spec=pltpu.PrefetchScalarGridSpec(
            num_scalar_prefetch=1,
            grid=(count // 2,),
            in_specs=[anywhere] * (len(mids) + 1 + len(weights))
            + [pl.BlockSpec(down.shape, lambda step, info: (0, 0))]
            + [anywhere] * len(awaited),
            out_specs=(flat(width), flat(width), flat(units), flat(units2), send, keep),
            scratch_shapes=[
                pltpu.VMEM((count, rows, width), BF16),
                pltpu.VMEM((count, rows, width), BF16),
                pltpu.VMEM((len(weights), depth, units2), BF16),
                pltpu.SemaphoreType.DMA((count,)),
                pltpu.SemaphoreType.DMA((count,)),
                pltpu.SemaphoreType.DMA((len(weights),)),
            ],
        ),
        compiler_params=pltpu.CompilerParams(vmem_limit_bytes=56 * 1024 * 1024),
        cost_estimate=pl.CostEstimate(
            flops=10 * count * rows * width * units,
            transcendentals=count * rows * units,
            bytes_accessed=12 * count * rows * width,
        ),
    )(info, *mids, outers, *weights, down, *awaited)


def hidden_weight_kernel(mid_ref, grads_ref, out_ref):
    planes, _, rows, width = out_ref.shape
    total = transpose_by(mid_ref[...], grads_ref[...])
    out_ref[:, 0] = total.reshape(planes, rows, width).astype(BF16)


def hidden_weight(mid, grads, near, planes):
    count, width = mid.shape
    units2 = grads.shape[1]
    rows = width // near // planes
    return pl.pallas_call(
        hidden_weight_kernel,
        out_shape=jax.ShapeDtypeStruct((planes, near, rows, units2), BF16),
        grid=(near,),
        in_specs=[
            pl.BlockSpec((count, width // near), lambda step: (0, step)),
            pl.BlockSpec((count, units2), lambda step: (0, 0)),
        ],
        out_specs=pl.BlockSpec((planes, 1, rows, units2), lambda step: (0, step, 0, 0)),
        compiler_params=pltpu.CompilerParams(vmem_limit_bytes=48 * 1024 * 1024),
        cost_estimate=pl.CostEstimate(
            flops=2 * count * width * units2,
            transcendentals=0,
            bytes_accessed=2 * count * (width + units2) + 2 * width * units2,
        ),
    )(mid, grads)


def down_spread_kernel(low_ref, mine_ref, other_ref, out_ref):
    main = mine_ref.shape[0] - TAIL
    low = low_ref[...] == 0
    mine, other = mine_ref[...].astype(F32), other_ref[...].astype(F32)
    first, second = jnp.where(low, mine, other), jnp.where(low, other, mine)
    out_ref[:main] = first[:main]
    out_ref[main : 2 * main] = second[:main]
    out_ref[2 * main : 2 * main + TAIL] = first[main:]
    out_ref[2 * main + TAIL :] = second[main:]


def awaiting(count):
    return [pl.BlockSpec(memory_space=pl.ANY)] * count


def whole_spec(shape):
    return pl.BlockSpec(shape, lambda *_: (0,) * len(shape))


def split_rows(blocks, cut, awaited):
    rows, width = blocks[0].shape
    count = len(blocks)

    def kernel(*refs):
        for index in range(count):
            refs[-2][index] = refs[index][:cut]
            refs[-1][index] = refs[index][cut:]

    return pl.pallas_call(
        kernel,
        out_shape=(
            jax.ShapeDtypeStruct((count, cut, width), BF16),
            jax.ShapeDtypeStruct((count, rows - cut, width), BF16),
        ),
        grid=(1,),
        in_specs=[whole_spec((rows, width))] * count + awaiting(len(awaited)),
        out_specs=(whole_spec((count, cut, width)), whole_spec((count, rows - cut, width))),
        cost_estimate=pl.CostEstimate(
            flops=0, transcendentals=0, bytes_accessed=4 * count * rows * width
        ),
    )(*blocks, *awaited)


def head_message(first, second, rest, awaited):
    def kernel(first_ref, second_ref, rest_ref, *refs):
        rows = first_ref.shape[0]
        refs[-1][:rows] = (first_ref[...].astype(F32) + second_ref[...].astype(F32)).astype(BF16)
        refs[-1][rows:] = rest_ref[...].astype(BF16)

    rows, width = first.shape
    shape = (rows + rest.shape[0], width)
    return pl.pallas_call(
        kernel,
        out_shape=jax.ShapeDtypeStruct(shape, BF16),
        grid=(1,),
        in_specs=[whole_spec(a.shape) for a in (first, second, rest)] + awaiting(len(awaited)),
        out_specs=whole_spec(shape),
        cost_estimate=pl.CostEstimate(
            flops=0, transcendentals=0, bytes_accessed=6 * rows * width
        ),
    )(first, second, rest, *awaited)


def per_device(
    inputs,
    lengths,
    positions,
    cotangent,
    w_query,
    w_key,
    w_value,
    w_output,
    w_gate,
    w_up,
    w_down,
    attn_gain,
    ffn_gain,
    query_gain,
    key_gain,
):
    groups, slot_count, model_width = inputs.shape
    row_count = groups * slot_count
    own_rows = w_query.shape[0]
    ctx_size = lax.axis_size("ctx")
    fsdp_size = lax.axis_size("fsdp")
    me_f = lax.axis_index("fsdp")
    me_c = lax.axis_index("ctx")
    inner = KV_HEADS
    outer = ctx_size // inner
    inner_groups = [[o * inner + i for i in range(inner)] for o in range(outer)]
    outer_groups = [[o * inner + i for o in range(outer)] for i in range(inner)]
    planes = ctx_size // 2
    plane_groups_z = [[2 * i + low for i in range(planes)] for low in range(2)]
    low_bit = me_c % 2
    my_head = me_c % inner
    mix = 4 * HEAD
    wide = GROUP * HEAD
    ff_shard = w_down.shape[0]
    ff_own = ff_shard // 2
    ff_main = ff_own - TAIL

    slots = me_c * slot_count + jnp.arange(slot_count)
    valid = (slots[None, :] < lengths[:, None]).astype(F32).reshape(row_count, 1)
    info = jnp.concatenate([(me_c // inner * inner)[None].astype(jnp.int32), lengths])
    device_info = jnp.stack([me_f, low_bit]).astype(jnp.int32)
    plane_info = jnp.stack([me_f, low_bit, low_bit * fsdp_size + me_f]).astype(jnp.int32)

    small = query_gain.shape[0]
    gains = jnp.concatenate([attn_gain, ffn_gain, query_gain, key_gain]).astype(BF16)[None]
    gains = jnp.concatenate(gather_near(gains), axis=0).astype(F32)
    gains = jnp.stack([pick(gains, me_f ^ k) for k in range(fsdp_size)])
    attn_scale = gains[:, :own_rows].reshape(1, model_width)
    ffn_scale = gains[:, own_rows : 2 * own_rows].reshape(1, model_width)
    qgain_scale = gains[:, 2 * own_rows : 2 * own_rows + small].reshape(-1)
    kgain_scale = gains[:, 2 * own_rows + small :].reshape(-1)
    head_gain = jnp.concatenate(
        [qgain_scale] * GROUP + [kgain_scale, jnp.ones((HEAD,), F32)]
    ).reshape(1, mix)

    line = Line()
    rows_shape = (row_count, model_width)

    line = Line()
    rows_shape = (row_count, model_width)
    rows_flops = 2 * row_count * model_width * model_width

    flat_low = inputs.reshape(row_count, model_width)
    place_row = positions.reshape(1, row_count)
    digits = jnp.concatenate([place_row // POSITION_BASE, place_row % POSITION_BASE], axis=0)
    digits = jnp.pad(
        digits.astype(BF16), ((0, POSITION_ROWS - 2), (0, model_width - row_count))
    )
    near = line(lambda a, b: jnp.concatenate([a, b], axis=0), flat_low, digits)
    far, following = trade(near, 4), ring_step(near)
    places = ring_places(my_head // 2)
    frequency = rope_base ** (-jnp.arange(0, HEAD, 2).astype(F32) / HEAD)
    frequency = jnp.concatenate([frequency] * (2 * GROUP)).reshape(1, wide)

    qkv_own = line(mix_heads, w_query, w_key, w_value)
    head_weight = lax.dynamic_slice_in_dim(qkv_own, my_head * mix, mix, 1)
    head_weight = jnp.stack(gather_near(head_weight))
    output_own = line(lambda a: a.astype(BF16), w_output)
    output_weight = lax.all_gather(output_own, "fsdp", axis=0, tiled=True)
    gu_own = line(lambda a, b: pack(device_info, a, b, fsdp_size), w_gate, w_up)
    gu_parts = [gu_own[0]] + [trade(gu_own[k], k) for k in range(1, fsdp_size)]

    earlier = ()
    for step in range(4):
        if step < 3:
            far, following = line.wait(far, following)
            next_far = trade(following, 4)
            after_next = ring_step(following) if step < 2 else None
        else:
            gu_parts = line.wait(*gu_parts)
        project_info = jnp.stack([me_f, low_bit, places[step]]).astype(jnp.int32)
        earlier = line(
            lambda a, b, c, *rest: project(
                project_info, a, b, c, attn_scale, head_gain, frequency, inner, rest or None
            ),
            near,
            far,
            head_weight,
            *earlier,
        )
        near, far, following = following, next_far, after_next
    normed_all, projected, mixed, cosine, sine = earlier
    mixed = mixed.reshape(inner, groups, slot_count, mix)

    qkv_weight = lax.all_gather(qkv_own, "fsdp", axis=0, tiled=True)
    if outer == 1:
        attended = line(lambda a: attention(info, a, a, None, (qkv_weight,)), mixed)
    else:
        shared = lax.all_gather(
            mixed[..., 2 * HEAD :], "ctx", axis=0, axis_index_groups=outer_groups, tiled=True
        )
        attended = line(lambda a, b: attention(info, a, b), mixed, shared)

    def exchange(values):
        return lax.all_to_all(values, "ctx", 0, 0, axis_index_groups=inner_groups, tiled=True)

    attended = exchange(attended.reshape(inner, row_count, wide))
    outer_low = line(
        lambda a: (a.reshape(rows_shape).astype(F32) * valid).astype(BF16), cotangent
    )
    outer_all = lax.all_gather(
        outer_low, ("ctx", "fsdp"), axis=0, axis_index_groups=plane_groups(), tiled=False
    )
    down_weight = line(
        lambda a: jnp.concatenate(
            [
                lax.dynamic_slice_in_dim(a, low_bit * ff_main, ff_main, 0),
                lax.dynamic_slice_in_dim(a, 2 * ff_main + low_bit * TAIL, TAIL, 0),
            ],
            axis=0,
        ).astype(BF16),
        w_down,
    )
    hidden_res, mid_low = line(
        lambda *a: row_call(
            join_kernel, ((rows_shape, F32), (rows_shape, BF16)), rows_flops, *a
        ),
        attended,
        output_weight,
        flat_low,
        ffn_scale,
    )
    mid_x, mid_y = trade(mid_low, 2), trade(mid_low, 4)
    mid_cut = line(cut_far, mid_x, mid_y)
    mid_corner = trade(mid_cut[0], 4), trade(mid_cut[1], 2)
    mid_all = gather_plane(mid_low, mid_x, mid_y, mid_corner)

    mid_all, outer_all, inner_low, grad_gu, send, keep = line(
        lambda *a: feed(plane_info, a[:10], a[10], a[11:15], a[15]),
        *mid_all,
        outer_all,
        *gu_parts,
        down_weight,
    )
    got = trade(send, 1)
    gu_part = line(lambda a, b: hidden_weight(a, b, fsdp_size, planes), mid_all, grad_gu)
    gu_sum = lax.psum_scatter(
        gu_part.reshape(-1, 2 * ff_own),
        "ctx",
        scatter_dimension=0,
        axis_index_groups=plane_groups_z,
        tiled=True,
    )
    low_send, high_send, low, high = line(cut_plane, got, keep)
    low_got, high_got = trade(low_send, 2), trade(high_send, 4)
    down_part = line(lambda a, b: transpose_by(a, b).astype(BF16), inner_low, outer_all)
    down_sum = lax.psum(down_part, "ctx", axis_index_groups=plane_groups_z)
    result_part = line(lambda a, b: product(a, b).astype(BF16), inner_low, down_weight)
    low_far, high_far, low_own, high_own = line(join_plane, low, high, low_got, high_got)
    low_got, high_got = trade(low_far, 4), trade(high_far, 2)
    (qkv_weight,) = line.wait(qkv_weight)
    grad_hidden, grad_attn_low, grad_heads, ffn_part = line(
        lambda *a: row_call(
            middle_kernel,
            (
                (rows_shape, F32),
                (rows_shape, BF16),
                ((inner, row_count, wide), BF16),
                ((1, model_width), F32),
            ),
            rows_flops,
            *a,
        ),
        low_own,
        low_got,
        high_own,
        high_got,
        hidden_res,
        outer_low,
        ffn_scale,
        output_weight,
    )

    grad_heads = exchange(grad_heads).reshape(inner, groups, slot_count, wide)
    (output_part,) = line(
        lambda *a: row_call(
            output_weight_kernel, (((model_width, model_width), BF16),), rows_flops, *a
        ),
        attended,
        grad_attn_low,
    )
    gu_own = line(
        lambda a: tuple(
            pick(a.reshape(fsdp_size, own_rows // planes, 2 * ff_own), me_f ^ k)
            for k in range(fsdp_size)
        ),
        gu_sum,
    )
    gu_blocks = [gu_own[0]] + [trade(gu_own[k], k) for k in range(1, fsdp_size)]
    if outer == 1:
        grad_mixed = line(
            lambda a, b: attention(info, a, a, b, gu_own[1:]), mixed, grad_heads
        )
    else:
        grad_q, grad_kv = line(
            lambda a, b, c: attention(info, a, b, c), mixed, shared, grad_heads
        )
        grad_kv = lax.psum_scatter(
            grad_kv, "ctx", scatter_dimension=0, axis_index_groups=outer_groups, tiled=True
        )
        grad_mixed = jnp.concatenate([grad_q, grad_kv], axis=-1)
    grad_head, head_part = line(
        lambda *a: unproject(*a, gu_blocks[1:]),
        grad_mixed.reshape(inner, row_count, mix),
        projected,
        head_gain,
        cosine,
        sine,
    )
    grad_qkv = exchange(grad_head)
    head_rows = line(
        lambda a, b: transpose_by(
            a.reshape(inner * row_count, model_width), b.reshape(-1, mix)
        ).astype(BF16),
        normed_all,
        grad_head,
    )
    head_send, head_keep = line(
        lambda a: cut_near(a.reshape(fsdp_size, own_rows, mix), me_f), head_rows
    )
    head_got = trade(head_send, 1)
    cut = own_rows // planes // 2
    first_half, second_half = split_rows(gu_blocks, cut, (down_sum, grad_head))
    gu_mine = [
        lax.all_gather(piece, "ctx", axis=0, axis_index_groups=plane_groups_z, tiled=False)
        for piece in (first_half, second_half)
    ]
    gu_other = [trade(piece, fsdp_size) for piece in gu_mine]

    head_pair = line(add_low, head_keep, head_got)
    head_far = trade(head_pair[1], 2)
    output_send, output_keep = line(
        lambda a: cut_near(a.reshape(fsdp_size, own_rows, model_width), me_f), output_part
    )
    output_got = trade(output_send, 1)
    output_pair = line(add_low, output_keep, output_got)
    output_far = trade(output_pair[1], 2)
    down_other = trade(down_sum, fsdp_size)
    input_grad, attn_part = line(
        lambda *a: row_call(
            input_kernel,
            ((rows_shape, F32), ((1, model_width), F32)),
            rows_flops * KV_HEADS * mix // model_width,
            *a,
            awaited=(gu_mine[0],),
        ),
        grad_qkv,
        qkv_weight,
        flat_low,
        grad_hidden,
        attn_scale,
    )
    input_grad = input_grad.reshape(groups, slot_count, model_width)
    qgain_part = sum(head_part[0, i * HEAD : (i + 1) * HEAD] for i in range(GROUP))
    kgain_part = head_part[0, GROUP * HEAD : (GROUP + 1) * HEAD]
    gain_parts = jnp.concatenate(
        [
            attn_part.reshape(fsdp_size, own_rows),
            ffn_part.reshape(fsdp_size, own_rows),
            qgain_part.reshape(fsdp_size, small),
            kgain_part.reshape(fsdp_size, small),
        ],
        axis=-1,
    )
    output_own = line(add_low, output_pair[0], output_far)
    output_grad = (
        ctx_sum(output_own.reshape(ctx_size, own_rows // ctx_size, model_width))
        .reshape(own_rows, model_width)
        .astype(F32)
    )
    result_send, result_keep = halves(result_part)
    got = trade(result_send, 1)
    gain_count = gain_parts.size
    gain_near = gain_parts + trade(gain_parts, 1)
    gain_near = gain_near + trade(gain_near, 2)
    gain_rows = -(-gain_count // (16 * mix)) * 16
    gain_near = jnp.pad(gain_near.reshape(-1), (0, gain_rows * mix - gain_count))
    gain_near = gain_near.reshape(gain_rows, mix)
    head_first, head_second = head_pair[0], head_far
    if outer > 1:
        gain_near = lax.psum(gain_near, "ctx", axis_index_groups=outer_groups)
        head_first = lax.psum(
            add_low(head_first, head_second).astype(F32), "ctx", axis_index_groups=outer_groups
        ).astype(BF16)
        head_second = jnp.zeros_like(head_first)
    head_own = head_message(head_first, head_second, gain_near, ())
    head_blocks = lax.all_gather(
        head_own, "ctx", axis=0, axis_index_groups=inner_groups, tiled=False
    )
    gain_sum = jnp.sum(head_blocks[:, own_rows:].astype(F32), axis=0)
    gain_sum = pick(gain_sum.reshape(-1)[:gain_count].reshape(gain_parts.shape), me_f)
    low_send, high_send, result_low, result_high = line(cut_plane, got, result_keep)
    result_low_got, result_high_got = trade(low_send, 2), trade(high_send, 4)
    low_far, high_far, low_own, high_own = line(
        join_plane, result_low, result_high, result_low_got, result_high_got
    )
    low_got, high_got = trade(low_far, 4), trade(high_far, 2)
    result = line(
        lambda a, b, c, d, e: (
            valid * (e + jnp.concatenate([a + b.astype(F32), c + d.astype(F32)], axis=0))
        ).astype(BF16),
        low_own,
        low_got,
        high_own,
        high_got,
        hidden_res,
    )
    block_output = result.reshape(groups, slot_count, model_width)

    query_grad, key_grad, value_grad = part_heads(head_blocks, own_rows)
    (down_grad,) = row_call(
        down_spread_kernel,
        (((2 * ff_own, model_width), F32),),
        0,
        low_bit.reshape(1, 1),
        down_sum,
        down_other,
        awaited=(gu_mine[1], head_own),
    )
    gate_grad, up_grad = spread(device_info, gu_mine, gu_other)

    return (
        block_output,
        input_grad,
        query_grad,
        key_grad,
        value_grad,
        output_grad,
        gate_grad,
        up_grad,
        down_grad,
        gain_sum[:own_rows],
        gain_sum[own_rows : 2 * own_rows],
        gain_sum[2 * own_rows : 2 * own_rows + small],
        gain_sum[2 * own_rows + small :],
    )


def solution(mesh):
    return jax.shard_map(
        per_device,
        mesh=mesh,
        in_specs=(
            P("fsdp", "ctx", None),
            P("fsdp"),
            P("fsdp", "ctx"),
            P("fsdp", "ctx", None),
            P("fsdp", None),
            P("fsdp", None),
            P("fsdp", None),
            P("fsdp", None),
            P("fsdp", None),
            P("fsdp", None),
            P("fsdp", None),
            P("fsdp"),
            P("fsdp"),
            P("fsdp"),
            P("fsdp"),
        ),
        out_specs=(
            P("fsdp", "ctx", None),
            P("fsdp", "ctx", None),
            P("fsdp", None),
            P("fsdp", None),
            P("fsdp", None),
            P("fsdp", None),
            P("fsdp", None),
            P("fsdp", None),
            P("fsdp", None),
            P("fsdp"),
            P("fsdp"),
            P("fsdp"),
            P("fsdp"),
        ),
        check_vma=False,
    )
```

```python
import jax
import jax.numpy as jnp
from jax import lax
from jax.experimental import pallas as pl
from jax.experimental.pallas import tpu as pltpu
from jax.sharding import PartitionSpec as P

HEADS = 16
KV_HEADS = 8
HEAD = 64
GROUP = HEADS // KV_HEADS


epsilon = 1e-05
rope_base = 1000000.0
masked = -1e30
F32 = jnp.float32
BF16 = jnp.bfloat16


def dot_over(left, right, left_dim, right_dim):
    return lax.dot_general(
        left, right, (((left_dim,), (right_dim,)), ((), ())), preferred_element_type=F32
    )


def product(left, right):
    return dot_over(left, right, 1, 0)


def by_transpose(left, right):
    return dot_over(left, right, 1, 1)


def transpose_by(left, right):
    return dot_over(left, right, 0, 0)


PLANE = 8


def trade(values, step):
    size = lax.axis_size("ctx") * lax.axis_size("fsdp")
    return lax.ppermute(values, ("ctx", "fsdp"), [(i, i ^ step) for i in range(size)])


def pick(values, index, axis=0):
    return lax.dynamic_index_in_dim(values, index, axis, keepdims=False)


class Line:
    def __init__(self):
        self.last = None

    def __call__(self, step, *operands):
        if self.last is not None:
            operands = lax.optimization_barrier((*operands, self.last))[:-1]
        result = step(*operands)
        self.last = jax.tree.leaves(result)[0]
        return result

    def wait(self, *values):
        *values, self.last = lax.optimization_barrier((*values, self.last))
        return values


def add_low(first, second):
    return (first.astype(F32) + second.astype(F32)).astype(BF16)


def halves(values):
    half = values.shape[0] // 2
    return values[:half], values[half:]


def cut_far(over_x, over_y):
    return halves(over_x)[0], halves(over_y)[1]


def gather_plane(values, over_x, over_y, corner):
    far = [values, over_x, over_y, *corner]
    return [trade(block, 1) for block in far] + far


def plane_groups():
    size = lax.axis_size("ctx") * lax.axis_size("fsdp")
    return [list(range(start, start + PLANE)) for start in range(0, size, PLANE)]


def cut_plane(send_got, keep):
    pair = add_low(keep, send_got).reshape(4, -1, keep.shape[1])
    half = pair.shape[1] // 2
    low, high = pair[:, :half], pair[:, half:]
    return jnp.stack([low[1], low[3]]), jnp.stack([high[2], high[3]]), low[::2], high[:2]


def join_plane(low, high, low_got, high_got):
    low_own = low[0].astype(F32) + low_got[0].astype(F32)
    high_own = high[0].astype(F32) + high_got[0].astype(F32)
    return add_low(low[1], low_got[1]), add_low(high[1], high_got[1]), low_own, high_own


def cut_near(part, me_f):
    blocks = [pick(part, me_f ^ k) for k in range(4)]
    return jnp.stack([blocks[1], blocks[3]]), jnp.stack([blocks[0], blocks[2]])


def gather_near(values):
    far = trade(values, 2)
    near = trade(values, 1)
    return [values, near, far, trade(far, 1)]


def sum_everywhere(values):
    step = 1
    while step < lax.axis_size("ctx") * lax.axis_size("fsdp"):
        values = values + trade(values, step)
        step *= 2
    return values


RING = (0, 1, 3, 2)


def ring_step(values):
    following = {RING[i]: RING[(i + 1) % 4] for i in range(4)}
    pairs = []
    for c in range(lax.axis_size("ctx")):
        outer, place, low = c // 8, c // 2 % 4, c % 2
        pairs.append((c, outer * 8 + following[place] * 2 + low))
    return lax.ppermute(values, "ctx", pairs)


def ring_places(place):
    before = {RING[(i + 1) % 4]: RING[i] for i in range(4)}
    table = []
    for start in range(4):
        row = [start]
        for _ in range(3):
            row.append(before[row[-1]])
        table.append(row)
    return jnp.array(table, jnp.int32)[place]


def plane_step(values, moves):
    size = lax.axis_size("ctx") * lax.axis_size("fsdp")
    pairs = []
    for device in range(size):
        place, rest = device // PLANE, device % PLANE
        pairs += [(device, to * PLANE + rest) for start, to in moves if start == place]
    return lax.ppermute(values, ("ctx", "fsdp"), pairs)


def ctx_bits():
    size = lax.axis_size("ctx")
    bits = []
    step = 1
    while step < size:
        bits.append(step)
        step *= 2
    return bits


def ctx_sum(values):
    me = lax.axis_index("ctx")
    near = lax.axis_size("fsdp")
    for step in ctx_bits():
        shape = values.shape
        halves = values.reshape((2, shape[0] // 2) + shape[1:])
        mine = (me // step) % 2
        got = trade(pick(halves, 1 - mine), step * near)
        values = (pick(halves, mine).astype(F32) + got.astype(F32)).astype(BF16)
    for step in reversed(ctx_bits()):
        mine = (me // step) % 2
        got = trade(values, step * near)
        first = jnp.where(mine == 0, values, got)
        second = jnp.where(mine == 0, got, values)
        values = jnp.concatenate([first, second], axis=0)
    return values


def two_heads(block):
    return jnp.concatenate([block[:, :HEAD], block[:, HEAD:]], axis=0)


def side_by_side(stacked):
    rows = stacked.shape[0] // 2
    return jnp.concatenate([stacked[:rows], stacked[rows:]], axis=1)


def allowed_mask(rows, count, first_query, first_key, seq_len):
    query_slot = first_query + lax.broadcasted_iota(jnp.int32, (rows, count), 0) % (rows // GROUP)
    key_slot = first_key + lax.broadcasted_iota(jnp.int32, (rows, count), 1)
    return (key_slot <= query_slot) & (key_slot < seq_len)


def whole_row(q_ref, kv_ref, index, seq_len):
    slots = q_ref.shape[2]
    count = (index + 1) * slots
    query = two_heads(q_ref[index, 0]) * (HEAD**-0.5)
    both = kv_ref[: index + 1, 0].reshape(count, 2 * HEAD)
    key, value = both[:, :HEAD], both[:, HEAD:]
    scores = by_transpose(query, key)
    scores = jnp.where(
        allowed_mask(GROUP * slots, count, index * slots, 0, seq_len), scores, masked
    )
    exponent = jnp.exp(scores - jnp.max(scores, axis=-1, keepdims=True))
    weights = exponent * (1.0 / jnp.sum(exponent, axis=-1, keepdims=True))
    return query, key, value, weights


def forward_small(info_ref, q_ref, kv_ref, *refs):
    out_ref = refs[-1]
    seq_len = info_ref[pl.program_id(0) + 1]
    slots = q_ref.shape[2]
    for index in range(q_ref.shape[0]):

        @pl.when(index * slots < seq_len)
        def _():
            _, _, value, weights = whole_row(q_ref, kv_ref, index, seq_len)
            out_ref[index, 0] = side_by_side(product(weights.astype(BF16), value)).astype(BF16)

        @pl.when(index * slots >= seq_len)
        def _():
            out_ref[index, 0] = jnp.zeros(out_ref.shape[2:], BF16)


def backward_small(info_ref, q_ref, kv_ref, grad_ref, *refs):
    out_ref, key_acc, value_acc = refs[-3:]
    seq_len = info_ref[pl.program_id(0) + 1]
    blocks, _, slots, _ = q_ref.shape
    key_acc[...] = jnp.zeros_like(key_acc)
    value_acc[...] = jnp.zeros_like(value_acc)
    for index in range(blocks):

        @pl.when(index * slots < seq_len)
        def _():
            count = (index + 1) * slots
            query, key, value, weights = whole_row(q_ref, kv_ref, index, seq_len)
            grad = two_heads(grad_ref[index, 0])
            grad_weights = by_transpose(grad, value)
            delta = jnp.sum(weights * grad_weights, axis=-1, keepdims=True)
            grad_scores = (weights * (grad_weights - delta)).astype(BF16)
            out_ref[index, 0, :, : 2 * HEAD] = side_by_side(
                product(grad_scores, key) * (HEAD**-0.5)
            )
            key_acc[:count] += transpose_by(grad_scores, query)
            value_acc[:count] += transpose_by(weights.astype(BF16), grad)

        @pl.when(index * slots >= seq_len)
        def _():
            out_ref[index, 0, :, : 2 * HEAD] = jnp.zeros((slots, 2 * HEAD), F32)

    for index in range(blocks):
        rows = slice(index * slots, (index + 1) * slots)
        out_ref[index, 0, :, 2 * HEAD :] = jnp.concatenate(
            [key_acc[rows], value_acc[rows]], axis=1
        )


def row_stats(query, kv_ref, index, first_query, seq_len):
    slots = kv_ref.shape[2]
    rows = query.shape[0]

    def scores_of(block):
        both = kv_ref[block, 0]
        scores = by_transpose(query, both[:, :HEAD])
        allowed = allowed_mask(rows, slots, first_query, block * slots, seq_len)
        return both, jnp.where(allowed, scores, masked)

    def step(block, state):
        top, total = state
        _, scores = scores_of(block)
        new_top = jnp.maximum(top, jnp.max(scores, axis=-1, keepdims=True))
        grown = jnp.sum(jnp.exp(scores - new_top), axis=-1, keepdims=True)
        return new_top, total * jnp.exp(top - new_top) + grown

    start = (jnp.full((rows, 1), masked, F32), jnp.zeros((rows, 1), F32))
    top, total = lax.fori_loop(0, index + 1, step, start)
    inverse = 1.0 / total

    def weights_of(block):
        both, scores = scores_of(block)
        return both, jnp.exp(scores - top) * inverse

    return weights_of


def forward_large(info_ref, q_ref, kv_ref, out_ref):
    seq_len = info_ref[pl.program_id(0) + 1]
    slots = q_ref.shape[2]
    index = info_ref[0] + pl.program_id(1)
    live = index * slots < seq_len

    @pl.when(live)
    def _():
        query = two_heads(q_ref[0, 0]) * (HEAD**-0.5)
        weights_of = row_stats(query, kv_ref, index, index * slots, seq_len)

        def step(block, total):
            both, weights = weights_of(block)
            return total + product(weights.astype(BF16), both[:, HEAD:])

        total = lax.fori_loop(0, index + 1, step, jnp.zeros((GROUP * slots, HEAD), F32))
        out_ref[0, 0] = side_by_side(total).astype(BF16)

    @pl.when(jnp.logical_not(live))
    def _():
        out_ref[0, 0] = jnp.zeros(out_ref.shape[2:], BF16)


def backward_large(info_ref, q_ref, kv_ref, grad_ref, out_ref, kv_out_ref):
    seq_len = info_ref[pl.program_id(0) + 1]
    slots = q_ref.shape[2]
    index = info_ref[0] + pl.program_id(1)
    live = index * slots < seq_len

    @pl.when(pl.program_id(1) == 0)
    def _():
        kv_out_ref[...] = jnp.zeros_like(kv_out_ref)

    @pl.when(live)
    def _():
        query = two_heads(q_ref[0, 0]) * (HEAD**-0.5)
        grad = two_heads(grad_ref[0, 0])
        weights_of = row_stats(query, kv_ref, index, index * slots, seq_len)

        def delta_step(block, total):
            both, weights = weights_of(block)
            grad_weights = by_transpose(grad, both[:, HEAD:])
            return total + jnp.sum(weights * grad_weights, axis=-1, keepdims=True)

        delta = lax.fori_loop(0, index + 1, delta_step, jnp.zeros((GROUP * slots, 1), F32))

        def step(block, total):
            both, weights = weights_of(block)
            grad_weights = by_transpose(grad, both[:, HEAD:])
            grad_scores = (weights * (grad_weights - delta)).astype(BF16)
            kv_out_ref[block, 0] += jnp.concatenate(
                [transpose_by(grad_scores, query), transpose_by(weights.astype(BF16), grad)], axis=1
            )
            return total + product(grad_scores, both[:, :HEAD])

        total = lax.fori_loop(0, index + 1, step, jnp.zeros((GROUP * slots, HEAD), F32))
        out_ref[0, 0] = side_by_side(total * (HEAD**-0.5))

    @pl.when(jnp.logical_not(live))
    def _():
        out_ref[0, 0] = jnp.zeros(out_ref.shape[2:], F32)


def attention_cost(q_blocks, k_blocks, seqs, slots, products):
    pairs = seqs * GROUP * q_blocks * k_blocks * slots * slots // 2
    return pl.CostEstimate(
        flops=pairs * HEAD * 2 * products,
        transcendentals=pairs,
        bytes_accessed=4 * seqs * slots * 4 * HEAD * (q_blocks + k_blocks),
    )


def attention(info, mixed, shared, grad=None, awaited=()):
    blocks, seqs, slots, _ = mixed.shape
    wide = 2 * HEAD
    small = shared is mixed
    k_blocks = shared.shape[0]
    params = dict(vmem_limit_bytes=48 * 1024 * 1024)
    cost = attention_cost(blocks, k_blocks, seqs, slots, 2 if grad is None else 5)
    if small:
        whole = lambda part: pl.BlockSpec(
            (blocks, 1, slots, wide), lambda seq, info: (0, seq, 0, part)
        )
        if grad is None:
            return pl.pallas_call(
                forward_small,
                out_shape=jax.ShapeDtypeStruct((blocks, seqs, slots, wide), BF16),
                grid_spec=pltpu.PrefetchScalarGridSpec(
                    num_scalar_prefetch=1,
                    grid=(seqs,),
                    in_specs=[whole(0), whole(1)]
                    + [pl.BlockSpec(memory_space=pl.ANY)] * len(awaited),
                    out_specs=whole(0),
                ),
                compiler_params=pltpu.CompilerParams(**params),
                cost_estimate=cost,
            )(info, mixed, mixed, *awaited)
        return pl.pallas_call(
            backward_small,
            out_shape=jax.ShapeDtypeStruct((blocks, seqs, slots, 2 * wide), F32),
            grid_spec=pltpu.PrefetchScalarGridSpec(
                num_scalar_prefetch=1,
                grid=(seqs,),
                in_specs=[whole(0), whole(1), whole(0)]
                + [pl.BlockSpec(memory_space=pl.ANY)] * len(awaited),
                out_specs=pl.BlockSpec(
                    (blocks, 1, slots, 2 * wide), lambda seq, info: (0, seq, 0, 0)
                ),
                scratch_shapes=[pltpu.VMEM((blocks * slots, HEAD), F32)] * 2,
            ),
            compiler_params=pltpu.CompilerParams(**params),
            cost_estimate=cost,
        )(info, mixed, mixed, grad, *awaited)
    one = pl.BlockSpec((1, 1, slots, wide), lambda seq, block, info: (block, seq, 0, 0))
    every = pl.BlockSpec((k_blocks, 1, slots, wide), lambda seq, block, info: (0, seq, 0, 0))
    out = jax.ShapeDtypeStruct((blocks, seqs, slots, wide), BF16)
    if grad is None:
        return pl.pallas_call(
            forward_large,
            out_shape=out,
            grid_spec=pltpu.PrefetchScalarGridSpec(
                num_scalar_prefetch=1, grid=(seqs, blocks), in_specs=[one, every], out_specs=one
            ),
            compiler_params=pltpu.CompilerParams(**params),
            cost_estimate=cost,
        )(info, mixed, shared)
    return pl.pallas_call(
        backward_large,
        out_shape=(
            jax.ShapeDtypeStruct((blocks, seqs, slots, wide), F32),
            jax.ShapeDtypeStruct((k_blocks, seqs, slots, wide), F32),
        ),
        grid_spec=pltpu.PrefetchScalarGridSpec(
            num_scalar_prefetch=1,
            grid=(seqs, blocks),
            in_specs=[one, every, one],
            out_specs=(one, every),
        ),
        compiler_params=pltpu.CompilerParams(**params),
        cost_estimate=cost,
    )(info, mixed, shared, grad)


POSITION_ROWS = 16
POSITION_BASE = 256


def lane_of(shape):
    return lax.broadcasted_iota(jnp.int32, shape, 1)


def head_mean(values):
    lanes = values.shape[1]
    same = (
        lax.broadcasted_iota(jnp.int32, (lanes, lanes), 0) // HEAD
        == lax.broadcasted_iota(jnp.int32, (lanes, lanes), 1) // HEAD
    )
    ones = jnp.where(same, 1.0, 0.0).astype(BF16)
    high = values.astype(BF16)
    rest = values - high.astype(F32)
    middle = rest.astype(BF16)
    low = (rest - middle.astype(F32)).astype(BF16)
    return (product(high, ones) + product(middle, ones) + product(low, ones)) * (1.0 / HEAD)


def turn(values):
    lanes = values.shape[1]
    first = lane_of(values.shape) % HEAD < HEAD // 2
    return jnp.where(
        first,
        -pltpu.roll(values, lanes - HEAD // 2, 1),
        pltpu.roll(values, HEAD // 2, 1),
    )


def project_kernel(info_ref, near_ref, far_ref, weight_ref, gain_ref, head_gain_ref, freq_ref, *rest):
    normed_ref, projected_ref, mixed_ref, cosine_ref, sine_ref = rest[-5:]
    my_row, my_place = info_ref[0], info_ref[1]
    depth = weight_ref.shape[1]
    rows = normed_ref.shape[1]
    wide = 2 * HEAD
    for which, ref in enumerate((near_ref, far_ref)):
        place = my_place if which == 0 else 1 - my_place
        values = ref[:rows].astype(F32)
        scale = lax.rsqrt(jnp.mean(values * values, axis=-1, keepdims=True) + epsilon)
        normed = (values * scale * gain_ref[...]).astype(BF16)
        normed_ref[place] = normed
        total = jnp.zeros((rows, weight_ref.shape[2]), F32)
        for block in range(weight_ref.shape[0]):
            weight = weight_ref[block ^ my_row]
            total = total + product(normed[:, block * depth : (block + 1) * depth], weight)
        projected_ref[place] = total
        digits = ref[rows : rows + POSITION_ROWS, :rows].astype(F32)
        position = digits[0:1] * POSITION_BASE + digits[1:2]
        angle = jnp.broadcast_to(position, (wide, rows)).T * freq_ref[...]
        cosine, sine = jnp.cos(angle), jnp.sin(angle)
        cosine_ref[place] = cosine
        sine_ref[place] = sine
        for part in range(2):
            lanes = slice(part * wide, (part + 1) * wide)
            piece = total[:, lanes]
            scaled = piece * lax.rsqrt(head_mean(piece * piece) + epsilon) * head_gain_ref[:, lanes]
            turned = scaled * cosine + turn(scaled) * sine
            if part == 1:
                turned = jnp.where(lane_of(turned.shape) < HEAD, turned, piece)
            mixed_ref[place, :, lanes] = turned.astype(BF16)


def project(info, near, far, weight, gain, head_gain, frequency, blocks, earlier):
    rows, width = near.shape
    rows -= POSITION_ROWS
    mix = weight.shape[2]
    wide = 2 * HEAD
    whole = lambda *shape: pl.BlockSpec(shape, lambda step, info: (0,) * len(shape))
    pair = lambda last: pl.BlockSpec((2, rows, last), lambda step, info: (info[2], 0, 0))
    outs = ((width, BF16), (mix, F32), (mix, BF16), (wide, F32), (wide, F32))
    in_specs = [
        whole(*near.shape),
        whole(*near.shape),
        whole(*weight.shape),
        whole(1, width),
        whole(1, mix),
        whole(1, wide),
    ]
    aliases = {}
    operands = [near, far, weight, gain, head_gain, frequency]
    if earlier is not None:
        aliases = {1 + len(operands) + i: i for i in range(len(outs))}
        in_specs += [pl.BlockSpec(memory_space=pl.ANY)] * len(outs)
        operands += list(earlier)
    return pl.pallas_call(
        project_kernel,
        out_shape=tuple(jax.ShapeDtypeStruct((blocks, rows, last), kind) for last, kind in outs),
        grid_spec=pltpu.PrefetchScalarGridSpec(
            num_scalar_prefetch=1,
            grid=(1,),
            in_specs=in_specs,
            out_specs=tuple(pair(last) for last, _ in outs),
        ),
        input_output_aliases=aliases,
        compiler_params=pltpu.CompilerParams(vmem_limit_bytes=32 * 1024 * 1024),
        cost_estimate=pl.CostEstimate(
            flops=4 * rows * width * mix, transcendentals=0, bytes_accessed=8 * rows * width
        ),
    )(info, *operands)


def unproject_kernel(
    grad_ref, projected_ref, head_gain_ref, cosine_ref, sine_ref, *refs
):
    out_ref, gain_ref = refs[-2:]
    wide = 2 * HEAD

    @pl.when(pl.program_id(0) == 0)
    def _():
        gain_ref[...] = jnp.zeros_like(gain_ref)

    cosine, sine = cosine_ref[0], sine_ref[0]
    for part in range(2):
        lanes = slice(part * wide, (part + 1) * wide)
        grad = grad_ref[0, :, lanes]
        piece = projected_ref[0, :, lanes]
        back = grad * cosine - turn(grad) * sine
        scale = lax.rsqrt(head_mean(piece * piece) + epsilon)
        hat = piece * scale
        gain_ref[:, lanes] += jnp.sum(back * hat, axis=0, keepdims=True)
        back = back * head_gain_ref[:, lanes]
        back = scale * (back - hat * head_mean(back * hat))
        if part == 1:
            back = jnp.where(lane_of(back.shape) < HEAD, back, grad)
        out_ref[0, :, lanes] = back.astype(BF16)


def unproject(grad, projected, head_gain, cosine, sine, awaited=()):
    blocks, rows, mix = grad.shape
    one = lambda last: pl.BlockSpec((1, rows, last), lambda step: (step, 0, 0))
    flat = pl.BlockSpec((1, mix), lambda step: (0, 0))
    return pl.pallas_call(
        unproject_kernel,
        out_shape=(
            jax.ShapeDtypeStruct((blocks, rows, mix), BF16),
            jax.ShapeDtypeStruct((1, mix), F32),
        ),
        grid=(blocks,),
        in_specs=[one(mix), one(mix), flat, one(cosine.shape[2]), one(cosine.shape[2])]
        + [pl.BlockSpec(memory_space=pl.ANY)] * len(awaited),
        out_specs=(one(mix), flat),
        compiler_params=pltpu.CompilerParams(vmem_limit_bytes=32 * 1024 * 1024),
        cost_estimate=pl.CostEstimate(
            flops=100 * blocks * rows * mix, transcendentals=0, bytes_accessed=12 * blocks * rows * mix
        ),
    )(grad, projected, head_gain, cosine, sine, *awaited)


TAIL = 64


def half_tile(low, tile, keep_low):
    rolled = pltpu.roll(tile, TAIL, 1)
    return jnp.where(low, tile, rolled) if keep_low else jnp.where(low, rolled, tile)


def pack_kernel(info_ref, gate_ref, up_ref, *out_refs):
    low = info_ref[1] == 0
    main = (gate_ref.shape[1] - 2 * TAIL) // 2
    for index, out_ref in enumerate(out_refs):

        @pl.when(pl.program_id(0) == index)
        def _():
            for place in range(2):

                @pl.when(info_ref[1] == place)
                def _():
                    lanes = slice(place * main, (place + 1) * main)
                    out_ref[:, :main] = gate_ref[:, lanes].astype(BF16)
                    out_ref[:, main : 2 * main] = up_ref[:, lanes].astype(BF16)

            gate = half_tile(low, gate_ref[:, 2 * main :], True)
            up = half_tile(low, up_ref[:, 2 * main :], False)
            both = jnp.where(lane_of(gate.shape) < TAIL, gate, up)
            out_ref[:, 2 * main :] = both.astype(BF16)


def pack(info, gate, up, near):
    rows, width = gate.shape
    shard = width // near
    block = pl.BlockSpec((rows, shard), lambda step, info: (0, info[0] ^ step))
    out = pl.BlockSpec((rows, shard), lambda step, info: (0, 0))
    return pl.pallas_call(
        pack_kernel,
        out_shape=(jax.ShapeDtypeStruct((rows, shard), BF16),) * near,
        grid_spec=pltpu.PrefetchScalarGridSpec(
            num_scalar_prefetch=1, grid=(near,), in_specs=[block, block], out_specs=(out,) * near
        ),
        compiler_params=pltpu.CompilerParams(vmem_limit_bytes=32 * 1024 * 1024),
        cost_estimate=pl.CostEstimate(
            flops=0, transcendentals=0, bytes_accessed=10 * rows * width
        ),
    )(info, gate, up)


def spread_kernel(info_ref, *refs):
    pieces = (len(refs) - 2) // 2
    gate_ref, up_ref = refs[2 * pieces :]
    rows, shard = gate_ref.shape
    main = (shard - 2 * TAIL) // 2
    low = info_ref[1] == 0

    def whole(parts):
        parts = [ref[:, 0] for ref in parts]
        return jnp.concatenate(parts, axis=1).reshape(rows, shard).astype(F32)

    mine, other = whole(refs[:pieces]), whole(refs[pieces : 2 * pieces])
    first = jnp.where(low, mine, other)
    second = jnp.where(low, other, mine)
    gate_ref[:, :main] = first[:, :main]
    gate_ref[:, main : 2 * main] = second[:, :main]
    up_ref[:, :main] = first[:, main : 2 * main]
    up_ref[:, main : 2 * main] = second[:, main : 2 * main]
    first, second = first[:, 2 * main :], second[:, 2 * main :]
    lower = lane_of(first.shape) < TAIL
    gate_ref[:, 2 * main :] = jnp.where(lower, first, pltpu.roll(second, TAIL, 1))
    up_ref[:, 2 * main :] = jnp.where(lower, pltpu.roll(first, TAIL, 1), second)


def spread(info, mine, other):
    planes, near, _, width = mine[0].shape
    rows = planes * sum(piece.shape[2] for piece in mine)
    block = lambda piece: pl.BlockSpec(
        (planes, 1, piece.shape[2], width), lambda step, info: (0, step, 0, 0)
    )
    out = pl.BlockSpec((rows, width), lambda step, info: (0, info[0] ^ step))
    shape = jax.ShapeDtypeStruct((rows, near * width), F32)
    return pl.pallas_call(
        spread_kernel,
        out_shape=(shape, shape),
        grid_spec=pltpu.PrefetchScalarGridSpec(
            num_scalar_prefetch=1,
            grid=(near,),
            in_specs=[block(piece) for piece in (*mine, *other)],
            out_specs=(out, out),
        ),
        compiler_params=pltpu.CompilerParams(vmem_limit_bytes=40 * 1024 * 1024),
        cost_estimate=pl.CostEstimate(
            flops=0, transcendentals=0, bytes_accessed=12 * near * rows * width
        ),
    )(info, *mine, *other)


def mix_heads_kernel(query_ref, key_ref, value_ref, out_ref):
    wide = 2 * HEAD
    for head in range(KV_HEADS):
        out_ref[:, 2 * head * wide : (2 * head + 1) * wide] = query_ref[
            :, head * wide : (head + 1) * wide
        ].astype(BF16)
        tile = slice(head // 2 * wide, (head // 2 + 1) * wide)
        key, value = key_ref[:, tile], value_ref[:, tile]
        if head % 2 == 0:
            value = pltpu.roll(value, HEAD, 1)
        else:
            key = pltpu.roll(key, HEAD, 1)
        both = jnp.where(lane_of(key.shape) < HEAD, key, value)
        out_ref[:, (2 * head + 1) * wide : (2 * head + 2) * wide] = both.astype(BF16)


def mix_heads(query, key, value):
    rows = query.shape[0]
    width = query.shape[1] + key.shape[1] + value.shape[1]
    return pl.pallas_call(
        mix_heads_kernel,
        out_shape=jax.ShapeDtypeStruct((rows, width), BF16),
        compiler_params=pltpu.CompilerParams(vmem_limit_bytes=32 * 1024 * 1024),
        cost_estimate=pl.CostEstimate(flops=0, transcendentals=0, bytes_accessed=6 * rows * width),
    )(query, key, value)


def part_heads_kernel(mixed_ref, query_ref, key_ref, value_ref):
    wide = 2 * HEAD
    for pair in range(KV_HEADS // 2):
        tile = slice(pair * wide, (pair + 1) * wide)
        for head in (2 * pair, 2 * pair + 1):
            query_ref[:, head * wide : (head + 1) * wide] = mixed_ref[head, :, :wide].astype(F32)
        first = mixed_ref[2 * pair, :, wide:].astype(F32)
        second = mixed_ref[2 * pair + 1, :, wide:].astype(F32)
        lower = lane_of(first.shape) < HEAD
        key_ref[:, tile] = jnp.where(lower, first, pltpu.roll(second, HEAD, 1))
        value_ref[:, tile] = jnp.where(lower, pltpu.roll(first, HEAD, 1), second)


def part_heads(mixed, rows):
    heads, _, mix = mixed.shape
    block = pl.BlockSpec((heads, rows, mix), lambda step: (0, 0, 0))
    out = lambda count: pl.BlockSpec((rows, count * HEAD), lambda step: (0, 0))
    shape = lambda count: jax.ShapeDtypeStruct((rows, count * HEAD), F32)
    return pl.pallas_call(
        part_heads_kernel,
        out_shape=(shape(GROUP * heads), shape(heads), shape(heads)),
        grid=(1,),
        in_specs=[block],
        out_specs=(out(GROUP * heads), out(heads), out(heads)),
        compiler_params=pltpu.CompilerParams(vmem_limit_bytes=32 * 1024 * 1024),
        cost_estimate=pl.CostEstimate(
            flops=0, transcendentals=0, bytes_accessed=6 * rows * heads * 4 * HEAD
        ),
    )(mixed)


def row_scale(values):
    return lax.rsqrt(jnp.mean(values * values, axis=-1, keepdims=True) + epsilon)


def norm_back(grad, values, gain):
    scale = row_scale(values)
    gain_grad = jnp.sum(grad * values * scale, axis=0, keepdims=True)
    grad = grad * gain
    mean = jnp.mean(grad * values, axis=-1, keepdims=True)
    return scale * grad - values * (scale * scale * scale) * mean, gain_grad


def row_call(kernel, outs, flops, *operands, awaited=()):
    moved = sum(a.size * a.dtype.itemsize for a in operands)
    count = len(operands)

    def body(*refs):
        kernel(*refs[:count], *refs[count + len(awaited) :])

    return pl.pallas_call(
        body,
        grid=(1,),
        in_specs=[whole_spec(a.shape) for a in operands] + awaiting(len(awaited)),
        out_specs=tuple(whole_spec(shape) for shape, _ in outs),
        out_shape=tuple(jax.ShapeDtypeStruct(shape, kind) for shape, kind in outs),
        compiler_params=pltpu.CompilerParams(vmem_limit_bytes=40 * 1024 * 1024),
        cost_estimate=pl.CostEstimate(flops=flops, transcendentals=0, bytes_accessed=moved),
    )(*operands, *awaited)


def join_kernel(heads_ref, weight_ref, input_ref, gain_ref, hidden_ref, mid_ref):
    wide = heads_ref.shape[2]
    total = input_ref[...].astype(F32)
    for head in range(0, heads_ref.shape[0], 2):
        both = jnp.concatenate([heads_ref[head], heads_ref[head + 1]], axis=1)
        total = total + product(both, weight_ref[head * wide : (head + 2) * wide])
    hidden_ref[...] = total
    mid_ref[...] = (total * row_scale(total) * gain_ref[...]).astype(BF16)


def middle_kernel(
    low_own, low_got, high_own, high_got, hidden_ref, outer_ref, gain_ref, weight_ref,
    grad_ref, low_ref, heads_ref, part_ref,
):
    grad_mid = jnp.concatenate(
        [
            low_own[...] + low_got[...].astype(F32),
            high_own[...] + high_got[...].astype(F32),
        ],
        axis=0,
    )
    through, gain_grad = norm_back(grad_mid, hidden_ref[...], gain_ref[...])
    part_ref[...] = gain_grad
    grad = outer_ref[...].astype(F32) + through
    grad_ref[...] = grad
    low = grad.astype(BF16)
    low_ref[...] = low
    wide = heads_ref.shape[2]
    for head in range(0, heads_ref.shape[0], 2):
        both = by_transpose(low, weight_ref[head * wide : (head + 2) * wide]).astype(BF16)
        heads_ref[head] = both[:, :wide]
        heads_ref[head + 1] = both[:, wide:]


def output_weight_kernel(heads_ref, grad_ref, out_ref):
    wide = heads_ref.shape[2]
    for head in range(heads_ref.shape[0]):
        out_ref[head * wide : (head + 1) * wide] = transpose_by(
            heads_ref[head], grad_ref[...]
        ).astype(BF16)


def input_kernel(heads_ref, weight_ref, input_ref, hidden_ref, gain_ref, grad_ref, part_ref):
    mix = heads_ref.shape[2]
    total = jnp.zeros(grad_ref.shape, F32)
    for head in range(heads_ref.shape[0]):
        total = total + by_transpose(
            heads_ref[head], weight_ref[:, head * mix : (head + 1) * mix]
        )
    through, gain_grad = norm_back(total, input_ref[...].astype(F32), gain_ref[...])
    part_ref[...] = gain_grad
    grad_ref[...] = hidden_ref[...] + through


def feed_kernel(info_ref, *refs):
    mids, outers, weights = refs[:10], refs[10], refs[11:15]
    down_ref = refs[15]
    mid_ref, outer_ref, inner_ref, grads_ref, send_ref, keep_ref = refs[-12:-6]
    mid_all, outer_all, weight_all, mid_sem, outer_sem, weight_sem = refs[-6:]
    step = pl.program_id(0)
    main = inner_ref.shape[1] - TAIL

    def weight_copy(block):
        return pltpu.make_async_copy(
            weights[block], weight_all.at[info_ref[0] ^ block], weight_sem.at[block]
        )

    @pl.when(step == 0)
    def _():
        for block in range(len(weights)):
            weight_copy(block).start()
        for block in range(PLANE):
            change = 2 * block + 1 if block < 4 else 2 * block - 8
            pltpu.make_async_copy(
                outers.at[change ^ info_ref[2]], outer_all.at[block], outer_sem.at[block]
            ).start()
            first = 5 * (block // 4) + block % 4
            if block % 4 < 3:
                pltpu.make_async_copy(mids[first], mid_all.at[block], mid_sem.at[block]).start()
            else:
                half = mids[first].shape[0]
                for part in range(2):
                    target = mid_all.at[block].at[pl.ds(part * half, half)]
                    pltpu.make_async_copy(mids[first + part], target, mid_sem.at[block]).start()
        for block in range(len(weights)):
            weight_copy(block).wait()

    for which in range(2):
        block = 2 * step + which
        pltpu.make_async_copy(mids[0], mid_all.at[block], mid_sem.at[block]).wait()
        pltpu.make_async_copy(outers.at[0], outer_all.at[block], outer_sem.at[block]).wait()
    fsdp, depth, width = weight_all.shape
    weight = weight_all[...].reshape(fsdp * depth, width)
    rows = mid_all.shape[1]

    def unit(gate, up, back):
        share = jax.nn.sigmoid(gate)
        silu = gate * share
        inner = (silu * up).astype(BF16)
        grad_gate = (back * up * (share + silu * (1.0 - share))).astype(BF16)
        return inner, grad_gate, (back * silu).astype(BF16)

    tail = slice(2 * main, 2 * main + TAIL)
    last = slice(2 * main + TAIL, 2 * main + 2 * TAIL)
    parts = []
    for which in range(2):
        mine = slice(which * rows, (which + 1) * rows)
        mid, outer = mid_all[2 * step + which], outer_all[2 * step + which]
        mid_ref[mine] = mid
        outer_ref[mine] = outer
        both = product(mid, weight)
        back = by_transpose(outer, down_ref[...])
        inner, gate, up = unit(both[:, :main], both[:, main : 2 * main], back[:, :main])
        inner_ref[mine, :main] = inner
        inner, gate_tail, up_tail = unit(both[:, tail], both[:, last], back[:, main:])
        inner_ref[mine, main:] = inner
        grads = jnp.concatenate([gate, up, gate_tail, up_tail], axis=1)
        grads_ref[mine] = grads
        parts.append(by_transpose(grads, weight).astype(BF16))

    @pl.when(step < 2)
    def _():
        send_ref[:rows] = parts[0]
        send_ref[rows:] = parts[1]

    @pl.when(step >= 2)
    def _():
        keep_ref[:rows] = parts[0]
        keep_ref[rows:] = parts[1]


def feed(info, mids, outers, weights, down, awaited=()):
    rows, width = mids[0].shape
    depth, units2 = weights[0].shape
    units = units2 // 2
    count = PLANE
    anywhere = pl.BlockSpec(memory_space=pl.ANY)
    flat = lambda last: pl.BlockSpec((2 * rows, last), lambda step, info: (step, 0))
    send = pl.BlockSpec((2 * rows, width), lambda step, info: (jnp.minimum(step, 1), 0))
    keep = pl.BlockSpec((2 * rows, width), lambda step, info: (jnp.maximum(step - 2, 0), 0))
    shape = lambda tall, last: jax.ShapeDtypeStruct((tall * rows, last), BF16)
    return pl.pallas_call(
        feed_kernel,
        out_shape=(
            shape(count, width),
            shape(count, width),
            shape(count, units),
            shape(count, units2),
            shape(count // 2, width),
            shape(count // 2, width),
        ),
        grid_spec=pltpu.PrefetchScalarGridSpec(
            num_scalar_prefetch=1,
            grid=(count // 2,),
            in_specs=[anywhere] * (len(mids) + 1 + len(weights))
            + [pl.BlockSpec(down.shape, lambda step, info: (0, 0))]
            + [anywhere] * len(awaited),
            out_specs=(flat(width), flat(width), flat(units), flat(units2), send, keep),
            scratch_shapes=[
                pltpu.VMEM((count, rows, width), BF16),
                pltpu.VMEM((count, rows, width), BF16),
                pltpu.VMEM((len(weights), depth, units2), BF16),
                pltpu.SemaphoreType.DMA((count,)),
                pltpu.SemaphoreType.DMA((count,)),
                pltpu.SemaphoreType.DMA((len(weights),)),
            ],
        ),
        compiler_params=pltpu.CompilerParams(vmem_limit_bytes=56 * 1024 * 1024),
        cost_estimate=pl.CostEstimate(
            flops=10 * count * rows * width * units,
            transcendentals=count * rows * units,
            bytes_accessed=12 * count * rows * width,
        ),
    )(info, *mids, outers, *weights, down, *awaited)


def hidden_weight_kernel(mid_ref, grads_ref, out_ref):
    planes, _, rows, width = out_ref.shape
    total = transpose_by(mid_ref[...], grads_ref[...])
    out_ref[:, 0] = total.reshape(planes, rows, width).astype(BF16)


def hidden_weight(mid, grads, near, planes):
    count, width = mid.shape
    units2 = grads.shape[1]
    rows = width // near // planes
    return pl.pallas_call(
        hidden_weight_kernel,
        out_shape=jax.ShapeDtypeStruct((planes, near, rows, units2), BF16),
        grid=(near,),
        in_specs=[
            pl.BlockSpec((count, width // near), lambda step: (0, step)),
            pl.BlockSpec((count, units2), lambda step: (0, 0)),
        ],
        out_specs=pl.BlockSpec((planes, 1, rows, units2), lambda step: (0, step, 0, 0)),
        compiler_params=pltpu.CompilerParams(vmem_limit_bytes=48 * 1024 * 1024),
        cost_estimate=pl.CostEstimate(
            flops=2 * count * width * units2,
            transcendentals=0,
            bytes_accessed=2 * count * (width + units2) + 2 * width * units2,
        ),
    )(mid, grads)


def down_spread_kernel(low_ref, mine_ref, other_ref, out_ref):
    main = mine_ref.shape[0] - TAIL
    low = low_ref[...] == 0
    mine, other = mine_ref[...].astype(F32), other_ref[...].astype(F32)
    first, second = jnp.where(low, mine, other), jnp.where(low, other, mine)
    out_ref[:main] = first[:main]
    out_ref[main : 2 * main] = second[:main]
    out_ref[2 * main : 2 * main + TAIL] = first[main:]
    out_ref[2 * main + TAIL :] = second[main:]


def awaiting(count):
    return [pl.BlockSpec(memory_space=pl.ANY)] * count


def whole_spec(shape):
    return pl.BlockSpec(shape, lambda *_: (0,) * len(shape))


def split_rows(blocks, cut, awaited):
    rows, width = blocks[0].shape
    count = len(blocks)

    def kernel(*refs):
        for index in range(count):
            refs[-2][index] = refs[index][:cut]
            refs[-1][index] = refs[index][cut:]

    return pl.pallas_call(
        kernel,
        out_shape=(
            jax.ShapeDtypeStruct((count, cut, width), BF16),
            jax.ShapeDtypeStruct((count, rows - cut, width), BF16),
        ),
        grid=(1,),
        in_specs=[whole_spec((rows, width))] * count + awaiting(len(awaited)),
        out_specs=(whole_spec((count, cut, width)), whole_spec((count, rows - cut, width))),
        cost_estimate=pl.CostEstimate(
            flops=0, transcendentals=0, bytes_accessed=4 * count * rows * width
        ),
    )(*blocks, *awaited)


def head_message(first, second, rest, awaited):
    def kernel(first_ref, second_ref, rest_ref, *refs):
        rows = first_ref.shape[0]
        refs[-1][:rows] = (first_ref[...].astype(F32) + second_ref[...].astype(F32)).astype(BF16)
        refs[-1][rows:] = rest_ref[...].astype(BF16)

    rows, width = first.shape
    shape = (rows + rest.shape[0], width)
    return pl.pallas_call(
        kernel,
        out_shape=jax.ShapeDtypeStruct(shape, BF16),
        grid=(1,),
        in_specs=[whole_spec(a.shape) for a in (first, second, rest)] + awaiting(len(awaited)),
        out_specs=whole_spec(shape),
        cost_estimate=pl.CostEstimate(
            flops=0, transcendentals=0, bytes_accessed=6 * rows * width
        ),
    )(first, second, rest, *awaited)


def per_device(
    inputs,
    lengths,
    positions,
    cotangent,
    w_query,
    w_key,
    w_value,
    w_output,
    w_gate,
    w_up,
    w_down,
    attn_gain,
    ffn_gain,
    query_gain,
    key_gain,
):
    groups, slot_count, model_width = inputs.shape
    row_count = groups * slot_count
    own_rows = w_query.shape[0]
    ctx_size = lax.axis_size("ctx")
    fsdp_size = lax.axis_size("fsdp")
    me_f = lax.axis_index("fsdp")
    me_c = lax.axis_index("ctx")
    inner = KV_HEADS
    outer = ctx_size // inner
    inner_groups = [[o * inner + i for i in range(inner)] for o in range(outer)]
    outer_groups = [[o * inner + i for o in range(outer)] for i in range(inner)]
    planes = ctx_size // 2
    plane_groups_z = [[2 * i + low for i in range(planes)] for low in range(2)]
    low_bit = me_c % 2
    my_head = me_c % inner
    mix = 4 * HEAD
    wide = GROUP * HEAD
    ff_shard = w_down.shape[0]
    ff_own = ff_shard // 2
    ff_main = ff_own - TAIL

    slots = me_c * slot_count + jnp.arange(slot_count)
    valid = (slots[None, :] < lengths[:, None]).astype(F32).reshape(row_count, 1)
    info = jnp.concatenate([(me_c // inner * inner)[None].astype(jnp.int32), lengths])
    device_info = jnp.stack([me_f, low_bit]).astype(jnp.int32)
    plane_info = jnp.stack([me_f, low_bit, low_bit * fsdp_size + me_f]).astype(jnp.int32)

    small = query_gain.shape[0]
    gains = jnp.concatenate([attn_gain, ffn_gain, query_gain, key_gain]).astype(BF16)[None]
    gains = jnp.concatenate(gather_near(gains), axis=0).astype(F32)
    gains = jnp.stack([pick(gains, me_f ^ k) for k in range(fsdp_size)])
    attn_scale = gains[:, :own_rows].reshape(1, model_width)
    ffn_scale = gains[:, own_rows : 2 * own_rows].reshape(1, model_width)
    qgain_scale = gains[:, 2 * own_rows : 2 * own_rows + small].reshape(-1)
    kgain_scale = gains[:, 2 * own_rows + small :].reshape(-1)
    head_gain = jnp.concatenate(
        [qgain_scale] * GROUP + [kgain_scale, jnp.ones((HEAD,), F32)]
    ).reshape(1, mix)

    line = Line()
    rows_shape = (row_count, model_width)

    line = Line()
    rows_shape = (row_count, model_width)
    rows_flops = 2 * row_count * model_width * model_width

    flat_low = inputs.reshape(row_count, model_width)
    place_row = positions.reshape(1, row_count)
    digits = jnp.concatenate([place_row // POSITION_BASE, place_row % POSITION_BASE], axis=0)
    digits = jnp.pad(
        digits.astype(BF16), ((0, POSITION_ROWS - 2), (0, model_width - row_count))
    )
    near = line(lambda a, b: jnp.concatenate([a, b], axis=0), flat_low, digits)
    far, following = trade(near, 4), ring_step(near)
    places = ring_places(my_head // 2)
    frequency = rope_base ** (-jnp.arange(0, HEAD, 2).astype(F32) / HEAD)
    frequency = jnp.concatenate([frequency] * (2 * GROUP)).reshape(1, wide)

    qkv_own = line(mix_heads, w_query, w_key, w_value)
    head_weight = lax.dynamic_slice_in_dim(qkv_own, my_head * mix, mix, 1)
    head_weight = jnp.stack(gather_near(head_weight))
    output_own = line(lambda a: a.astype(BF16), w_output)
    output_weight = lax.all_gather(output_own, "fsdp", axis=0, tiled=True)
    gu_own = line(lambda a, b: pack(device_info, a, b, fsdp_size), w_gate, w_up)
    gu_parts = [gu_own[0]] + [trade(gu_own[k], k) for k in range(1, fsdp_size)]

    earlier = ()
    for step in range(4):
        if step < 3:
            far, following = line.wait(far, following)
            next_far = trade(following, 4)
            after_next = ring_step(following) if step < 2 else None
        else:
            gu_parts = line.wait(*gu_parts)
        project_info = jnp.stack([me_f, low_bit, places[step]]).astype(jnp.int32)
        earlier = line(
            lambda a, b, c, *rest: project(
                project_info, a, b, c, attn_scale, head_gain, frequency, inner, rest or None
            ),
            near,
            far,
            head_weight,
            *earlier,
        )
        near, far, following = following, next_far, after_next
    normed_all, projected, mixed, cosine, sine = earlier
    mixed = mixed.reshape(inner, groups, slot_count, mix)

    qkv_weight = lax.all_gather(qkv_own, "fsdp", axis=0, tiled=True)
    if outer == 1:
        attended = line(lambda a: attention(info, a, a, None, (qkv_weight,)), mixed)
    else:
        shared = lax.all_gather(
            mixed[..., 2 * HEAD :], "ctx", axis=0, axis_index_groups=outer_groups, tiled=True
        )
        attended = line(lambda a, b: attention(info, a, b), mixed, shared)

    def exchange(values):
        return lax.all_to_all(values, "ctx", 0, 0, axis_index_groups=inner_groups, tiled=True)

    attended = exchange(attended.reshape(inner, row_count, wide))
    outer_low = line(
        lambda a: (a.reshape(rows_shape).astype(F32) * valid).astype(BF16), cotangent
    )
    outer_all = lax.all_gather(
        outer_low, ("ctx", "fsdp"), axis=0, axis_index_groups=plane_groups(), tiled=False
    )
    down_weight = line(
        lambda a: jnp.concatenate(
            [
                lax.dynamic_slice_in_dim(a, low_bit * ff_main, ff_main, 0),
                lax.dynamic_slice_in_dim(a, 2 * ff_main + low_bit * TAIL, TAIL, 0),
            ],
            axis=0,
        ).astype(BF16),
        w_down,
    )
    hidden_res, mid_low = line(
        lambda *a: row_call(
            join_kernel, ((rows_shape, F32), (rows_shape, BF16)), rows_flops, *a
        ),
        attended,
        output_weight,
        flat_low,
        ffn_scale,
    )
    mid_x, mid_y = trade(mid_low, 2), trade(mid_low, 4)
    mid_cut = line(cut_far, mid_x, mid_y)
    mid_corner = trade(mid_cut[0], 4), trade(mid_cut[1], 2)
    mid_all = gather_plane(mid_low, mid_x, mid_y, mid_corner)

    mid_all, outer_all, inner_low, grad_gu, send, keep = line(
        lambda *a: feed(plane_info, a[:10], a[10], a[11:15], a[15]),
        *mid_all,
        outer_all,
        *gu_parts,
        down_weight,
    )
    got = trade(send, 1)
    gu_part = line(lambda a, b: hidden_weight(a, b, fsdp_size, planes), mid_all, grad_gu)
    gu_sum = lax.psum_scatter(
        gu_part.reshape(-1, 2 * ff_own),
        "ctx",
        scatter_dimension=0,
        axis_index_groups=plane_groups_z,
        tiled=True,
    )
    low_send, high_send, low, high = line(cut_plane, got, keep)
    low_got, high_got = trade(low_send, 2), trade(high_send, 4)
    down_part = line(lambda a, b: transpose_by(a, b).astype(BF16), inner_low, outer_all)
    down_sum = lax.psum(down_part, "ctx", axis_index_groups=plane_groups_z)
    result_part = line(lambda a, b: product(a, b).astype(BF16), inner_low, down_weight)
    low_far, high_far, low_own, high_own = line(join_plane, low, high, low_got, high_got)
    low_got, high_got = trade(low_far, 4), trade(high_far, 2)
    (qkv_weight,) = line.wait(qkv_weight)
    grad_hidden, grad_attn_low, grad_heads, ffn_part = line(
        lambda *a: row_call(
            middle_kernel,
            (
                (rows_shape, F32),
                (rows_shape, BF16),
                ((inner, row_count, wide), BF16),
                ((1, model_width), F32),
            ),
            rows_flops,
            *a,
        ),
        low_own,
        low_got,
        high_own,
        high_got,
        hidden_res,
        outer_low,
        ffn_scale,
        output_weight,
    )

    grad_heads = exchange(grad_heads).reshape(inner, groups, slot_count, wide)
    (output_part,) = line(
        lambda *a: row_call(
            output_weight_kernel, (((model_width, model_width), BF16),), rows_flops, *a
        ),
        attended,
        grad_attn_low,
    )
    gu_own = line(
        lambda a: tuple(
            pick(a.reshape(fsdp_size, own_rows // planes, 2 * ff_own), me_f ^ k)
            for k in range(fsdp_size)
        ),
        gu_sum,
    )
    gu_blocks = [gu_own[0]] + [trade(gu_own[k], k) for k in range(1, fsdp_size)]
    if outer == 1:
        grad_mixed = line(
            lambda a, b: attention(info, a, a, b, gu_own[1:]), mixed, grad_heads
        )
    else:
        grad_q, grad_kv = line(
            lambda a, b, c: attention(info, a, b, c), mixed, shared, grad_heads
        )
        grad_kv = lax.psum_scatter(
            grad_kv, "ctx", scatter_dimension=0, axis_index_groups=outer_groups, tiled=True
        )
        grad_mixed = jnp.concatenate([grad_q, grad_kv], axis=-1)
    result_send, result_keep = halves(result_part)
    got = trade(result_send, 1)
    grad_head, head_part = line(
        lambda *a: unproject(*a, (*gu_blocks[1:], got)),
        grad_mixed.reshape(inner, row_count, mix),
        projected,
        head_gain,
        cosine,
        sine,
    )
    grad_qkv = exchange(grad_head)
    low_send, high_send, result_low, result_high = line(cut_plane, got, result_keep)
    result_low_got, result_high_got = trade(low_send, 2), trade(high_send, 4)
    head_rows = line(
        lambda a, b: transpose_by(
            a.reshape(inner * row_count, model_width), b.reshape(-1, mix)
        ).astype(BF16),
        normed_all,
        grad_head,
    )
    head_send, head_keep = line(
        lambda a: cut_near(a.reshape(fsdp_size, own_rows, mix), me_f), head_rows
    )
    head_got = trade(head_send, 1)
    cut = own_rows // planes // 2
    first_half, second_half = split_rows(gu_blocks, cut, (down_sum, grad_head))
    gu_mine = [
        lax.all_gather(piece, "ctx", axis=0, axis_index_groups=plane_groups_z, tiled=False)
        for piece in (first_half, second_half)
    ]
    gu_other = [trade(piece, fsdp_size) for piece in gu_mine]

    head_pair = line(add_low, head_keep, head_got)
    head_far = trade(head_pair[1], 2)
    output_send, output_keep = line(
        lambda a: cut_near(a.reshape(fsdp_size, own_rows, model_width), me_f), output_part
    )
    output_got = trade(output_send, 1)
    output_pair = line(add_low, output_keep, output_got)
    output_far = trade(output_pair[1], 2)
    down_other = trade(down_sum, fsdp_size)
    input_grad, attn_part = line(
        lambda *a: row_call(
            input_kernel,
            ((rows_shape, F32), ((1, model_width), F32)),
            rows_flops * KV_HEADS * mix // model_width,
            *a,
            awaited=(gu_mine[0], result_low_got, result_high_got),
        ),
        grad_qkv,
        qkv_weight,
        flat_low,
        grad_hidden,
        attn_scale,
    )
    input_grad = input_grad.reshape(groups, slot_count, model_width)
    qgain_part = sum(head_part[0, i * HEAD : (i + 1) * HEAD] for i in range(GROUP))
    kgain_part = head_part[0, GROUP * HEAD : (GROUP + 1) * HEAD]
    gain_parts = jnp.concatenate(
        [
            attn_part.reshape(fsdp_size, own_rows),
            ffn_part.reshape(fsdp_size, own_rows),
            qgain_part.reshape(fsdp_size, small),
            kgain_part.reshape(fsdp_size, small),
        ],
        axis=-1,
    )
    output_own = line(add_low, output_pair[0], output_far)
    output_grad = (
        ctx_sum(output_own.reshape(ctx_size, own_rows // ctx_size, model_width))
        .reshape(own_rows, model_width)
        .astype(F32)
    )
    gain_count = gain_parts.size
    gain_near = gain_parts + trade(gain_parts, 1)
    gain_near = gain_near + trade(gain_near, 2)
    gain_rows = -(-gain_count // (16 * mix)) * 16
    gain_near = jnp.pad(gain_near.reshape(-1), (0, gain_rows * mix - gain_count))
    gain_near = gain_near.reshape(gain_rows, mix)
    head_first, head_second = head_pair[0], head_far
    if outer > 1:
        gain_near = lax.psum(gain_near, "ctx", axis_index_groups=outer_groups)
        head_first = lax.psum(
            add_low(head_first, head_second).astype(F32), "ctx", axis_index_groups=outer_groups
        ).astype(BF16)
        head_second = jnp.zeros_like(head_first)
    low_far, high_far, low_own, high_own = line(
        join_plane, result_low, result_high, result_low_got, result_high_got
    )
    low_got, high_got = trade(low_far, 4), trade(high_far, 2)
    head_own = head_message(head_first, head_second, gain_near, (low_got, high_got))
    head_blocks = lax.all_gather(
        head_own, "ctx", axis=0, axis_index_groups=inner_groups, tiled=False
    )
    gain_sum = jnp.sum(head_blocks[:, own_rows:].astype(F32), axis=0)
    gain_sum = pick(gain_sum.reshape(-1)[:gain_count].reshape(gain_parts.shape), me_f)
    result = line(
        lambda a, b, c, d, e: (
            valid * (e + jnp.concatenate([a + b.astype(F32), c + d.astype(F32)], axis=0))
        ).astype(BF16),
        low_own,
        low_got,
        high_own,
        high_got,
        hidden_res,
    )
    block_output = result.reshape(groups, slot_count, model_width)

    query_grad, key_grad, value_grad = part_heads(head_blocks, own_rows)
    (down_grad,) = row_call(
        down_spread_kernel,
        (((2 * ff_own, model_width), F32),),
        0,
        low_bit.reshape(1, 1),
        down_sum,
        down_other,
        awaited=(gu_mine[1], head_own),
    )
    gate_grad, up_grad = spread(device_info, gu_mine, gu_other)

    return (
        block_output,
        input_grad,
        query_grad,
        key_grad,
        value_grad,
        output_grad,
        gate_grad,
        up_grad,
        down_grad,
        gain_sum[:own_rows],
        gain_sum[own_rows : 2 * own_rows],
        gain_sum[2 * own_rows : 2 * own_rows + small],
        gain_sum[2 * own_rows + small :],
    )


def solution(mesh):
    return jax.shard_map(
        per_device,
        mesh=mesh,
        in_specs=(
            P("fsdp", "ctx", None),
            P("fsdp"),
            P("fsdp", "ctx"),
            P("fsdp", "ctx", None),
            P("fsdp", None),
            P("fsdp", None),
            P("fsdp", None),
            P("fsdp", None),
            P("fsdp", None),
            P("fsdp", None),
            P("fsdp", None),
            P("fsdp"),
            P("fsdp"),
            P("fsdp"),
            P("fsdp"),
        ),
        out_specs=(
            P("fsdp", "ctx", None),
            P("fsdp", "ctx", None),
            P("fsdp", None),
            P("fsdp", None),
            P("fsdp", None),
            P("fsdp", None),
            P("fsdp", None),
            P("fsdp", None),
            P("fsdp", None),
            P("fsdp"),
            P("fsdp"),
            P("fsdp"),
            P("fsdp"),
        ),
        check_vma=False,
    )
```
